256 devices in a mesh: grp: 2 (over x_lo), fsdp: 128 (over z, y, x_hi, core).
Axes of the slice: x: 4 (x_hi: 2, x_lo: 2; x = x_hi * 2 + x_lo), y: 4, z: 8, core: 2. Of those that a mesh axis runs over, the one named last changes fastest.
Arguments:
- replay_states: bfloat16 [131072, 4096], P(('grp', 'fsdp')), may hold values from -30 to 30
- replay_embed: bfloat16 [131072, 1024], P(('grp', 'fsdp')), may hold values from -6 to 6
- replay_index: int32 [32768], P(('grp', 'fsdp')), may hold values from 0 to 511
- episode_first: int32 [32768], P(('grp', 'fsdp')), may hold values 0 or 1
- prior_weight: bfloat16 [4096, 1024], P('fsdp'), may hold values from -0.09375 to 0.09375
- transition_weight: bfloat16 [1024, 4096], P('fsdp'), may hold values from -0.1875 to 0.1875
- action_weight: bfloat16 [56, 4096], replicated, may hold values from -0.75 to 0.75
- trunk_weight: bfloat16 [1024, 2048], replicated, may hold values from -0.1875 to 0.1875
- value_head: bfloat16 [2048], replicated, may hold values from -0.125 to 0.125
- policy_head: bfloat16 [2048, 56], replicated, may hold values from -0.125 to 0.125
- reward_head: bfloat16 [4096], replicated, may hold values from -0.09375 to 0.09375
- latent_scale: float32 [1024], replicated, may hold values from 0.2 to 1
- action_noise: bfloat16 [2, 32768, 56], P(None, ('grp', 'fsdp')), may hold values from -6 to 6
- latent_noise: bfloat16 [2, 32768, 1024], P(None, ('grp', 'fsdp')), may hold values from -24 to 24
Outputs:
- final_states: bfloat16 [32768, 4096], P(('grp', 'fsdp'))
- returns: float32 [2, 32768], P(None, ('grp', 'fsdp'))
- trunk_grad: float32 [1024, 2048], P('fsdp')
The draws below stay inside these ranges and needn't reach their ends.
Inputs may be any that keep to these rules, and one draw needn't show every extreme that they name: `replay_index`: start i reads the replay block of the device that holds start i. `episode_first`: 1 marks a start at the first step of an episode.
All inputs are finite; a program needn't handle non-finite values. No bound on the sum of `episode_first` on one device may be relied on, other than what follows from the above.
Results may differ from the reference program's by a relative error of at most 0.0065.
Values may be sent and summed in bfloat16 or wider, within the bound.
No kernel may reach another device: no remote copies, remote signals or barrier semaphores. Data moves between devices by JAX's collectives and lax.ppermute only.
A program may use at most 128 MiB of HBM per device.

```python
import math
import jax
import jax.numpy as jnp
from jax import lax

D = 4096
Z = 1024
H = 2048
A = 56
R = 128
REPLAY = 512
STEPS = 2
ROWS = 32768
REPLAY_ROWS = 131072
N_GRP = 2
N_FSDP = 128


def draw_replay_states(key, part):
    rows = N_GRP * N_FSDP * REPLAY
    key_base, key_row, key_col = jax.random.split(key, 3)
    row_scale = jnp.exp(jax.random.uniform(key_row, (rows, 1), jnp.float32, -1.2, 1.2))
    col_scale = jnp.exp(jax.random.uniform(key_col, (1, D), jnp.float32, -1.2, 1.2))
    base = jax.random.normal(key_base, (rows, D), jnp.float32)
    return jnp.clip(base * row_scale * col_scale, -30.0, 30.0).astype(jnp.bfloat16)


def touch_ends(values, own_key, low, largest):
    dims = values.shape
    place = [jax.random.randint(jax.random.fold_in(own_key, axis), (), 0, dims[axis]) for axis in range(len(dims))]
    values = values.at[tuple(place)].set(low)
    longest = dims.index(max(dims))
    place[longest] = (place[longest] + 1) % dims[longest]
    return values.at[tuple(place)].set(largest)


def strengthened(entries, rng, source, target, blocks, factor):
    owner, partner = [(jnp.arange(entries.shape[dim]) // (entries.shape[dim] // blocks)).reshape([-1 if axis == dim else 1 for axis in range(entries.ndim)]) for dim in (source, target)]
    chosen = jax.random.permutation(rng, blocks)[partner]
    strong = (owner == chosen) | (owner == (partner + blocks // 2) % blocks)
    return jnp.where(strong, factor * entries, entries)


def levels(key, shape, cuts, least, high):
    def one(axis_at, shards_of):
        steps = jax.random.uniform(jax.random.fold_in(jax.random.fold_in(key, 6), axis_at), (shards_of,), jnp.float32, least / len(cuts), high / len(cuts))
        return jnp.repeat(jnp.exp(steps), shape[axis_at] // shards_of).reshape((-1,) + (1,) * (len(shape) - axis_at - 1))

    gain = one(*cuts[0])
    for cut in cuts[1:]:
        gain = gain * one(*cut)
    return gain


def centred(own_key, extent, scale, limit, cuts=(), kind=jnp.bfloat16):
    array = jax.random.normal(own_key, extent, jnp.float32) * scale
    if len(cuts) > 0:
        array = levels(own_key, extent, cuts, -0.22, 0.18) * array
    return jnp.clip(array, min=-limit, max=limit).astype(kind)


def bell_draw_with(rng, shape, scale, limit, cuts, heavy, kind=jnp.bfloat16):
    entries = scale * jax.random.normal(rng, shape, jnp.float32)
    if cuts:
        entries = entries * levels(rng, shape, cuts, -0.22, 0.18)
    return jnp.clip(strengthened(entries, jax.random.fold_in(rng, 3), *heavy), -limit, limit).astype(kind)


def setup_inputs(seed: int = 0) -> dict:
    seeds = jax.random.split(jax.random.key(seed), 15)
    replay_states = draw_replay_states(jax.random.fold_in(seeds[14], 71), 0)
    replay_embed = centred(seeds[1], (REPLAY_ROWS, Z), 1.0, 6.0, ((0, 256),))
    replay_index = touch_ends(jax.random.randint(seeds[2], (ROWS,), 0, REPLAY), jax.random.fold_in(seeds[2], 1), 0, REPLAY - 1).astype(jnp.int32)
    episode_first = touch_ends((jax.random.randint(seeds[3], (ROWS,), 0, 8) < 1).astype(jnp.int32), jax.random.fold_in(seeds[3], 1), 0, 1)
    prior_weight = centred(seeds[4], (D, Z), D ** -0.5, 0.09375, ((0, 128),))
    transition_weight = centred(seeds[5], (Z, D), Z ** -0.5, 0.1875, ((0, 128),))
    action_weight = centred(seeds[6], (A, D), A ** -0.5, 0.75)
    trunk_weight = centred(seeds[7], (Z, H), Z ** -0.5, 0.1875)
    value_head = centred(seeds[8], (H,), H ** -0.5, 0.125)
    policy_head = centred(seeds[9], (H, A), H ** -0.5, 0.125)
    reward_head = centred(seeds[10], (D,), D ** -0.5, 0.09375)
    latent_scale = jnp.clip(jnp.exp(jax.random.uniform(seeds[11], (Z,), jnp.float32, math.log(0.2), math.log(1.0))), 0.2, 1.0)
    action_noise = centred(seeds[12], (STEPS, ROWS, A), 1.0, 6.0, ((1, 256),))
    latent_noise = bell_draw_with(seeds[13], (STEPS, ROWS, Z), 1.0, 24.0, ((1, 256),), (1, 2, 256, 6.0))
    return dict(replay_states=replay_states, replay_embed=replay_embed, replay_index=replay_index, episode_first=episode_first, prior_weight=prior_weight, transition_weight=transition_weight, action_weight=action_weight, trunk_weight=trunk_weight, value_head=value_head, policy_head=policy_head, reward_head=reward_head, latent_scale=latent_scale, action_noise=action_noise, latent_noise=latent_noise)


GAMMA = 0.985
LAMBDA = 0.95
EPS = 1e-06

def dsilu(pre):
    sig = jax.nn.sigmoid(pre)
    return sig * (1.0 + pre * (1.0 - sig))

def imagine(states, latents, weights, act_noise, lat_noise, grad_scale):
    prior_weight, transition_weight, action_weight, trunk_weight, value_head, policy_head, reward_head, latent_scale = weights
    steps = act_noise.shape[0]
    values, rewards, pres, kept = ([], [], [], [])
    for step in range(steps):
        pre = jnp.dot(latents, trunk_weight, preferred_element_type=jnp.float32)
        trunk = jax.nn.silu(pre).astype(jnp.bfloat16)
        values.append(jnp.dot(trunk, value_head, preferred_element_type=jnp.float32))
        action = jnp.tanh(jnp.dot(trunk, policy_head, preferred_element_type=jnp.float32) + act_noise[step].astype(jnp.float32)).astype(jnp.bfloat16)
        drive = jnp.dot(latents, transition_weight, preferred_element_type=jnp.float32) + jnp.dot(action, action_weight, preferred_element_type=jnp.float32)
        mixed = states.astype(jnp.float32) + jax.nn.silu(drive)
        states = (mixed * lax.rsqrt(lax.optimization_barrier(jnp.mean(mixed * mixed, axis=1, keepdims=True)) + EPS)).astype(jnp.bfloat16)
        rewards.append(jnp.dot(states, reward_head, preferred_element_type=jnp.float32))
        pres.append(pre)
        kept.append(latents)
        latents = (jnp.dot(states, prior_weight, preferred_element_type=jnp.float32) + latent_scale * lat_noise[step].astype(jnp.float32)).astype(jnp.bfloat16)
    last_trunk = jax.nn.silu(jnp.dot(latents, trunk_weight, preferred_element_type=jnp.float32)).astype(jnp.bfloat16)
    last_value = jnp.dot(last_trunk, value_head, preferred_element_type=jnp.float32)
    ahead = last_value
    target = last_value
    targets = [last_value] * steps
    for step in reversed(range(steps)):
        target = rewards[step] + GAMMA * ((1.0 - LAMBDA) * ahead + LAMBDA * target)
        targets[step] = target
        ahead = values[step]
    grad = jnp.zeros((trunk_weight.shape[0], trunk_weight.shape[1]), jnp.float32)
    for step in range(steps):
        delta = (values[step] - targets[step]) * grad_scale
        back = (delta[:, None] * value_head.astype(jnp.float32)[None, :] * dsilu(pres[step])).astype(jnp.bfloat16)
        grad = grad + jnp.dot(kept[step].T, back, preferred_element_type=jnp.float32)
    return (states, jnp.stack(targets), grad)

def reference(replay_states, replay_embed, replay_index, episode_first, prior_weight, transition_weight, action_weight, trunk_weight, value_head, policy_head, reward_head, latent_scale, action_noise, latent_noise):
    owner = jnp.arange(ROWS, dtype=jnp.int32) // R * REPLAY
    picked = owner + replay_index.astype(jnp.int32)
    keep = (1 - episode_first).astype(jnp.bfloat16)[:, None]
    start_states = replay_states[picked] * keep
    start_latents = (jnp.dot(start_states, prior_weight, preferred_element_type=jnp.float32) + replay_embed[picked].astype(jnp.float32)).astype(jnp.bfloat16)
    packed = jnp.concatenate([start_states, start_latents], axis=1)
    width = packed.shape[1]
    blocks = packed.reshape(N_GRP, N_FSDP, N_FSDP, R // N_FSDP, width)[::-1]
    relayed = jnp.transpose(blocks, (0, 2, 1, 3, 4)).reshape(ROWS, width)
    count = N_GRP * N_FSDP
    states = relayed[:, :D].reshape(count, R, D)
    latents = relayed[:, D:].reshape(count, R, Z)
    act = jnp.transpose(action_noise.reshape(STEPS, count, R, A), (1, 0, 2, 3))
    lat = jnp.transpose(latent_noise.reshape(STEPS, count, R, Z), (1, 0, 2, 3))
    weights = (prior_weight, transition_weight, action_weight, trunk_weight, value_head, policy_head, reward_head, latent_scale)
    grad_scale = 4.0 * (float(H) / float(ROWS * STEPS)) ** 0.5

    def one_block(grad, inputs):
        block_states, block_latents, block_act, block_lat = inputs
        final, targets, part = imagine(block_states, block_latents, weights, block_act, block_lat, grad_scale)
        return (grad + part, (final, targets))
    grad, (finals, targets) = lax.scan(one_block, jnp.zeros((Z, H), jnp.float32), (states, latents, act, lat))
    final_states = finals.reshape(ROWS, D)
    returns = jnp.transpose(targets, (1, 0, 2)).reshape(STEPS, ROWS)
    return (final_states, returns, grad)
```

```python
import jax
import jax.numpy as jnp
from jax import lax
from jax.sharding import Mesh, PartitionSpec as P

GAMMA = 0.985
LAMBDA = 0.95
EPS = 1e-06
F32 = jnp.float32
BF16 = jnp.bfloat16

NZ, NY, NX, NC = 8, 4, 2, 2
AXES = ("grp", "z", "y", "xh", "core")
FSDP = ("z", "y", "xh", "core")


def shift(n, d):
    return [(i, (i + d) % n) for i in range(n)]


def x_line(move):
    pairs = []
    for g in range(2):
        for h in range(2):
            to = move(2 * h + g) % 4
            pairs.append((2 * g + h, 2 * (to % 2) + to // 2))
    return pairs


def along_x(a, move):
    return lax.ppermute(a, ("grp", "xh"), x_line(move))


def swap_core(a):
    return lax.ppermute(a, "core", shift(2, 1))


def put(buf, piece, *place):
    return lax.dynamic_update_slice(buf, piece.reshape((1,) * len(place) + piece.shape), tuple(place) + (0,) * piece.ndim)


def gather_weight(shard, z, y, xh, core, g, last_step):
    rows, cols = shard.shape
    zbuf = jnp.zeros((NZ, rows, cols), shard.dtype)
    zbuf = put(zbuf, shard, z)
    up = down = shard
    for d in (1, 2, 3):
        up = lax.ppermute(up, "z", shift(NZ, 1))
        down = lax.ppermute(down, "z", shift(NZ, -1))
        zbuf = put(zbuf, up, (z - d) % NZ)
        zbuf = put(zbuf, down, (z + d) % NZ)
    far = lax.ppermute(up if last_step > 0 else down, "z", shift(NZ, last_step))
    zbuf = put(zbuf, far, (z + 4) % NZ)
    half = NZ // 2
    up = lax.ppermute(zbuf, "y", shift(NY, 1))
    down = lax.ppermute(zbuf, "y", shift(NY, -1))
    far_a = lax.ppermute(up[:half], "y", shift(NY, 1))
    far_b = lax.ppermute(down[half:], "y", shift(NY, -1))
    far = jnp.concatenate([far_a, far_b], axis=0)
    ybuf = jnp.zeros((NY, NZ, rows, cols), shard.dtype)
    ybuf = put(ybuf, zbuf, y)
    ybuf = put(ybuf, up, (y - 1) % NY)
    ybuf = put(ybuf, down, (y + 1) % NY)
    ybuf = put(ybuf, far, (y + 2) % NY)
    mine = lax.dynamic_slice(ybuf, (0, g * half, 0, 0), (NY, half, rows, cols))
    first = along_x(mine, lambda x: x + 1 if x % 2 else x - 1)
    second = along_x(first, lambda x: x ^ 1)
    own_other = swap_core(ybuf)
    first_other = swap_core(first)
    second_other = swap_core(second)
    full = jnp.zeros((NZ, NY, NX, NC, rows, cols), shard.dtype)

    def place(full, block, z0, h, c):
        block = jnp.swapaxes(block, 0, 1)[:, :, None, None]
        return lax.dynamic_update_slice(full, block, (z0, 0, h, c, 0, 0))

    full = place(full, ybuf, 0, xh, core)
    full = place(full, own_other, 0, xh, 1 - core)
    full = place(full, first, (1 - g) * half, 1 - xh, core)
    full = place(full, first_other, (1 - g) * half, 1 - xh, 1 - core)
    full = place(full, second, g * half, 1 - xh, core)
    full = place(full, second_other, g * half, 1 - xh, 1 - core)
    return full.reshape(NZ * NY * NX * NC * rows, cols)


def relay(packed_of, xh, core):
    near = jnp.stack([packed_of(xh, core), packed_of(xh, 1 - core)])
    away = jnp.stack([packed_of(1 - xh, core), packed_of(1 - xh, 1 - core)])
    near = along_x(near, lambda x: x ^ 1)
    away = along_x(away, lambda x: x - 1 if x % 2 == 0 else x + 1)
    crossed = swap_core(jnp.stack([near[1], away[1]]))
    same, other = jnp.stack([near[0], crossed[0]]), jnp.stack([away[0], crossed[1]])
    same = jnp.where(core == 0, same, same[::-1])
    other = jnp.where(core == 0, other, other[::-1])
    both = jnp.where(xh == 0, jnp.concatenate([same, other]), jnp.concatenate([other, same]))
    both = jnp.swapaxes(both, 0, 1)
    dealt = lax.all_to_all(both, ("z", "y"), split_axis=0, concat_axis=0, tiled=True)
    return dealt.reshape(-1, dealt.shape[-1])


def x_gather(latents):
    half = latents.shape[0] // 2
    up = along_x(latents, lambda x: x + 1)
    down = along_x(latents, lambda x: x - 1)
    far_a = along_x(up[:half], lambda x: x + 1)
    far_b = along_x(down[half:], lambda x: x - 1)
    mine = jnp.concatenate([latents, up, down, far_a, far_b], axis=0)
    return jnp.concatenate([mine, swap_core(mine)], axis=0)


def x_order(rows, g, xh, core):
    x = 2 * xh + g
    picked = []
    for c in (core, 1 - core):
        for d in (0, -1, 1, 2):
            at = (x + d) % 4
            picked.append(rows[((at % 2) * 2 + at // 2) * 2 + c])
    return jnp.concatenate(picked, axis=-1)


def dsilu(pre):
    sig = jax.nn.sigmoid(pre)
    return sig * (1.0 + pre * (1.0 - sig))


def local(
    replay_states,
    replay_embed,
    replay_index,
    episode_first,
    prior_weight,
    transition_weight,
    action_weight,
    trunk_weight,
    value_head,
    policy_head,
    reward_head,
    latent_scale,
    action_noise,
    latent_noise,
):
    g, z, y = lax.axis_index("grp"), lax.axis_index("z"), lax.axis_index("y")
    xh, core = lax.axis_index("xh"), lax.axis_index("core")
    width = replay_states.shape[1]
    rows = replay_index.shape[0]
    order = jnp.stack([replay_index, episode_first]).reshape(2, NZ * NY, NX, NC)

    def packed_of(h, c):
        picked = lax.dynamic_slice(order, (0, 0, h, c), (2, NZ * NY, 1, 1)).reshape(2, NZ * NY)
        keep = (1 - picked[1]).astype(BF16)[:, None]
        return jnp.concatenate(
            [jnp.take(replay_states, picked[0], axis=0) * keep, jnp.take(replay_embed, picked[0], axis=0)],
            axis=1,
        )

    dealt = relay(packed_of, xh, core)
    prior_full = gather_weight(prior_weight, z, y, xh, core, g, 1)
    transition_full = gather_weight(transition_weight, z, y, xh, core, g, -1)
    states = dealt[:, :width]
    latents = (
        jnp.dot(states, prior_full, preferred_element_type=F32) + dealt[:, width:].astype(F32)
    ).astype(BF16)
    steps = action_noise.shape[0]
    hidden_units = trunk_weight.shape[1]
    part = hidden_units // 8
    slot = (g * 2 + xh) * 2 + core
    trunk_part = lax.dynamic_slice(trunk_weight, (0, slot * part), (trunk_weight.shape[0], part))
    head_part = lax.dynamic_slice(value_head, (slot * part,), (part,)).astype(F32)
    values, rewards, slopes, kept = ([], [], [], [])
    for step in range(steps):
        line = x_gather(latents)
        kept.append(line)
        pre = jnp.dot(latents, trunk_weight, preferred_element_type=F32)
        trunk = jax.nn.silu(pre).astype(BF16)
        values.append(jnp.dot(trunk, value_head, preferred_element_type=F32))
        action = jnp.tanh(
            jnp.dot(trunk, policy_head, preferred_element_type=F32) + action_noise[step].astype(F32)
        ).astype(BF16)
        drive = jnp.dot(latents, transition_full, preferred_element_type=F32) + jnp.dot(
            action, action_weight, preferred_element_type=F32
        )
        mixed = states.astype(F32) + jax.nn.silu(drive)
        states = (mixed * lax.rsqrt(jnp.mean(mixed * mixed, axis=1, keepdims=True) + EPS)).astype(BF16)
        rewards.append(jnp.dot(states, reward_head, preferred_element_type=F32))
        latents = (
            jnp.dot(states, prior_full, preferred_element_type=F32)
            + latent_scale * latent_noise[step].astype(F32)
        ).astype(BF16)
        slopes.append(head_part * dsilu(jnp.dot(line, trunk_part, preferred_element_type=F32)))
    last_trunk = jax.nn.silu(jnp.dot(latents, trunk_weight, preferred_element_type=F32)).astype(BF16)
    last_value = jnp.dot(last_trunk, value_head, preferred_element_type=F32)
    ahead = last_value
    target = last_value
    targets = [last_value] * steps
    for step in reversed(range(steps)):
        target = rewards[step] + GAMMA * ((1.0 - LAMBDA) * ahead + LAMBDA * target)
        targets[step] = target
        ahead = values[step]
    count = lax.axis_size("grp") * NZ * NY * NX * NC
    grad_scale = 4.0 * (float(hidden_units) / float(count * rows * steps)) ** 0.5
    delta = (jnp.stack(values) - jnp.stack(targets)) * grad_scale
    line_delta = lax.all_gather(delta, ("grp", "xh", "core"), axis=0, tiled=False)
    line_delta = x_order(line_delta, g, xh, core)
    backs = [(line_delta[step][:, None] * slopes[step]).astype(BF16) for step in range(steps)]
    share = lax.dot_general(
        jnp.concatenate(kept, axis=0),
        jnp.concatenate(backs, axis=0),
        (((0,), (0,)), ((), ())),
        preferred_element_type=F32,
    )
    blocks = share.astype(BF16).reshape(NZ * NY, -1, part)
    met = lax.all_to_all(blocks, ("z", "y"), split_axis=0, concat_axis=0, tiled=True)
    summed = jnp.sum(met.astype(F32), axis=0)
    summed = summed.reshape(NX * NC, -1, part)
    sent = jnp.concatenate([summed, summed], axis=0)
    parts = lax.all_to_all(sent, ("grp", "xh", "core"), split_axis=0, concat_axis=0, tiled=True)
    trunk_grad = jnp.swapaxes(parts, 0, 1).reshape(parts.shape[1], hidden_units)
    return (states, jnp.stack(targets), trunk_grad)


def solution(mesh):
    fine = Mesh(mesh.devices.reshape(2, NZ, NY, NX, NC), AXES)
    return jax.shard_map(
        local,
        mesh=fine,
        in_specs=(
            P(AXES, None),
            P(AXES, None),
            P(AXES),
            P(AXES),
            P(FSDP, None),
            P(FSDP, None),
            P(),
            P(),
            P(),
            P(),
            P(),
            P(),
            P(None, AXES, None),
            P(None, AXES, None),
        ),
        out_specs=(P(AXES, None), P(None, AXES), P(FSDP, None)),
        check_vma=False,
    )
```

```python
import functools

import jax
import jax.numpy as jnp
from jax import lax
from jax.experimental import pallas as pl
from jax.experimental.pallas import tpu as pltpu
from jax.sharding import Mesh, PartitionSpec as P

GAMMA = 0.985
LAMBDA = 0.95
EPS = 1e-06
F32 = jnp.float32
BF16 = jnp.bfloat16

NZ, NY, NX, NC = 8, 4, 2, 2
AXES = ("grp", "z", "y", "xh", "core")
FSDP = ("z", "y", "xh", "core")


def shift(n, d):
    return [(i, (i + d) % n) for i in range(n)]


def x_line(move):
    pairs = []
    for g in range(2):
        for h in range(2):
            to = move(2 * h + g) % 4
            pairs.append((2 * g + h, 2 * (to % 2) + to // 2))
    return pairs


def along_x(a, move):
    return lax.ppermute(a, ("grp", "xh"), x_line(move))


def swap_core(a):
    return lax.ppermute(a, "core", shift(2, 1))


def split_ring(axis, n):
    return [(2 * i + c, 2 * ((i + 1 - 2 * c) % n) + c) for i in range(n) for c in range(2)]


def x_hop(slots):
    pairs = []
    for g in range(2):
        for h in range(2):
            if 0 in slots:
                pairs.append(((2 * g + h) * 2, (2 * (1 - g) + 1 - h) * 2))
            if 1 in slots:
                pairs.append(((2 * g + h) * 2 + 1, (2 * (1 - g) + h) * 2 + 1))
    return pairs


def gather_weights(prior, transition, g, core):
    depth = transition.shape[0]
    cols = prior.shape[1]
    blocks = transition.shape[1] // cols
    other_p, other_t = swap_core(prior), swap_core(transition)

    def both(mine, other):
        return jnp.where(core == 0, jnp.concatenate([mine, other]), jnp.concatenate([other, mine]))

    chip_t = both(transition, other_t).reshape(2 * depth, blocks, cols)
    unit = jnp.stack([both(prior, other_p), jnp.swapaxes(chip_t, 0, 1).reshape(-1, cols)])
    ring = [unit]
    for hop in range(4):
        pairs = split_ring("z", NZ)
        if hop == 3:
            pairs = [p for p in pairs if p[0] % 2]
        ring.append(lax.ppermute(ring[-1], ("z", "core"), pairs))
    own = jnp.where(core == 0, jnp.stack(ring[:4]), jnp.stack(ring[1:]))
    own_s = swap_core(own)
    side, side_s = [], []
    for w in range(2):
        side.append(lax.ppermute(jnp.stack([own[:, w], own_s[:, w]]), ("y", "core"), split_ring("y", NY)))
        side_s.append(swap_core(side[w]))
    far = lax.ppermute(jnp.stack([side[0][0], side[1][0]]), ("y", "core"), split_ring("y", NY))
    far_s = swap_core(far)
    chunks = [jnp.where(g == 0, own, own_s)]
    for w in range(2):
        a, b = side[w], side_s[w]
        chunks.append(jnp.where(g == 0, jnp.stack([a[0], b[1]]), jnp.stack([a[1], b[0]])))
    chunks.append(jnp.where(g == 0, far, far_s))
    hops, hops_s = [], []
    for k in range(5):
        if k == 0:
            sent, slots = chunks[0], (0,)
        elif k == 4:
            sent, slots = hops_s[3], (1,)
        else:
            sent, slots = jnp.where(core == 0, chunks[k].reshape(hops_s[k - 1].shape), hops_s[k - 1]), (0, 1)
        sent = sent.reshape(8, 64, cols)
        hops.append(lax.ppermute(sent, ("grp", "xh", "core"), x_hop(slots)))
        hops_s.append(swap_core(hops[k]))
    flat = [own.reshape(8, 64, cols), own_s.reshape(8, 64, cols)]
    for w in range(2):
        flat += [side[w].reshape(8, 64, cols), side_s[w].reshape(8, 64, cols)]
    flat += [far.reshape(8, 64, cols), far_s.reshape(8, 64, cols)]
    for k in range(5):
        flat += [hops[k], hops_s[k]]
    return flat


def pieces_of(flat, w):
    side = flat[2 + 2 * w : 4 + 2 * w]
    hops = flat[8:]
    used = (0, 1, 2, 3, 4) if w == 0 else (0, 1, 2, 3, 4)
    return flat[0:2] + side + flat[6:8] + [hops[2 * k + s] for k in used for s in range(2)]


def place_all(w, where, pieces, full, sem):
    z, y, xh, core, g = (where[i] for i in range(5))
    own, own_s, side, side_s, far, far_s = pieces[:6]
    hops = [pieces[6 + 2 * k : 8 + 2 * k] for k in range(5)]

    def zpos(group, j):
        return lax.rem(z + NZ + jnp.where(group == 0, -j, 1 + j), NZ)

    def copy(src, at, group, j, dy, h):
        dst = full.at[zpos(group, j), lax.rem(y + NY + dy, NY), h]
        pltpu.make_async_copy(src.at[at], dst, sem).start()

    turn = jnp.where(core == 0, -1, 1)
    for j in range(4):
        copy(own, 2 * j + w, core, j, 0, xh)
        copy(own_s, 2 * j + w, 1 - core, j, 0, xh)
        copy(far, 4 * w + j, core, j, 2, xh)
        copy(far_s, 4 * w + j, 1 - core, j, 2, xh)
        for r in range(2):
            copy(side, 4 * r + j, jnp.bitwise_xor(core, r), j, turn, xh)
            copy(side_s, 4 * r + j, jnp.bitwise_xor(1 - core, r), j, -turn, xh)

    def other_pair(first, second):
        for j in range(4):
            for group, k, src in ((1 - g, 0, first), (g, 1, second)):
                copy(src[0], 2 * j + w, group, j, 0, 1 - xh)
                copy(src[1 + w], j, group, j, -1, 1 - xh)
                copy(src[1 + w], 4 + j, group, j, 1, 1 - xh)
                copy(src[3], 4 * w + j, group, j, 2, 1 - xh)

    @pl.when(core == 0)
    def _():
        other_pair([hops[k][0] for k in range(4)], [hops[k + 1][1] for k in range(4)])

    @pl.when(core != 0)
    def _():
        other_pair([hops[k][1] for k in range(4)], [hops[k + 1][0] for k in range(4)])


def wait_all(full, sem):
    pltpu.make_async_copy(full, full, sem).wait()


def silu(v):
    return v / (1.0 + jnp.exp(-v))


TILE = 256


def prior_dot(h, full, n):
    cols = pl.ds(pl.multiple_of(n * TILE, TILE), TILE)
    return jnp.dot(h, full[:, :, :, :, cols].reshape(h.shape[1], TILE), preferred_element_type=F32), cols


def first_kernel(where, dealt, *refs):
    pieces, (latents, full, sem) = refs[:16], refs[16:]
    place_all(0, where, pieces, full, sem)
    width = dealt.shape[1] - latents.shape[1]
    wait_all(full, sem)

    @pl.loop(0, latents.shape[1] // TILE)
    def _(n):
        acc, cols = prior_dot(dealt[:, :width], full, n)
        embed = dealt[:, pl.ds(pl.multiple_of(width + n * TILE, TILE), TILE)]
        latents[:, cols] = (acc + embed.astype(F32)).astype(BF16)


def step_kernel(last, scale, where, states_in, latents_in, trunk_hbm, head, policy, action_w, reward_w, spread, act_noise, lat_noise, *refs):
    refs = list(refs)
    if last:
        value_0, reward_0 = refs[:2]
        refs = refs[2:]
    p_pieces, t_pieces, refs = refs[:16], refs[16:32], refs[32:]
    if last:
        states_out, outs, refs = refs[0], refs[1], refs[2:]
    else:
        states_out, latents_out, value_out, reward_out = refs[:4]
        refs = refs[4:]
    p_full, t_full, trunk_w, trunk, mixed, sems = refs[:6]
    if last:
        latents_out = refs[6]
    trunk_copy = pltpu.make_async_copy(trunk_hbm, trunk_w, sems.at[0])
    trunk_copy.start()
    place_all(1, where, t_pieces, t_full, sems.at[1])
    place_all(0, where, p_pieces, p_full, sems.at[2])
    trunk_copy.wait()
    rows, width = mixed.shape
    hidden = trunk_w.shape[1]

    def critic(z_ref):
        def tile(n, value):
            cols = pl.ds(pl.multiple_of(n * TILE, TILE), TILE)
            pre = jnp.dot(z_ref[...], trunk_w[:, cols], preferred_element_type=F32)
            out = silu(pre).astype(BF16)
            trunk[:, cols] = out
            part = out.astype(F32) * head[:, cols].astype(F32)
            return value + jnp.sum(part, axis=1, keepdims=True)

        return lax.fori_loop(0, hidden // TILE, tile, jnp.zeros((rows, 1), F32))

    value = critic(latents_in)
    action = jnp.tanh(
        jnp.dot(trunk[...], policy[...], preferred_element_type=F32) + act_noise[...].astype(F32)
    ).astype(BF16)
    wait_all(t_full, sems.at[1])
    blocks = t_full.shape[3] // 16
    block = width // blocks
    square = jnp.zeros((rows, 1), F32)
    for q in range(blocks):

        def tile(n, square):
            cols = pl.ds(pl.multiple_of(n * TILE, TILE), TILE)
            at = pl.ds(pl.multiple_of(q * block + n * TILE, TILE), TILE)
            weight = t_full[:, :, :, q * 16 : (q + 1) * 16, cols].reshape(latents_in.shape[1], TILE)
            drive = jnp.dot(latents_in[...], weight, preferred_element_type=F32) + jnp.dot(
                action, action_w[:, at], preferred_element_type=F32
            )
            m = states_in[:, at].astype(F32) + silu(drive)
            mixed[:, at] = m
            return square + jnp.sum(m * m, axis=1, keepdims=True)

        square = lax.fori_loop(0, block // TILE, tile, square)
    norm = lax.rsqrt(square * (1.0 / width) + EPS)

    def normed(n, reward):
        at = pl.ds(pl.multiple_of(n * TILE, TILE), TILE)
        out = (mixed[:, at] * norm).astype(BF16)
        states_out[:, at] = out
        return reward + jnp.sum(out.astype(F32) * reward_w[:, at].astype(F32), axis=1, keepdims=True)

    reward = lax.fori_loop(0, width // TILE, normed, jnp.zeros((rows, 1), F32))
    wait_all(p_full, sems.at[2])

    @pl.loop(0, latents_out.shape[1] // TILE)
    def _(n):
        acc, cols = prior_dot(states_out[...], p_full, n)
        latents_out[:, cols] = (acc + spread[:, cols] * lat_noise[:, cols].astype(F32)).astype(BF16)

    if not last:
        value_out[...] = value
        reward_out[...] = reward
        return
    last_value = critic(latents_out)
    second = reward + GAMMA * ((1.0 - LAMBDA) * last_value + LAMBDA * last_value)
    first = reward_0[...] + GAMMA * ((1.0 - LAMBDA) * value + LAMBDA * second)
    place = lax.broadcasted_iota(jnp.int32, (rows, 128), 1)
    out = jnp.where(place == 0, first, jnp.where(place == 1, second, 0.0))
    out = jnp.where(place == 2, (value_0[...] - first) * scale, out)
    out = jnp.where(place == 3, (value - second) * scale, out)
    outs[...] = out


VMEM_SPEC = pl.BlockSpec(memory_space=pltpu.VMEM)
ANY_SPEC = pl.BlockSpec(memory_space=pl.ANY)
SMEM_SPEC = pl.BlockSpec(memory_space=pltpu.SMEM)
LIMIT = 50 * 2**20


def full_scratch(cols):
    return pltpu.VMEM((NZ, NY, NX, 64, cols), BF16)


def first_call(where, dealt, pieces, cols):
    return pl.pallas_call(
        first_kernel,
        name="first_latents",
        out_shape=jax.ShapeDtypeStruct((dealt.shape[0], cols), BF16),
        in_specs=[SMEM_SPEC, VMEM_SPEC] + [ANY_SPEC] * len(pieces),
        out_specs=VMEM_SPEC,
        scratch_shapes=[full_scratch(cols), pltpu.SemaphoreType.DMA],
        compiler_params=pltpu.CompilerParams(vmem_limit_bytes=LIMIT),
        cost_estimate=pl.CostEstimate(flops=2 * 128 * 4096 * 1024, bytes_accessed=10 * 2**20, transcendentals=0),
    )(where, dealt, *pieces)


def step_call(last, scale, where, states, latents, weights, noise, early, p_pieces, t_pieces):
    trunk_weight, head, policy, action_w, reward_w, spread = weights
    rows, cols = latents.shape
    width, hidden = action_w.shape[1], trunk_weight.shape[1]
    column = jax.ShapeDtypeStruct((rows, 1), F32)
    shapes = [jax.ShapeDtypeStruct((rows, width), BF16)]
    if last:
        shapes += [jax.ShapeDtypeStruct((rows, 128), F32)]
    else:
        shapes += [jax.ShapeDtypeStruct((rows, cols), BF16), column, column]
    scratch = [
        full_scratch(cols),
        full_scratch(cols),
        pltpu.VMEM((cols, hidden), BF16),
        pltpu.VMEM((rows, hidden), BF16),
        pltpu.VMEM((rows, width), F32),
        pltpu.SemaphoreType.DMA((3,)),
    ]
    if last:
        scratch.append(pltpu.VMEM((rows, cols), BF16))
    small = [states, latents]
    heads = [head, policy, action_w, reward_w, spread, *noise, *early]
    specs = [SMEM_SPEC] + [VMEM_SPEC] * 2 + [ANY_SPEC] + [VMEM_SPEC] * len(heads) + [ANY_SPEC] * 32
    return pl.pallas_call(
        functools.partial(step_kernel, last, scale),
        name="last_step" if last else "first_step",
        out_shape=shapes,
        in_specs=specs,
        out_specs=[VMEM_SPEC] * len(shapes),
        scratch_shapes=scratch,
        compiler_params=pltpu.CompilerParams(vmem_limit_bytes=LIMIT),
        cost_estimate=pl.CostEstimate(flops=2 * 128 * 1024 * 10240, bytes_accessed=24 * 2**20, transcendentals=0),
    )(where, *small, trunk_weight, *heads, *p_pieces, *t_pieces)


def relay(packed, xh, core):
    near, away = packed[0], packed[1]
    near = along_x(near, lambda x: x ^ 1)
    away = along_x(away, lambda x: x - 1 if x % 2 == 0 else x + 1)
    crossed = swap_core(jnp.stack([near[1], away[1]]))
    same, other = jnp.stack([near[0], crossed[0]]), jnp.stack([away[0], crossed[1]])
    same = jnp.where(core == 0, same, same[::-1])
    other = jnp.where(core == 0, other, other[::-1])
    both = jnp.where(xh == 0, jnp.concatenate([same, other]), jnp.concatenate([other, same]))
    both = jnp.swapaxes(both, 0, 1)
    dealt = lax.all_to_all(both, ("z", "y"), split_axis=0, concat_axis=0, tiled=True)
    return dealt.reshape(-1, dealt.shape[-1])


def x_gather(latents):
    half = latents.shape[0] // 2
    up = along_x(latents, lambda x: x + 1)
    down = along_x(latents, lambda x: x - 1)
    far_a = along_x(up[:half], lambda x: x + 1)
    far_b = along_x(down[half:], lambda x: x - 1)
    mine = jnp.concatenate([latents, up, down, far_a, far_b], axis=0)
    return jnp.concatenate([mine, swap_core(mine)], axis=0)


def x_order(rows, g, xh, core):
    x = 2 * xh + g
    picked = []
    for c in (core, 1 - core):
        for d in (0, -1, 1, 2):
            at = (x + d) % 4
            picked.append(rows[((at % 2) * 2 + at // 2) * 2 + c])
    return jnp.concatenate(picked, axis=-1)


def dsilu(pre):
    sig = jax.nn.sigmoid(pre)
    return sig * (1.0 + pre * (1.0 - sig))


def local(
    replay_states,
    replay_embed,
    replay_index,
    episode_first,
    prior_weight,
    transition_weight,
    action_weight,
    trunk_weight,
    value_head,
    policy_head,
    reward_head,
    latent_scale,
    action_noise,
    latent_noise,
):
    g, z, y = lax.axis_index("grp"), lax.axis_index("z"), lax.axis_index("y")
    xh, core = lax.axis_index("xh"), lax.axis_index("core")
    width = replay_states.shape[1]
    rows = replay_index.shape[0]
    order = jnp.stack([replay_index, episode_first]).reshape(2, NZ * NY, NX, NC)
    order = jnp.transpose(order, (2, 3, 0, 1))
    order = jnp.where(xh == 0, order, order[::-1])
    order = jnp.where(core == 0, order, order[:, ::-1])
    order = jnp.swapaxes(order, 1, 2).swapaxes(0, 1).reshape(2, rows)
    keep = (1 - order[1]).astype(BF16)[:, None]
    packed = jnp.concatenate(
        [jnp.take(replay_states, order[0], axis=0) * keep, jnp.take(replay_embed, order[0], axis=0)],
        axis=1,
    ).reshape(NX, NC, NZ * NY, -1)
    dealt = relay(packed, xh, core)
    flat = gather_weights(prior_weight, transition_weight, g, core)
    p_pieces, t_pieces = pieces_of(flat, 0), pieces_of(flat, 1)
    where = jnp.stack([z, y, xh, core, g]).astype(jnp.int32)
    steps = action_noise.shape[0]
    hidden_units = trunk_weight.shape[1]
    cols = prior_weight.shape[1]
    part = hidden_units // 8
    slot = (g * 2 + xh) * 2 + core
    trunk_part = lax.dynamic_slice(trunk_weight, (0, slot * part), (trunk_weight.shape[0], part))
    head_part = lax.dynamic_slice(value_head, (slot * part,), (part,)).astype(F32)
    count = lax.axis_size("grp") * NZ * NY * NX * NC
    grad_scale = 4.0 * (float(hidden_units) / float(count * rows * steps)) ** 0.5
    weights = (
        trunk_weight,
        value_head[None],
        policy_head,
        action_weight,
        reward_head[None],
        latent_scale[None],
    )

    def slope_of(line):
        return head_part * dsilu(jnp.dot(line, trunk_part, preferred_element_type=F32))

    latents = first_call(where, dealt, p_pieces, cols)
    kept = [x_gather(latents)]
    states, latents, value_0, reward_0 = step_call(
        False, grad_scale, where, dealt, latents, weights, (action_noise[0], latent_noise[0]), (), p_pieces, t_pieces
    )
    kept.append(x_gather(latents))
    states, outs = step_call(
        True, grad_scale, where, states, latents, weights, (action_noise[1], latent_noise[1]), (value_0, reward_0), p_pieces, t_pieces
    )
    slopes = [slope_of(line) for line in kept]
    outs = outs[:, :4].T
    targets, delta = outs[:2], outs[2:]
    line_delta = lax.all_gather(delta, ("grp", "xh", "core"), axis=0, tiled=False)
    line_delta = x_order(line_delta, g, xh, core)
    backs = [(line_delta[step][:, None] * slopes[step]).astype(BF16) for step in range(steps)]
    share = lax.dot_general(
        jnp.concatenate(kept, axis=0),
        jnp.concatenate(backs, axis=0),
        (((0,), (0,)), ((), ())),
        preferred_element_type=F32,
    )
    blocks = share.astype(BF16).reshape(NZ * NY, -1, part)
    met = lax.all_to_all(blocks, ("z", "y"), split_axis=0, concat_axis=0, tiled=True)
    summed = jnp.sum(met.astype(F32), axis=0)
    summed = summed.reshape(NX * NC, -1, part)
    sent = jnp.concatenate([summed, summed], axis=0)
    parts = lax.all_to_all(sent, ("grp", "xh", "core"), split_axis=0, concat_axis=0, tiled=True)
    trunk_grad = jnp.swapaxes(parts, 0, 1).reshape(parts.shape[1], hidden_units)
    return (states, targets, trunk_grad)


def solution(mesh):
    fine = Mesh(mesh.devices.reshape(2, NZ, NY, NX, NC), AXES)
    return jax.shard_map(
        local,
        mesh=fine,
        in_specs=(
            P(AXES, None),
            P(AXES, None),
            P(AXES),
            P(AXES),
            P(FSDP, None),
            P(FSDP, None),
            P(),
            P(),
            P(),
            P(),
            P(),
            P(),
            P(None, AXES, None),
            P(None, AXES, None),
        ),
        out_specs=(P(AXES, None), P(None, AXES), P(FSDP, None)),
        check_vma=False,
    )
```

```python
import functools

import jax
import jax.numpy as jnp
from jax import lax
from jax.experimental import pallas as pl
from jax.experimental.pallas import tpu as pltpu
from jax.sharding import Mesh, PartitionSpec as P

GAMMA = 0.985
LAMBDA = 0.95
EPS = 1e-06
F32 = jnp.float32
BF16 = jnp.bfloat16

NZ, NY, NX, NC = 8, 4, 2, 2
AXES = ("grp", "z", "y", "xh", "core")
FSDP = ("z", "y", "xh", "core")


def shift(n, d):
    return [(i, (i + d) % n) for i in range(n)]


def x_line(move):
    pairs = []
    for g in range(2):
        for h in range(2):
            to = move(2 * h + g) % 4
            pairs.append((2 * g + h, 2 * (to % 2) + to // 2))
    return pairs


def along_x(a, move):
    return lax.ppermute(a, ("grp", "xh"), x_line(move))


def swap_core(a):
    return lax.ppermute(a, "core", shift(2, 1))


def split_ring(axis, n):
    return [(2 * i + c, 2 * ((i + 1 - 2 * c) % n) + c) for i in range(n) for c in range(2)]


def gather_weights(prior, transition, g, core, xh, order, packed_of):
    depth = transition.shape[0]
    cols = prior.shape[1]
    blocks = transition.shape[1] // cols
    other_p, other_t = swap_core(prior), swap_core(transition)

    def both(mine, other):
        return jnp.where(core == 0, jnp.concatenate([mine, other]), jnp.concatenate([other, mine]))

    chip_t = both(transition, other_t).reshape(2 * depth, blocks, cols)
    unit = jnp.stack([both(prior, other_p), jnp.swapaxes(chip_t, 0, 1).reshape(-1, cols)])
    unit, order = lax.optimization_barrier((unit, order))
    ring = [unit]
    for hop in range(4):
        pairs = split_ring("z", NZ)
        if hop == 3:
            pairs = [p for p in pairs if p[0] % 2]
        ring.append(lax.ppermute(ring[-1], ("z", "core"), pairs))
        if hop == 0:
            packed = packed_of(order)
            ring[-1], packed = lax.optimization_barrier((ring[-1], packed))
            near, away = relay_x(packed)
    ring[4], near, away = lax.optimization_barrier((ring[4], near, away))
    both = relay_rest(near, away, xh, core)
    own = jnp.where(core == 0, jnp.stack(ring[3::-1]), jnp.stack(ring[1:]))
    own_s = swap_core(own)
    chosen = g == core

    def share(a, b, axis):
        picked = jnp.where(chosen, a, b)
        return lax.dynamic_index_in_dim(picked, core, axis, keepdims=False)

    def hop(a):
        first = along_x(a, lambda x: x + 1 if x % 2 else x - 1)
        return first, along_x(first, lambda x: x ^ 1)

    across = [hop(share(own, own_s, 1))]
    side = [jnp.stack([own[:, 0], own_s[:, 0]]), jnp.stack([own[:, 1], own_s[:, 1]])]
    side[0] = lax.ppermute(side[0], ("y", "core"), split_ring("y", NY))
    side[0], side[1], both = lax.optimization_barrier((side[0], side[1], both))
    dealt = deal(both)
    side[1] = lax.ppermute(side[1], ("y", "core"), split_ring("y", NY))
    across.append(hop(jnp.where(chosen, side[0][0], side[0][1])))
    far = lax.ppermute(jnp.stack([side[0][0], side[1][0]]), ("y", "core"), split_ring("y", NY))
    across.append(hop(jnp.where(chosen, side[1][0], side[1][1])))
    far_s = swap_core(far)
    across.append(hop(share(far, far_s, 0)))
    flat = [own, own_s, far, far_s]
    for w in range(2):
        flat += [side[w], swap_core(side[w])]
    for first, second in across:
        flat += [first, swap_core(first), second, swap_core(second)]
    return dealt, flat


def pieces_of(flat, w):
    across = [flat[8 + 4 * k : 12 + 4 * k] for k in (0, 1 + w, 3)]
    return flat[:4] + flat[4 + 2 * w : 6 + 2 * w] + across[0] + across[1] + across[2]


N_PIECES = 18


def place_all(w, where, pieces, full, sem):
    y, xh, core, g = (where[i] for i in range(1, 5))
    own, own_s, far, far_s, side, side_s = pieces[:6]
    turn = jnp.where(core == 0, -1, 1)

    def copy(src, group, dy, h):
        dst = full.at[pl.ds(4 * group, 4), lax.rem(y + NY + dy, NY), h]
        pltpu.make_async_copy(src, dst, sem).start()

    copy(own.at[:, w], core, 0, xh)
    copy(own_s.at[:, w], 1 - core, 0, xh)
    for r in range(2):
        copy(side.at[r], jnp.bitwise_xor(core, r), turn, xh)
        copy(side_s.at[r], jnp.bitwise_xor(1 - core, r), -turn, xh)
    copy(far.at[w], core, 2, xh)
    copy(far_s.at[w], 1 - core, 2, xh)
    for way, group in ((0, 1 - g), (2, g)):
        near, beside, away = (pieces[6 + 4 * k + way : 8 + 4 * k + way] for k in range(3))
        copy(beside[0], group, turn, 1 - xh)
        copy(beside[1], group, -turn, 1 - xh)

        @pl.when(core == w)
        def _():
            copy(near[0], group, 0, 1 - xh)
            copy(away[0], group, 2, 1 - xh)

        @pl.when(core != w)
        def _():
            copy(near[1], group, 0, 1 - xh)
            copy(away[1], group, 2, 1 - xh)


def turn_columns(where, src, dst):
    size = dst.shape[1] // NZ
    for i in range(NZ):
        at = lax.rem(where[0] + NZ - 3 + i, NZ) * size
        dst[:, i * size : (i + 1) * size] = src[:, pl.ds(pl.multiple_of(at, size), size)]


def wait_all(full, sem):
    pltpu.make_async_copy(full, full, sem).wait()


def silu(v):
    return v / (1.0 + jnp.exp(-v))


TILE = 512


def prior_dot(h, full, n):
    cols = pl.ds(pl.multiple_of(n * TILE, TILE), TILE)
    return jnp.dot(h, full[:, :, :, :, cols].reshape(h.shape[1], TILE), preferred_element_type=F32), cols


def first_kernel(where, dealt, *refs):
    pieces, (latents, full, turned, sem) = refs[:N_PIECES], refs[N_PIECES:]
    place_all(0, where, pieces, full, sem)
    width = dealt.shape[1] - latents.shape[1]
    turn_columns(where, dealt, turned)
    wait_all(full, sem)

    @pl.loop(0, latents.shape[1] // TILE)
    def _(n):
        acc, cols = prior_dot(turned[...], full, n)
        embed = dealt[:, pl.ds(pl.multiple_of(width + n * TILE, TILE), TILE)]
        latents[:, cols] = (acc + embed.astype(F32)).astype(BF16)


def step_kernel(last, scale, where, states_in, latents_in, trunk_hbm, head, policy, action_w, reward_w, spread, act_noise, lat_noise, *refs):
    refs = list(refs)
    if last:
        value_0, reward_0 = refs[:2]
        refs = refs[2:]
    p_pieces, t_pieces, refs = refs[:N_PIECES], refs[N_PIECES : 2 * N_PIECES], refs[2 * N_PIECES :]
    if last:
        states_out, outs, refs = refs[0], refs[1], refs[2:]
    else:
        states_out, latents_out, value_out, reward_out = refs[:4]
        refs = refs[4:]
    p_full, t_full, trunk_w, trunk, mixed, turned_h, turned_z, sems = refs[:8]
    if last:
        latents_out = refs[8]
    trunk_copy = pltpu.make_async_copy(trunk_hbm, trunk_w, sems.at[0])
    trunk_copy.start()
    place_all(1, where, t_pieces, t_full, sems.at[1])
    place_all(0, where, p_pieces, p_full, sems.at[2])
    turn_columns(where, latents_in, turned_z)
    trunk_copy.wait()
    rows, width = mixed.shape
    hidden = trunk_w.shape[1]

    def critic(z_ref):
        def tile(n, value):
            cols = pl.ds(pl.multiple_of(n * TILE, TILE), TILE)
            pre = jnp.dot(z_ref[...], trunk_w[:, cols], preferred_element_type=F32)
            out = silu(pre).astype(BF16)
            trunk[:, cols] = out
            part = out.astype(F32) * head[:, cols].astype(F32)
            return value + jnp.sum(part, axis=1, keepdims=True)

        return lax.fori_loop(0, hidden // TILE, tile, jnp.zeros((rows, 1), F32))

    value = critic(latents_in)
    action = jnp.tanh(
        jnp.dot(trunk[...], policy[...], preferred_element_type=F32) + act_noise[...].astype(F32)
    ).astype(BF16)
    wait_all(t_full, sems.at[1])
    blocks = t_full.shape[3] // 16
    block = width // blocks
    square = jnp.zeros((rows, 1), F32)
    for q in range(blocks):

        def tile(n, square):
            cols = pl.ds(pl.multiple_of(n * TILE, TILE), TILE)
            at = pl.ds(pl.multiple_of(q * block + n * TILE, TILE), TILE)
            weight = t_full[:, :, :, q * 16 : (q + 1) * 16, cols].reshape(latents_in.shape[1], TILE)
            drive = jnp.dot(turned_z[...], weight, preferred_element_type=F32) + jnp.dot(
                action, action_w[:, at], preferred_element_type=F32
            )
            m = states_in[:, at].astype(F32) + silu(drive)
            mixed[:, at] = m
            return square + jnp.sum(m * m, axis=1, keepdims=True)

        square = lax.fori_loop(0, block // TILE, tile, square)
    norm = lax.rsqrt(square * (1.0 / width) + EPS)

    def normed(n, reward):
        at = pl.ds(pl.multiple_of(n * TILE, TILE), TILE)
        out = (mixed[:, at] * norm).astype(BF16)
        states_out[:, at] = out
        return reward + jnp.sum(out.astype(F32) * reward_w[:, at].astype(F32), axis=1, keepdims=True)

    reward = lax.fori_loop(0, width // TILE, normed, jnp.zeros((rows, 1), F32))
    turn_columns(where, states_out, turned_h)
    wait_all(p_full, sems.at[2])

    @pl.loop(0, latents_out.shape[1] // TILE)
    def _(n):
        acc, cols = prior_dot(turned_h[...], p_full, n)
        latents_out[:, cols] = (acc + spread[:, cols] * lat_noise[:, cols].astype(F32)).astype(BF16)

    if not last:
        value_out[...] = value
        reward_out[...] = reward
        return
    last_value = critic(latents_out)
    second = reward + GAMMA * ((1.0 - LAMBDA) * last_value + LAMBDA * last_value)
    first = reward_0[...] + GAMMA * ((1.0 - LAMBDA) * value + LAMBDA * second)
    place = lax.broadcasted_iota(jnp.int32, (rows, 128), 1)
    out = jnp.where(place == 0, first, jnp.where(place == 1, second, 0.0))
    out = jnp.where(place == 2, (value_0[...] - first) * scale, out)
    out = jnp.where(place == 3, (value - second) * scale, out)
    outs[...] = out


VMEM_SPEC = pl.BlockSpec(memory_space=pltpu.VMEM)
ANY_SPEC = pl.BlockSpec(memory_space=pl.ANY)
SMEM_SPEC = pl.BlockSpec(memory_space=pltpu.SMEM)
LIMIT = 50 * 2**20


def full_scratch(cols):
    return pltpu.VMEM((NZ, NY, NX, 64, cols), BF16)


def first_call(where, dealt, pieces, cols):
    return pl.pallas_call(
        first_kernel,
        name="first_latents",
        out_shape=jax.ShapeDtypeStruct((dealt.shape[0], cols), BF16),
        in_specs=[SMEM_SPEC, VMEM_SPEC] + [ANY_SPEC] * len(pieces),
        out_specs=VMEM_SPEC,
        scratch_shapes=[
            full_scratch(cols),
            pltpu.VMEM((dealt.shape[0], dealt.shape[1] - cols), BF16),
            pltpu.SemaphoreType.DMA,
        ],
        compiler_params=pltpu.CompilerParams(vmem_limit_bytes=LIMIT),
        cost_estimate=pl.CostEstimate(flops=2 * 128 * 4096 * 1024, bytes_accessed=10 * 2**20, transcendentals=0),
    )(where, dealt, *pieces)


def step_call(last, scale, where, states, latents, weights, noise, early, p_pieces, t_pieces):
    trunk_weight, head, policy, action_w, reward_w, spread = weights
    rows, cols = latents.shape
    width, hidden = action_w.shape[1], trunk_weight.shape[1]
    column = jax.ShapeDtypeStruct((rows, 1), F32)
    shapes = [jax.ShapeDtypeStruct((rows, width), BF16)]
    if last:
        shapes += [jax.ShapeDtypeStruct((rows, 128), F32)]
    else:
        shapes += [jax.ShapeDtypeStruct((rows, cols), BF16), column, column]
    scratch = [
        full_scratch(cols),
        full_scratch(cols),
        pltpu.VMEM((cols, hidden), BF16),
        pltpu.VMEM((rows, hidden), BF16),
        pltpu.VMEM((rows, width), F32),
        pltpu.VMEM((rows, width), BF16),
        pltpu.VMEM((rows, cols), BF16),
        pltpu.SemaphoreType.DMA((3,)),
    ]
    if last:
        scratch.append(pltpu.VMEM((rows, cols), BF16))
    small = [states, latents]
    heads = [head, policy, action_w, reward_w, spread, *noise, *early]
    specs = [SMEM_SPEC] + [VMEM_SPEC] * 2 + [ANY_SPEC] + [VMEM_SPEC] * len(heads) + [ANY_SPEC] * (2 * N_PIECES)
    return pl.pallas_call(
        functools.partial(step_kernel, last, scale),
        name="last_step" if last else "first_step",
        out_shape=shapes,
        in_specs=specs,
        out_specs=[VMEM_SPEC] * len(shapes),
        scratch_shapes=scratch,
        compiler_params=pltpu.CompilerParams(vmem_limit_bytes=LIMIT),
        cost_estimate=pl.CostEstimate(flops=2 * 128 * 1024 * 10240, bytes_accessed=24 * 2**20, transcendentals=0),
    )(where, *small, trunk_weight, *heads, *p_pieces, *t_pieces)


def slope_kernel(*refs):
    pieces, (trunk_part, head_part, turned, slopes) = refs[:16], refs[16:]
    for i, piece in enumerate(pieces):
        rows = piece.shape[0]
        at = i * rows
        latents = piece[...]
        pre = jnp.dot(latents, trunk_part[...], preferred_element_type=F32)
        sig = 1.0 / (1.0 + jnp.exp(-pre))
        slopes[at : at + rows] = head_part[...] * (sig * (1.0 + pre * (1.0 - sig)))
        turned[:, at : at + rows] = latents.T


def slope_call(kept, trunk_part, head_part):
    count = 16 * kept[0][0].shape[0]
    cols, part = trunk_part.shape
    return pl.pallas_call(
        slope_kernel,
        name="slopes",
        out_shape=[jax.ShapeDtypeStruct((cols, count), BF16), jax.ShapeDtypeStruct((count, part), F32)],
        in_specs=[VMEM_SPEC] * 18,
        out_specs=[VMEM_SPEC] * 2,
        compiler_params=pltpu.CompilerParams(vmem_limit_bytes=LIMIT),
        cost_estimate=pl.CostEstimate(flops=2 * 2048 * 1024 * 256, bytes_accessed=12 * 2**20, transcendentals=0),
    )(*kept[0], *kept[1], trunk_part, head_part)


def share_kernel(pair, below, above, away, turned, slopes, share, back):
    line = [part[c] for part in (pair, below, above, away) for c in range(2)]
    rows = pair.shape[1]
    for step in range(2):
        for i, column in enumerate(line):
            at = (8 * step + i) * rows
            back[at : at + rows] = (column[:, 2 + step : 3 + step] * slopes[at : at + rows]).astype(BF16)
    share[...] = jnp.dot(turned[...], back[...], preferred_element_type=F32).astype(BF16)


def share_call(columns, turned, slopes):
    return pl.pallas_call(
        share_kernel,
        name="gradient_share",
        out_shape=jax.ShapeDtypeStruct((turned.shape[0], slopes.shape[1]), BF16),
        in_specs=[VMEM_SPEC] * 6,
        out_specs=VMEM_SPEC,
        scratch_shapes=[pltpu.VMEM(slopes.shape, BF16)],
        compiler_params=pltpu.CompilerParams(vmem_limit_bytes=LIMIT),
        cost_estimate=pl.CostEstimate(flops=2 * 2048 * 1024 * 256, bytes_accessed=8 * 2**20, transcendentals=0),
    )(*columns, turned, slopes)


def relay_x(packed):
    near = along_x(packed[0], lambda x: x ^ 1)
    away = along_x(packed[1], lambda x: x - 1 if x % 2 == 0 else x + 1)
    return near, away


def relay_rest(near, away, xh, core):
    crossed = swap_core(jnp.stack([near[1], away[1]]))
    first, second = core == 0, xh == 0

    def by_core(mine, other):
        return [jnp.where(first, mine, other), jnp.where(first, other, mine)]

    same, other = by_core(near[0], crossed[0]), by_core(away[0], crossed[1])
    low = [jnp.where(second, same[c], other[c]) for c in range(2)]
    high = [jnp.where(second, other[c], same[c]) for c in range(2)]
    both = jnp.stack(low + high, axis=1)
    return both


def deal(both):
    dealt = lax.all_to_all(both, ("z", "y"), split_axis=0, concat_axis=0, tiled=True)
    return dealt.reshape(-1, dealt.shape[-1])


def x_gather(latents):
    mine = [latents] + [along_x(latents, lambda x, d=d: x + d) for d in (1, -1, 2)]
    return [swap_core(mine[0])] + mine


def x_gather_rest(line):
    pieces = [line[1], line[0]]
    for a in line[2:]:
        pieces += [a, swap_core(a)]
    return pieces


def x_columns(column):
    pair = jnp.stack([column, swap_core(column)])
    return [pair] + [along_x(pair, lambda x, d=d: x + d) for d in (1, -1, 2)]


def local(
    replay_states,
    replay_embed,
    replay_index,
    episode_first,
    prior_weight,
    transition_weight,
    action_weight,
    trunk_weight,
    value_head,
    policy_head,
    reward_head,
    latent_scale,
    action_noise,
    latent_noise,
):
    g, z, y = lax.axis_index("grp"), lax.axis_index("z"), lax.axis_index("y")
    xh, core = lax.axis_index("xh"), lax.axis_index("core")
    width = replay_states.shape[1]
    rows = replay_index.shape[0]
    order = jnp.stack([replay_index, episode_first]).reshape(2, NZ * NY, NX, NC)
    order = jnp.transpose(order, (2, 3, 0, 1))
    order = jnp.where(xh == 0, order, order[::-1])
    order = jnp.where(core == 0, order, order[:, ::-1])
    order = jnp.swapaxes(order, 1, 2).swapaxes(0, 1).reshape(2, rows)

    def packed_of(order):
        keep = (1 - order[1]).astype(BF16)[:, None]
        return jnp.concatenate(
            [jnp.take(replay_states, order[0], axis=0) * keep, jnp.take(replay_embed, order[0], axis=0)],
            axis=1,
        ).reshape(NX, NC, NZ * NY, -1)

    dealt, flat = gather_weights(prior_weight, transition_weight, g, core, xh, order, packed_of)
    p_pieces, t_pieces = pieces_of(flat, 0), pieces_of(flat, 1)
    where = jnp.stack([z, y, xh, core, g]).astype(jnp.int32)
    steps = action_noise.shape[0]
    hidden_units = trunk_weight.shape[1]
    cols = prior_weight.shape[1]
    part = hidden_units // 8
    slot = (g * 2 + xh) * 2 + core
    trunk_part = lax.dynamic_slice(trunk_weight, (0, slot * part), (trunk_weight.shape[0], part))
    head_part = lax.dynamic_slice(value_head, (slot * part,), (part,)).astype(F32)
    count = lax.axis_size("grp") * NZ * NY * NX * NC
    grad_scale = 4.0 * (float(hidden_units) / float(count * rows * steps)) ** 0.5
    weights = (
        trunk_weight,
        value_head[None],
        policy_head,
        action_weight,
        reward_head[None],
        latent_scale[None],
    )

    latents = first_call(where, dealt, p_pieces, cols)
    latents, trunk_part, head_part = lax.optimization_barrier((latents, trunk_part, head_part))
    kept = [x_gather(latents)]
    states, latents, value_0, reward_0 = step_call(
        False, grad_scale, where, dealt, latents, weights, (action_noise[0], latent_noise[0]), (), p_pieces, t_pieces
    )
    kept.append(x_gather(latents))
    states, outs = step_call(
        True, grad_scale, where, states, latents, weights, (action_noise[1], latent_noise[1]), (value_0, reward_0), p_pieces, t_pieces
    )
    columns = x_columns(outs)
    kept = [x_gather_rest(line) for line in kept]
    turned, slopes = slope_call(kept, trunk_part, head_part[None])
    blocks = share_call(columns, turned, slopes).reshape(NZ * NY, -1, part)
    targets = outs[:, :2].T
    met = lax.all_to_all(blocks, ("z", "y"), split_axis=0, concat_axis=0, tiled=True)
    summed = jnp.sum(met.astype(F32), axis=0)
    summed = summed.reshape(NX * NC, -1, part)
    sent = jnp.concatenate([summed, summed], axis=0)
    parts = lax.all_to_all(sent, ("grp", "xh", "core"), split_axis=0, concat_axis=0, tiled=True)
    trunk_grad = jnp.swapaxes(parts, 0, 1).reshape(parts.shape[1], hidden_units)
    return (states, targets, trunk_grad)


def solution(mesh):
    fine = Mesh(mesh.devices.reshape(2, NZ, NY, NX, NC), AXES)
    return jax.shard_map(
        local,
        mesh=fine,
        in_specs=(
            P(AXES, None),
            P(AXES, None),
            P(AXES),
            P(AXES),
            P(FSDP, None),
            P(FSDP, None),
            P(),
            P(),
            P(),
            P(),
            P(),
            P(),
            P(None, AXES, None),
            P(None, AXES, None),
        ),
        out_specs=(P(AXES, None), P(None, AXES), P(FSDP, None)),
        check_vma=False,
    )
```

```python
import functools

import jax
import jax.numpy as jnp
from jax import lax
from jax.experimental import pallas as pl
from jax.experimental.pallas import tpu as pltpu
from jax.sharding import Mesh, PartitionSpec as P

GAMMA = 0.985
LAMBDA = 0.95
EPS = 1e-06
F32 = jnp.float32
BF16 = jnp.bfloat16

NZ, NY, NX, NC = 8, 4, 2, 2
AXES = ("grp", "z", "y", "xh", "core")
FSDP = ("z", "y", "xh", "core")


def shift(n, d):
    return [(i, (i + d) % n) for i in range(n)]


def x_line(move):
    pairs = []
    for g in range(2):
        for h in range(2):
            to = move(2 * h + g) % 4
            pairs.append((2 * g + h, 2 * (to % 2) + to // 2))
    return pairs


def along_x(a, move):
    return lax.ppermute(a, ("grp", "xh"), x_line(move))


def swap_core(a):
    return lax.ppermute(a, "core", shift(2, 1))


def split_ring(axis, n):
    return [(2 * i + c, 2 * ((i + 1 - 2 * c) % n) + c) for i in range(n) for c in range(2)]


def gather_weights(prior, transition, g, core, xh, order, packed_of):
    depth = transition.shape[0]
    cols = prior.shape[1]
    blocks = transition.shape[1] // cols
    other_p, other_t = swap_core(prior), swap_core(transition)

    def both(mine, other):
        return jnp.where(core == 0, jnp.concatenate([mine, other]), jnp.concatenate([other, mine]))

    chip_t = both(transition, other_t).reshape(2 * depth, blocks, cols)
    unit = jnp.stack([both(prior, other_p), jnp.swapaxes(chip_t, 0, 1).reshape(-1, cols)])
    unit, order = lax.optimization_barrier((unit, order))
    ring = [unit]
    for hop in range(4):
        pairs = split_ring("z", NZ)
        if hop == 3:
            pairs = [p for p in pairs if p[0] % 2]
        ring.append(lax.ppermute(ring[-1], ("z", "core"), pairs))
        if hop == 0:
            packed = packed_of(order)
            ring[-1], packed = lax.optimization_barrier((ring[-1], packed))
            near, away = relay_x(packed)
    ring[4], near, away = lax.optimization_barrier((ring[4], near, away))
    both = relay_rest(near, away, xh, core)
    own = jnp.where(core == 0, jnp.stack(ring[3::-1]), jnp.stack(ring[1:]))
    own_s = swap_core(own)
    chosen = g == core

    def share(a, b, axis):
        picked = jnp.where(chosen, a, b)
        return lax.dynamic_index_in_dim(picked, core, axis, keepdims=False)

    def pair_hop(a):
        return along_x(a, lambda x: x + 1 if x % 2 else x - 1)

    def partner_hop(a):
        return along_x(a, lambda x: x ^ 1)

    def y_hop(a):
        return lax.ppermute(a, ("y", "core"), split_ring("y", NY))

    mine = [jnp.stack([own[:, w], own_s[:, w]]) for w in range(2)]
    near = share(own, own_s, 1)
    side_p, near_1 = y_hop(mine[0]), pair_hop(near)
    mine_t, side_p, near_1, both = lax.optimization_barrier((mine[1], side_p, near_1, both))
    dealt = deal(both)
    beside_p = jnp.where(chosen, side_p[0], side_p[1])
    side_t, beside_p1, near_2 = y_hop(mine_t), pair_hop(beside_p), partner_hop(near_1)
    side_ps, near_1s = swap_core(side_p), swap_core(near_1)
    side_t, beside_p1, near_2, side_ps, near_1s = lax.optimization_barrier(
        (side_t, beside_p1, near_2, side_ps, near_1s)
    )
    beside_t = jnp.where(chosen, side_t[0], side_t[1])
    far = y_hop(jnp.stack([side_p[0], side_t[0]]))
    beside_t1, beside_p2 = pair_hop(beside_t), partner_hop(beside_p1)
    side_ts, near_2s, beside_p1s = swap_core(side_t), swap_core(near_2), swap_core(beside_p1)
    far, beside_t1, beside_p2, side_ts, near_2s, beside_p1s, dealt = lax.optimization_barrier(
        (far, beside_t1, beside_p2, side_ts, near_2s, beside_p1s, dealt)
    )
    far_s = swap_core(far)
    away_1, beside_t2 = pair_hop(share(far, far_s, 0)), partner_hop(beside_t1)
    beside_p2s, beside_t1s = swap_core(beside_p2), swap_core(beside_t1)
    away_1, beside_t2, beside_p2s, beside_t1s = lax.optimization_barrier(
        (away_1, beside_t2, beside_p2s, beside_t1s)
    )
    away_2 = partner_hop(away_1)
    flat = [own, own_s, far, far_s, side_p, side_ps, side_t, side_ts]
    flat += [near_1, near_1s, near_2, near_2s]
    flat += [beside_p1, beside_p1s, beside_p2, beside_p2s]
    flat += [beside_t1, beside_t1s, beside_t2, swap_core(beside_t2)]
    flat += [away_1, swap_core(away_1), away_2, swap_core(away_2)]
    return dealt, flat


def pieces_of(flat, w):
    across = [flat[8 + 4 * k : 12 + 4 * k] for k in (0, 1 + w, 3)]
    return flat[:4] + flat[4 + 2 * w : 6 + 2 * w] + across[0] + across[1] + across[2]


N_PIECES = 18


def place_all(w, where, pieces, full, sem):
    y, xh, core, g = (where[i] for i in range(1, 5))
    own, own_s, far, far_s, side, side_s = pieces[:6]
    turn = jnp.where(core == 0, -1, 1)

    def copy(src, group, dy, h):
        dst = full.at[pl.ds(4 * group, 4), lax.rem(y + NY + dy, NY), h]
        pltpu.make_async_copy(src, dst, sem).start()

    copy(own.at[:, w], core, 0, xh)
    copy(own_s.at[:, w], 1 - core, 0, xh)
    for r in range(2):
        copy(side.at[r], jnp.bitwise_xor(core, r), turn, xh)
        copy(side_s.at[r], jnp.bitwise_xor(1 - core, r), -turn, xh)
    copy(far.at[w], core, 2, xh)
    copy(far_s.at[w], 1 - core, 2, xh)
    for way, group in ((0, 1 - g), (2, g)):
        near, beside, away = (pieces[6 + 4 * k + way : 8 + 4 * k + way] for k in range(3))
        copy(beside[0], group, turn, 1 - xh)
        copy(beside[1], group, -turn, 1 - xh)

        @pl.when(core == w)
        def _():
            copy(near[0], group, 0, 1 - xh)
            copy(away[0], group, 2, 1 - xh)

        @pl.when(core != w)
        def _():
            copy(near[1], group, 0, 1 - xh)
            copy(away[1], group, 2, 1 - xh)


def turn_columns(where, src, dst):
    size = dst.shape[1] // NZ
    for i in range(NZ):
        at = lax.rem(where[0] + NZ - 3 + i, NZ) * size
        dst[:, i * size : (i + 1) * size] = src[:, pl.ds(pl.multiple_of(at, size), size)]


def wait_all(full, sem):
    pltpu.make_async_copy(full, full, sem).wait()


def silu(v):
    return v / (1.0 + jnp.exp(-v))


TILE = 512


def prior_dot(h, full, n):
    cols = pl.ds(pl.multiple_of(n * TILE, TILE), TILE)
    return jnp.dot(h, full[:, :, :, :, cols].reshape(h.shape[1], TILE), preferred_element_type=F32), cols


def first_kernel(where, dealt, *refs):
    pieces, (latents, full, turned, sem) = refs[:N_PIECES], refs[N_PIECES:]
    place_all(0, where, pieces, full, sem)
    width = dealt.shape[1] - latents.shape[1]
    turn_columns(where, dealt, turned)
    wait_all(full, sem)

    @pl.loop(0, latents.shape[1] // TILE)
    def _(n):
        acc, cols = prior_dot(turned[...], full, n)
        embed = dealt[:, pl.ds(pl.multiple_of(width + n * TILE, TILE), TILE)]
        latents[:, cols] = (acc + embed.astype(F32)).astype(BF16)


def step_kernel(last, scale, where, states_in, latents_in, trunk_hbm, head, policy, action_w, reward_w, spread, act_noise, lat_noise, *refs):
    refs = list(refs)
    if last:
        value_0, reward_0 = refs[:2]
        refs = refs[2:]
    p_pieces, t_pieces, refs = refs[:N_PIECES], refs[N_PIECES : 2 * N_PIECES], refs[2 * N_PIECES :]
    if last:
        states_out, outs, refs = refs[0], refs[1], refs[2:]
    else:
        states_out, latents_out, value_out, reward_out = refs[:4]
        refs = refs[4:]
    p_full, t_full, trunk_w, trunk, mixed, turned_h, turned_z, sems = refs[:8]
    if last:
        latents_out = refs[8]
    trunk_copy = pltpu.make_async_copy(trunk_hbm, trunk_w, sems.at[0])
    trunk_copy.start()
    place_all(1, where, t_pieces, t_full, sems.at[1])
    place_all(0, where, p_pieces, p_full, sems.at[2])
    turn_columns(where, latents_in, turned_z)
    trunk_copy.wait()
    rows, width = mixed.shape
    hidden = trunk_w.shape[1]

    def critic(z_ref):
        def tile(n, value):
            cols = pl.ds(pl.multiple_of(n * TILE, TILE), TILE)
            pre = jnp.dot(z_ref[...], trunk_w[:, cols], preferred_element_type=F32)
            out = silu(pre).astype(BF16)
            trunk[:, cols] = out
            part = out.astype(F32) * head[:, cols].astype(F32)
            return value + jnp.sum(part, axis=1, keepdims=True)

        return lax.fori_loop(0, hidden // TILE, tile, jnp.zeros((rows, 1), F32))

    value = critic(latents_in)
    action = jnp.tanh(
        jnp.dot(trunk[...], policy[...], preferred_element_type=F32) + act_noise[...].astype(F32)
    ).astype(BF16)
    wait_all(t_full, sems.at[1])
    blocks = t_full.shape[3] // 16
    block = width // blocks
    square = jnp.zeros((rows, 1), F32)
    for q in range(blocks):

        def tile(n, square):
            cols = pl.ds(pl.multiple_of(n * TILE, TILE), TILE)
            at = pl.ds(pl.multiple_of(q * block + n * TILE, TILE), TILE)
            weight = t_full[:, :, :, q * 16 : (q + 1) * 16, cols].reshape(latents_in.shape[1], TILE)
            drive = jnp.dot(turned_z[...], weight, preferred_element_type=F32) + jnp.dot(
                action, action_w[:, at], preferred_element_type=F32
            )
            m = states_in[:, at].astype(F32) + silu(drive)
            mixed[:, at] = m
            return square + jnp.sum(m * m, axis=1, keepdims=True)

        square = lax.fori_loop(0, block // TILE, tile, square)
    norm = lax.rsqrt(square * (1.0 / width) + EPS)

    def normed(n, reward):
        at = pl.ds(pl.multiple_of(n * TILE, TILE), TILE)
        out = (mixed[:, at] * norm).astype(BF16)
        states_out[:, at] = out
        return reward + jnp.sum(out.astype(F32) * reward_w[:, at].astype(F32), axis=1, keepdims=True)

    reward = lax.fori_loop(0, width // TILE, normed, jnp.zeros((rows, 1), F32))
    turn_columns(where, states_out, turned_h)
    wait_all(p_full, sems.at[2])

    @pl.loop(0, latents_out.shape[1] // TILE)
    def _(n):
        acc, cols = prior_dot(turned_h[...], p_full, n)
        latents_out[:, cols] = (acc + spread[:, cols] * lat_noise[:, cols].astype(F32)).astype(BF16)

    if not last:
        value_out[...] = value
        reward_out[...] = reward
        return
    last_value = critic(latents_out)
    second = reward + GAMMA * ((1.0 - LAMBDA) * last_value + LAMBDA * last_value)
    first = reward_0[...] + GAMMA * ((1.0 - LAMBDA) * value + LAMBDA * second)
    place = lax.broadcasted_iota(jnp.int32, (rows, 128), 1)
    out = jnp.where(place == 0, first, jnp.where(place == 1, second, 0.0))
    out = jnp.where(place == 2, (value_0[...] - first) * scale, out)
    out = jnp.where(place == 3, (value - second) * scale, out)
    outs[...] = out


VMEM_SPEC = pl.BlockSpec(memory_space=pltpu.VMEM)
ANY_SPEC = pl.BlockSpec(memory_space=pl.ANY)
SMEM_SPEC = pl.BlockSpec(memory_space=pltpu.SMEM)
LIMIT = 50 * 2**20


def full_scratch(cols):
    return pltpu.VMEM((NZ, NY, NX, 64, cols), BF16)


def first_call(where, dealt, pieces, cols):
    return pl.pallas_call(
        first_kernel,
        name="first_latents",
        out_shape=jax.ShapeDtypeStruct((dealt.shape[0], cols), BF16),
        in_specs=[SMEM_SPEC, VMEM_SPEC] + [ANY_SPEC] * len(pieces),
        out_specs=VMEM_SPEC,
        scratch_shapes=[
            full_scratch(cols),
            pltpu.VMEM((dealt.shape[0], dealt.shape[1] - cols), BF16),
            pltpu.SemaphoreType.DMA,
        ],
        compiler_params=pltpu.CompilerParams(vmem_limit_bytes=LIMIT),
        cost_estimate=pl.CostEstimate(flops=2 * 128 * 4096 * 1024, bytes_accessed=10 * 2**20, transcendentals=0),
    )(where, dealt, *pieces)


def step_call(last, scale, where, states, latents, weights, noise, early, p_pieces, t_pieces):
    trunk_weight, head, policy, action_w, reward_w, spread = weights
    rows, cols = latents.shape
    width, hidden = action_w.shape[1], trunk_weight.shape[1]
    column = jax.ShapeDtypeStruct((rows, 1), F32)
    shapes = [jax.ShapeDtypeStruct((rows, width), BF16)]
    if last:
        shapes += [jax.ShapeDtypeStruct((rows, 128), F32)]
    else:
        shapes += [jax.ShapeDtypeStruct((rows, cols), BF16), column, column]
    scratch = [
        full_scratch(cols),
        full_scratch(cols),
        pltpu.VMEM((cols, hidden), BF16),
        pltpu.VMEM((rows, hidden), BF16),
        pltpu.VMEM((rows, width), F32),
        pltpu.VMEM((rows, width), BF16),
        pltpu.VMEM((rows, cols), BF16),
        pltpu.SemaphoreType.DMA((3,)),
    ]
    if last:
        scratch.append(pltpu.VMEM((rows, cols), BF16))
    small = [states, latents]
    heads = [head, policy, action_w, reward_w, spread, *noise, *early]
    specs = [SMEM_SPEC] + [VMEM_SPEC] * 2 + [ANY_SPEC] + [VMEM_SPEC] * len(heads) + [ANY_SPEC] * (2 * N_PIECES)
    return pl.pallas_call(
        functools.partial(step_kernel, last, scale),
        name="last_step" if last else "first_step",
        out_shape=shapes,
        in_specs=specs,
        out_specs=[VMEM_SPEC] * len(shapes),
        scratch_shapes=scratch,
        compiler_params=pltpu.CompilerParams(vmem_limit_bytes=LIMIT),
        cost_estimate=pl.CostEstimate(flops=2 * 128 * 1024 * 10240, bytes_accessed=24 * 2**20, transcendentals=0),
    )(where, *small, trunk_weight, *heads, *p_pieces, *t_pieces)


def slope_kernel(*refs):
    pieces, (trunk_part, head_part, turned, slopes) = refs[:16], refs[16:]
    for i, piece in enumerate(pieces):
        rows = piece.shape[0]
        at = i * rows
        latents = piece[...]
        pre = jnp.dot(latents, trunk_part[...], preferred_element_type=F32)
        sig = 1.0 / (1.0 + jnp.exp(-pre))
        slopes[at : at + rows] = head_part[...] * (sig * (1.0 + pre * (1.0 - sig)))
        turned[:, at : at + rows] = latents.T


def slope_call(kept, trunk_part, head_part):
    count = 16 * kept[0][0].shape[0]
    cols, part = trunk_part.shape
    return pl.pallas_call(
        slope_kernel,
        name="slopes",
        out_shape=[jax.ShapeDtypeStruct((cols, count), BF16), jax.ShapeDtypeStruct((count, part), F32)],
        in_specs=[VMEM_SPEC] * 18,
        out_specs=[VMEM_SPEC] * 2,
        compiler_params=pltpu.CompilerParams(vmem_limit_bytes=LIMIT),
        cost_estimate=pl.CostEstimate(flops=2 * 2048 * 1024 * 256, bytes_accessed=12 * 2**20, transcendentals=0),
    )(*kept[0], *kept[1], trunk_part, head_part)


def share_kernel(where, pair, below, above, away, turned, slopes, *refs):
    outs, (back, total) = refs[:4], refs[4:]
    line = [part[c] for part in (pair, below, above, away) for c in range(2)]
    rows = pair.shape[1]
    for step in range(2):
        for i, column in enumerate(line):
            at = (8 * step + i) * rows
            back[at : at + rows] = (column[:, 2 + step : 3 + step] * slopes[at : at + rows]).astype(BF16)
    share = jnp.dot(turned[...], back[...], preferred_element_type=F32).astype(BF16)
    total[...] = share.reshape(total.shape)
    for out, d in zip(outs, (0, 1, -1, 2)):
        out[...] = total[:, lax.rem(where[1] + NY + d, NY)]


def share_call(where, columns, turned, slopes):
    cols, part = turned.shape[0], slopes.shape[1]
    block = jax.ShapeDtypeStruct((NZ, cols // (NZ * NY), part), BF16)
    return pl.pallas_call(
        share_kernel,
        name="gradient_share",
        out_shape=[block] * 4,
        in_specs=[SMEM_SPEC] + [VMEM_SPEC] * 6,
        out_specs=[VMEM_SPEC] * 4,
        scratch_shapes=[
            pltpu.VMEM(slopes.shape, BF16),
            pltpu.VMEM((NZ, NY, cols // (NZ * NY), part), BF16),
        ],
        compiler_params=pltpu.CompilerParams(vmem_limit_bytes=LIMIT),
        cost_estimate=pl.CostEstimate(flops=2 * 2048 * 1024 * 256, bytes_accessed=8 * 2**20, transcendentals=0),
    )(where, *columns, turned, slopes)


def relay_x(packed):
    near = along_x(packed[0], lambda x: x ^ 1)
    away = along_x(packed[1], lambda x: x - 1 if x % 2 == 0 else x + 1)
    return near, away


def relay_rest(near, away, xh, core):
    crossed = swap_core(jnp.stack([near[1], away[1]]))
    first, second = core == 0, xh == 0

    def by_core(mine, other):
        return [jnp.where(first, mine, other), jnp.where(first, other, mine)]

    same, other = by_core(near[0], crossed[0]), by_core(away[0], crossed[1])
    low = [jnp.where(second, same[c], other[c]) for c in range(2)]
    high = [jnp.where(second, other[c], same[c]) for c in range(2)]
    both = jnp.stack(low + high, axis=1)
    return both


def deal(both):
    dealt = lax.all_to_all(both, ("z", "y"), split_axis=0, concat_axis=0, tiled=True)
    return dealt.reshape(-1, dealt.shape[-1])


def x_gather(latents):
    mine = [latents] + [along_x(latents, lambda x, d=d: x + d) for d in (1, -1, 2)]
    return [swap_core(mine[0])] + mine


def x_gather_rest(line):
    pieces = [line[1], line[0]]
    for a in line[2:]:
        pieces += [a, swap_core(a)]
    return pieces


def x_columns(column):
    pair = jnp.stack([column, swap_core(column)])
    return [pair] + [along_x(pair, lambda x, d=d: x + d) for d in (1, -1, 2)]


def local(
    replay_states,
    replay_embed,
    replay_index,
    episode_first,
    prior_weight,
    transition_weight,
    action_weight,
    trunk_weight,
    value_head,
    policy_head,
    reward_head,
    latent_scale,
    action_noise,
    latent_noise,
):
    g, z, y = lax.axis_index("grp"), lax.axis_index("z"), lax.axis_index("y")
    xh, core = lax.axis_index("xh"), lax.axis_index("core")
    width = replay_states.shape[1]
    rows = replay_index.shape[0]
    order = jnp.stack([replay_index, episode_first]).reshape(2, NZ * NY, NX, NC)
    order = jnp.transpose(order, (2, 3, 0, 1))
    order = jnp.where(xh == 0, order, order[::-1])
    order = jnp.where(core == 0, order, order[:, ::-1])
    order = jnp.swapaxes(order, 1, 2).swapaxes(0, 1).reshape(2, rows)

    def packed_of(order):
        keep = (1 - order[1]).astype(BF16)[:, None]
        return jnp.concatenate(
            [jnp.take(replay_states, order[0], axis=0) * keep, jnp.take(replay_embed, order[0], axis=0)],
            axis=1,
        ).reshape(NX, NC, NZ * NY, -1)

    dealt, flat = gather_weights(prior_weight, transition_weight, g, core, xh, order, packed_of)
    p_pieces, t_pieces = pieces_of(flat, 0), pieces_of(flat, 1)
    where = jnp.stack([z, y, xh, core, g]).astype(jnp.int32)
    steps = action_noise.shape[0]
    hidden_units = trunk_weight.shape[1]
    cols = prior_weight.shape[1]
    part = hidden_units // 8
    slot = (g * 2 + xh) * 2 + core
    trunk_part = lax.dynamic_slice(trunk_weight, (0, slot * part), (trunk_weight.shape[0], part))
    head_part = lax.dynamic_slice(value_head, (slot * part,), (part,)).astype(F32)
    count = lax.axis_size("grp") * NZ * NY * NX * NC
    grad_scale = 4.0 * (float(hidden_units) / float(count * rows * steps)) ** 0.5
    weights = (
        trunk_weight,
        value_head[None],
        policy_head,
        action_weight,
        reward_head[None],
        latent_scale[None],
    )

    latents = first_call(where, dealt, p_pieces, cols)
    latents, trunk_part, head_part = lax.optimization_barrier((latents, trunk_part, head_part))
    kept = [x_gather(latents)]
    states, latents, value_0, reward_0 = step_call(
        False, grad_scale, where, dealt, latents, weights, (action_noise[0], latent_noise[0]), (), p_pieces, t_pieces
    )
    latents, kept[0] = lax.optimization_barrier((latents, kept[0]))
    kept.append(x_gather(latents))
    states, outs = step_call(
        True, grad_scale, where, states, latents, weights, (action_noise[1], latent_noise[1]), (value_0, reward_0), p_pieces, t_pieces
    )
    columns = x_columns(outs)
    kept = [x_gather_rest(line) for line in kept]
    turned, slopes = slope_call(kept, trunk_part, head_part[None])
    keep, *others = share_call(where, columns, turned, slopes)
    targets = outs[:, :2].T
    met = keep.astype(F32)
    for block, d in zip(others, (1, -1, 2)):
        met = met + lax.ppermute(block, "y", shift(NY, d)).astype(F32)
    sent = met.astype(BF16).reshape(1, NZ, NX * NC, -1, part)
    sent = jnp.concatenate([sent, sent], axis=0).reshape(2 * NZ * NX * NC, -1, part)
    parts = lax.all_to_all(sent, ("grp", "z", "xh", "core"), split_axis=0, concat_axis=0, tiled=True)
    parts = jnp.sum(parts.astype(F32).reshape(2, NZ, NX * NC, -1, part), axis=1)
    trunk_grad = jnp.transpose(parts, (2, 0, 1, 3)).reshape(-1, hidden_units)
    return (states, targets, trunk_grad)


def solution(mesh):
    fine = Mesh(mesh.devices.reshape(2, NZ, NY, NX, NC), AXES)
    return jax.shard_map(
        local,
        mesh=fine,
        in_specs=(
            P(AXES, None),
            P(AXES, None),
            P(AXES),
            P(AXES),
            P(FSDP, None),
            P(FSDP, None),
            P(),
            P(),
            P(),
            P(),
            P(),
            P(),
            P(None, AXES, None),
            P(None, AXES, None),
        ),
        out_specs=(P(AXES, None), P(None, AXES), P(FSDP, None)),
        check_vma=False,
    )
```

```python
import functools

import jax
import jax.numpy as jnp
from jax import lax
from jax.experimental import pallas as pl
from jax.experimental.pallas import tpu as pltpu
from jax.sharding import Mesh, PartitionSpec as P

GAMMA = 0.985
LAMBDA = 0.95
EPS = 1e-06
F32 = jnp.float32
BF16 = jnp.bfloat16

NZ, NY, NX, NC = 8, 4, 2, 2
AXES = ("grp", "z", "y", "xh", "core")
FSDP = ("z", "y", "xh", "core")


def shift(n, d):
    return [(i, (i + d) % n) for i in range(n)]


def x_line(move):
    pairs = []
    for g in range(2):
        for h in range(2):
            to = move(2 * h + g) % 4
            pairs.append((2 * g + h, 2 * (to % 2) + to // 2))
    return pairs


def along_x(a, move):
    return lax.ppermute(a, ("grp", "xh"), x_line(move))


def swap_core(a):
    return lax.ppermute(a, "core", shift(2, 1))


def split_ring(axis, n):
    return [(2 * i + c, 2 * ((i + 1 - 2 * c) % n) + c) for i in range(n) for c in range(2)]


def gather_weights(prior, transition, g, core, xh, order, packed_of):
    depth = transition.shape[0]
    cols = prior.shape[1]
    blocks = transition.shape[1] // cols
    other_p, other_t = swap_core(prior), swap_core(transition)

    def both(mine, other):
        return jnp.where(core == 0, jnp.concatenate([mine, other]), jnp.concatenate([other, mine]))

    chip_t = both(transition, other_t).reshape(2 * depth, blocks, cols)
    unit = jnp.stack([both(prior, other_p), jnp.swapaxes(chip_t, 0, 1).reshape(-1, cols)])
    unit, order = lax.optimization_barrier((unit, order))
    ring = [unit]
    for hop in range(4):
        pairs = split_ring("z", NZ)
        if hop == 3:
            pairs = [p for p in pairs if p[0] % 2]
        ring.append(lax.ppermute(ring[-1], ("z", "core"), pairs))
        if hop == 0:
            packed = packed_of(order)
            ring[-1], packed = lax.optimization_barrier((ring[-1], packed))
            near, away = relay_x(packed)
    ring[4], near, away = lax.optimization_barrier((ring[4], near, away))
    both = relay_rest(near, away, xh, core)
    own = jnp.where(core == 0, jnp.stack(ring[3::-1], axis=1), jnp.stack(ring[1:], axis=1))
    chosen = g == core

    def pair_hop(a):
        return along_x(a, lambda x: x + 1 if x % 2 else x - 1)

    def partner_hop(a):
        return along_x(a, lambda x: x ^ 1)

    def y_hop(a):
        return lax.ppermute(a, ("y", "core"), split_ring("y", NY))

    def half(a):
        return lax.dynamic_index_in_dim(a, g, 0, keepdims=False)

    near_1 = pair_hop(half(own))
    own_s = swap_core(own)
    mine = [jnp.stack([own[w], own_s[w]]) for w in range(2)]
    side_p = y_hop(mine[0])
    mine_t, side_p, near_1 = lax.optimization_barrier((mine[1], side_p, near_1))
    dealt = deal(both)
    beside_p = jnp.where(chosen, side_p[0], side_p[1])
    side_t, beside_p1, near_2 = y_hop(mine_t), pair_hop(beside_p), partner_hop(near_1)
    side_ps, near_1s = swap_core(side_p), swap_core(near_1)
    mine_t, beside_p1, near_2, near_1s, side_ps = lax.optimization_barrier(
        (mine_t, beside_p1, near_2, near_1s, side_ps)
    )
    beside_p2 = partner_hop(beside_p1)
    beside_p1s = swap_core(beside_p1)
    far = y_hop(jnp.stack([side_p[0], side_t[0]]))
    beside_t1 = pair_hop(jnp.where(chosen, side_t[0], side_t[1]))
    near_2s, side_ts = swap_core(near_2), swap_core(side_t)
    far, beside_t1, beside_p2, near_2s, beside_p1s, side_ts, dealt = lax.optimization_barrier(
        (far, beside_t1, beside_p2, near_2s, beside_p1s, side_ts, dealt)
    )
    away_1, beside_t2 = pair_hop(half(far)), partner_hop(beside_t1)
    far_s, beside_p2s, beside_t1s = swap_core(far), swap_core(beside_p2), swap_core(beside_t1)
    away_1, beside_t2, far_s, beside_p2s, beside_t1s = lax.optimization_barrier(
        (away_1, beside_t2, far_s, beside_p2s, beside_t1s)
    )
    away_2 = partner_hop(away_1)
    flat = [own, own_s, far, far_s, side_p, side_ps, side_t, side_ts]
    flat += [near_1, near_1s, near_2, near_2s]
    flat += [beside_p1, beside_p1s, beside_p2, beside_p2s]
    flat += [beside_t1, beside_t1s, beside_t2, swap_core(beside_t2)]
    flat += [away_1, swap_core(away_1), away_2, swap_core(away_2)]
    return dealt, flat


def pieces_of(flat, w):
    across = [flat[8 + 4 * k : 12 + 4 * k] for k in (0, 1 + w, 3)]
    return flat[:4] + flat[4 + 2 * w : 6 + 2 * w] + across[0] + across[1] + across[2]


N_PIECES = 18


def place_all(w, where, pieces, full, sem):
    y, xh, core, g = (where[i] for i in range(1, 5))
    own, own_s, far, far_s, side, side_s = pieces[:6]
    turn = jnp.where(core == 0, -1, 1)

    def copy(src, group, dy, h):
        dst = full.at[pl.ds(4 * group, 4), lax.rem(y + NY + dy, NY), h]
        pltpu.make_async_copy(src, dst, sem).start()

    copy(own.at[w], core, 0, xh)
    copy(own_s.at[w], 1 - core, 0, xh)
    for r in range(2):
        copy(side.at[r], jnp.bitwise_xor(core, r), turn, xh)
        copy(side_s.at[r], jnp.bitwise_xor(1 - core, r), -turn, xh)
    copy(far.at[w], core, 2, xh)
    copy(far_s.at[w], 1 - core, 2, xh)
    near, beside, away = (pieces[6 + 4 * k : 10 + 4 * k] for k in range(3))
    for way, group in ((0, 1 - g), (2, g)):
        copy(beside[way], group, turn, 1 - xh)
        copy(beside[way + 1], group, -turn, 1 - xh)

        @pl.when(group == w)
        def _():
            copy(near[way], core, 0, 1 - xh)
            copy(near[way + 1], 1 - core, 0, 1 - xh)
            copy(away[way], core, 2, 1 - xh)
            copy(away[way + 1], 1 - core, 2, 1 - xh)


def turn_columns(where, src, dst):
    size = dst.shape[1] // NZ
    for i in range(NZ):
        at = lax.rem(where[0] + NZ - 3 + i, NZ) * size
        dst[:, i * size : (i + 1) * size] = src[:, pl.ds(pl.multiple_of(at, size), size)]


def wait_all(full, sem):
    pltpu.make_async_copy(full, full, sem).wait()


def silu(v):
    return v / (1.0 + jnp.exp(-v))


TILE = 512


def prior_dot(h, full, n):
    cols = pl.ds(pl.multiple_of(n * TILE, TILE), TILE)
    return jnp.dot(h, full[:, :, :, :, cols].reshape(h.shape[1], TILE), preferred_element_type=F32), cols


def first_kernel(where, dealt, *refs):
    pieces, (latents, full, turned, sem) = refs[:N_PIECES], refs[N_PIECES:]
    place_all(0, where, pieces, full, sem)
    width = dealt.shape[1] - latents.shape[1]
    turn_columns(where, dealt, turned)
    wait_all(full, sem)

    @pl.loop(0, latents.shape[1] // TILE)
    def _(n):
        acc, cols = prior_dot(turned[...], full, n)
        embed = dealt[:, pl.ds(pl.multiple_of(width + n * TILE, TILE), TILE)]
        latents[:, cols] = (acc + embed.astype(F32)).astype(BF16)


def step_kernel(last, scale, where, states_in, latents_in, trunk_hbm, head, policy, action_w, reward_w, spread, act_noise, lat_noise, *refs):
    refs = list(refs)
    if last:
        value_0, reward_0 = refs[:2]
        refs = refs[2:]
    p_pieces, t_pieces, refs = refs[:N_PIECES], refs[N_PIECES : 2 * N_PIECES], refs[2 * N_PIECES :]
    if last:
        states_out, outs, refs = refs[0], refs[1], refs[2:]
    else:
        states_out, latents_out, value_out, reward_out = refs[:4]
        refs = refs[4:]
    p_full, t_full, trunk_w, trunk, mixed, turned_h, turned_z, sems = refs[:8]
    if last:
        latents_out = refs[8]
    trunk_copy = pltpu.make_async_copy(trunk_hbm, trunk_w, sems.at[0])
    trunk_copy.start()
    place_all(1, where, t_pieces, t_full, sems.at[1])
    place_all(0, where, p_pieces, p_full, sems.at[2])
    turn_columns(where, latents_in, turned_z)
    trunk_copy.wait()
    rows, width = mixed.shape
    hidden = trunk_w.shape[1]

    def critic(z_ref):
        def tile(n, value):
            cols = pl.ds(pl.multiple_of(n * TILE, TILE), TILE)
            pre = jnp.dot(z_ref[...], trunk_w[:, cols], preferred_element_type=F32)
            out = silu(pre).astype(BF16)
            trunk[:, cols] = out
            part = out.astype(F32) * head[:, cols].astype(F32)
            return value + jnp.sum(part, axis=1, keepdims=True)

        return lax.fori_loop(0, hidden // TILE, tile, jnp.zeros((rows, 1), F32))

    value = critic(latents_in)
    action = jnp.tanh(
        jnp.dot(trunk[...], policy[...], preferred_element_type=F32) + act_noise[...].astype(F32)
    ).astype(BF16)
    wait_all(t_full, sems.at[1])
    blocks = t_full.shape[3] // 16
    block = width // blocks
    square = jnp.zeros((rows, 1), F32)
    for q in range(blocks):

        def tile(n, square):
            cols = pl.ds(pl.multiple_of(n * TILE, TILE), TILE)
            at = pl.ds(pl.multiple_of(q * block + n * TILE, TILE), TILE)
            weight = t_full[:, :, :, q * 16 : (q + 1) * 16, cols].reshape(latents_in.shape[1], TILE)
            drive = jnp.dot(turned_z[...], weight, preferred_element_type=F32) + jnp.dot(
                action, action_w[:, at], preferred_element_type=F32
            )
            m = states_in[:, at].astype(F32) + silu(drive)
            mixed[:, at] = m
            return square + jnp.sum(m * m, axis=1, keepdims=True)

        square = lax.fori_loop(0, block // TILE, tile, square)
    norm = lax.rsqrt(square * (1.0 / width) + EPS)

    def normed(n, reward):
        at = pl.ds(pl.multiple_of(n * TILE, TILE), TILE)
        out = (mixed[:, at] * norm).astype(BF16)
        states_out[:, at] = out
        return reward + jnp.sum(out.astype(F32) * reward_w[:, at].astype(F32), axis=1, keepdims=True)

    reward = lax.fori_loop(0, width // TILE, normed, jnp.zeros((rows, 1), F32))
    turn_columns(where, states_out, turned_h)
    wait_all(p_full, sems.at[2])

    @pl.loop(0, latents_out.shape[1] // TILE)
    def _(n):
        acc, cols = prior_dot(turned_h[...], p_full, n)
        latents_out[:, cols] = (acc + spread[:, cols] * lat_noise[:, cols].astype(F32)).astype(BF16)

    if not last:
        value_out[...] = value
        reward_out[...] = reward
        return
    last_value = critic(latents_out)
    second = reward + GAMMA * ((1.0 - LAMBDA) * last_value + LAMBDA * last_value)
    first = reward_0[...] + GAMMA * ((1.0 - LAMBDA) * value + LAMBDA * second)
    place = lax.broadcasted_iota(jnp.int32, (rows, 128), 1)
    out = jnp.where(place == 0, first, jnp.where(place == 1, second, 0.0))
    out = jnp.where(place == 2, (value_0[...] - first) * scale, out)
    out = jnp.where(place == 3, (value - second) * scale, out)
    outs[...] = out


VMEM_SPEC = pl.BlockSpec(memory_space=pltpu.VMEM)
ANY_SPEC = pl.BlockSpec(memory_space=pl.ANY)
SMEM_SPEC = pl.BlockSpec(memory_space=pltpu.SMEM)
LIMIT = 50 * 2**20


def full_scratch(cols):
    return pltpu.VMEM((NZ, NY, NX, 64, cols), BF16)


def first_call(where, dealt, pieces, cols):
    return pl.pallas_call(
        first_kernel,
        name="first_latents",
        out_shape=jax.ShapeDtypeStruct((dealt.shape[0], cols), BF16),
        in_specs=[SMEM_SPEC, VMEM_SPEC] + [ANY_SPEC] * len(pieces),
        out_specs=VMEM_SPEC,
        scratch_shapes=[
            full_scratch(cols),
            pltpu.VMEM((dealt.shape[0], dealt.shape[1] - cols), BF16),
            pltpu.SemaphoreType.DMA,
        ],
        compiler_params=pltpu.CompilerParams(vmem_limit_bytes=LIMIT),
        cost_estimate=pl.CostEstimate(flops=2 * 128 * 4096 * 1024, bytes_accessed=10 * 2**20, transcendentals=0),
    )(where, dealt, *pieces)


def step_call(last, scale, where, states, latents, weights, noise, early, p_pieces, t_pieces):
    trunk_weight, head, policy, action_w, reward_w, spread = weights
    rows, cols = latents.shape
    width, hidden = action_w.shape[1], trunk_weight.shape[1]
    column = jax.ShapeDtypeStruct((rows, 1), F32)
    shapes = [jax.ShapeDtypeStruct((rows, width), BF16)]
    if last:
        shapes += [jax.ShapeDtypeStruct((rows, 128), F32)]
    else:
        shapes += [jax.ShapeDtypeStruct((rows, cols), BF16), column, column]
    scratch = [
        full_scratch(cols),
        full_scratch(cols),
        pltpu.VMEM((cols, hidden), BF16),
        pltpu.VMEM((rows, hidden), BF16),
        pltpu.VMEM((rows, width), F32),
        pltpu.VMEM((rows, width), BF16),
        pltpu.VMEM((rows, cols), BF16),
        pltpu.SemaphoreType.DMA((3,)),
    ]
    if last:
        scratch.append(pltpu.VMEM((rows, cols), BF16))
    small = [states, latents]
    heads = [head, policy, action_w, reward_w, spread, *noise, *early]
    specs = [SMEM_SPEC] + [VMEM_SPEC] * 2 + [ANY_SPEC] + [VMEM_SPEC] * len(heads) + [ANY_SPEC] * (2 * N_PIECES)
    return pl.pallas_call(
        functools.partial(step_kernel, last, scale),
        name="last_step" if last else "first_step",
        out_shape=shapes,
        in_specs=specs,
        out_specs=[VMEM_SPEC] * len(shapes),
        scratch_shapes=scratch,
        compiler_params=pltpu.CompilerParams(vmem_limit_bytes=LIMIT),
        cost_estimate=pl.CostEstimate(flops=2 * 128 * 1024 * 10240, bytes_accessed=24 * 2**20, transcendentals=0),
    )(where, *small, trunk_weight, *heads, *p_pieces, *t_pieces)


def slope_kernel(*refs):
    pieces, (trunk_part, head_part, turned, slopes) = refs[:16], refs[16:]
    for i, piece in enumerate(pieces):
        rows = piece.shape[0]
        at = i * rows
        latents = piece[...]
        pre = jnp.dot(latents, trunk_part[...], preferred_element_type=F32)
        sig = 1.0 / (1.0 + jnp.exp(-pre))
        slopes[at : at + rows] = head_part[...] * (sig * (1.0 + pre * (1.0 - sig)))
        turned[:, at : at + rows] = latents.T


def slope_call(kept, trunk_part, head_part):
    count = 16 * kept[0][0].shape[0]
    cols, part = trunk_part.shape
    return pl.pallas_call(
        slope_kernel,
        name="slopes",
        out_shape=[jax.ShapeDtypeStruct((cols, count), BF16), jax.ShapeDtypeStruct((count, part), F32)],
        in_specs=[VMEM_SPEC] * 18,
        out_specs=[VMEM_SPEC] * 2,
        compiler_params=pltpu.CompilerParams(vmem_limit_bytes=LIMIT),
        cost_estimate=pl.CostEstimate(flops=2 * 2048 * 1024 * 256, bytes_accessed=12 * 2**20, transcendentals=0),
    )(*kept[0], *kept[1], trunk_part, head_part)


def share_kernel(where, pair, below, above, away, turned, slopes, *refs):
    outs, (back, total) = refs[:4], refs[4:]
    line = [part[c] for part in (pair, below, above, away) for c in range(2)]
    rows = pair.shape[1]
    for step in range(2):
        for i, column in enumerate(line):
            at = (8 * step + i) * rows
            back[at : at + rows] = (column[:, 2 + step : 3 + step] * slopes[at : at + rows]).astype(BF16)
    share = jnp.dot(turned[...], back[...], preferred_element_type=F32).astype(BF16)
    total[...] = share.reshape(total.shape)
    for out, d in zip(outs, (0, 1, -1, 2)):
        out[...] = total[:, lax.rem(where[1] + NY + d, NY)]


def share_call(where, columns, turned, slopes):
    cols, part = turned.shape[0], slopes.shape[1]
    block = jax.ShapeDtypeStruct((NZ, cols // (NZ * NY), part), BF16)
    return pl.pallas_call(
        share_kernel,
        name="gradient_share",
        out_shape=[block] * 4,
        in_specs=[SMEM_SPEC] + [VMEM_SPEC] * 6,
        out_specs=[VMEM_SPEC] * 4,
        scratch_shapes=[
            pltpu.VMEM(slopes.shape, BF16),
            pltpu.VMEM((NZ, NY, cols // (NZ * NY), part), BF16),
        ],
        compiler_params=pltpu.CompilerParams(vmem_limit_bytes=LIMIT),
        cost_estimate=pl.CostEstimate(flops=2 * 2048 * 1024 * 256, bytes_accessed=8 * 2**20, transcendentals=0),
    )(where, *columns, turned, slopes)


def relay_x(packed):
    near = along_x(packed[0], lambda x: x ^ 1)
    away = along_x(packed[1], lambda x: x - 1 if x % 2 == 0 else x + 1)
    return near, away


def relay_rest(near, away, xh, core):
    crossed = swap_core(jnp.stack([near[1], away[1]]))
    first, second = core == 0, xh == 0

    def by_core(mine, other):
        return [jnp.where(first, mine, other), jnp.where(first, other, mine)]

    same, other = by_core(near[0], crossed[0]), by_core(away[0], crossed[1])
    low = [jnp.where(second, same[c], other[c]) for c in range(2)]
    high = [jnp.where(second, other[c], same[c]) for c in range(2)]
    both = jnp.stack(low + high, axis=1)
    return both


def deal(both):
    dealt = lax.all_to_all(both, ("z", "y"), split_axis=0, concat_axis=0, tiled=True)
    return dealt.reshape(-1, dealt.shape[-1])


def x_gather(latents):
    mine = [latents] + [along_x(latents, lambda x, d=d: x + d) for d in (1, -1, 2)]
    return [swap_core(mine[0])] + mine


def x_gather_rest(line):
    pieces = [line[1], line[0]]
    for a in line[2:]:
        pieces += [a, swap_core(a)]
    return pieces


def x_columns(column):
    pair = jnp.stack([column, swap_core(column)])
    return [pair] + [along_x(pair, lambda x, d=d: x + d) for d in (1, -1, 2)]


def local(
    replay_states,
    replay_embed,
    replay_index,
    episode_first,
    prior_weight,
    transition_weight,
    action_weight,
    trunk_weight,
    value_head,
    policy_head,
    reward_head,
    latent_scale,
    action_noise,
    latent_noise,
):
    g, z, y = lax.axis_index("grp"), lax.axis_index("z"), lax.axis_index("y")
    xh, core = lax.axis_index("xh"), lax.axis_index("core")
    width = replay_states.shape[1]
    rows = replay_index.shape[0]
    order = jnp.stack([replay_index, episode_first]).reshape(2, NZ * NY, NX, NC)
    order = jnp.transpose(order, (2, 3, 0, 1))
    order = jnp.where(xh == 0, order, order[::-1])
    order = jnp.where(core == 0, order, order[:, ::-1])
    order = jnp.swapaxes(order, 1, 2).swapaxes(0, 1).reshape(2, rows)

    def packed_of(order):
        keep = (1 - order[1]).astype(BF16)[:, None]
        return jnp.concatenate(
            [jnp.take(replay_states, order[0], axis=0) * keep, jnp.take(replay_embed, order[0], axis=0)],
            axis=1,
        ).reshape(NX, NC, NZ * NY, -1)

    dealt, flat = gather_weights(prior_weight, transition_weight, g, core, xh, order, packed_of)
    p_pieces, t_pieces = pieces_of(flat, 0), pieces_of(flat, 1)
    where = jnp.stack([z, y, xh, core, g]).astype(jnp.int32)
    steps = action_noise.shape[0]
    hidden_units = trunk_weight.shape[1]
    cols = prior_weight.shape[1]
    part = hidden_units // 8
    slot = (g * 2 + xh) * 2 + core
    trunk_part = lax.dynamic_slice(trunk_weight, (0, slot * part), (trunk_weight.shape[0], part))
    head_part = lax.dynamic_slice(value_head, (slot * part,), (part,)).astype(F32)
    count = lax.axis_size("grp") * NZ * NY * NX * NC
    grad_scale = 4.0 * (float(hidden_units) / float(count * rows * steps)) ** 0.5
    weights = (
        trunk_weight,
        value_head[None],
        policy_head,
        action_weight,
        reward_head[None],
        latent_scale[None],
    )

    latents = first_call(where, dealt, p_pieces, cols)
    latents, trunk_part, head_part = lax.optimization_barrier((latents, trunk_part, head_part))
    kept = [x_gather(latents)]
    states, latents, value_0, reward_0 = step_call(
        False, grad_scale, where, dealt, latents, weights, (action_noise[0], latent_noise[0]), (), p_pieces, t_pieces
    )
    latents, kept[0] = lax.optimization_barrier((latents, kept[0]))
    kept.append(x_gather(latents))
    states, outs = step_call(
        True, grad_scale, where, states, latents, weights, (action_noise[1], latent_noise[1]), (value_0, reward_0), p_pieces, t_pieces
    )
    outs, kept[1] = lax.optimization_barrier((outs, kept[1]))
    columns = x_columns(outs)
    kept = [x_gather_rest(line) for line in kept]
    turned, slopes = slope_call(kept, trunk_part, head_part[None])
    keep, *others = share_call(where, columns, turned, slopes)
    targets = outs[:, :2].T
    met = keep.astype(F32)
    for block, d in zip(others, (1, -1, 2)):
        met = met + lax.ppermute(block, "y", shift(NY, d)).astype(F32)
    sent = met.astype(BF16).reshape(1, NZ, NX * NC, -1, part)
    sent = jnp.concatenate([sent, sent], axis=0).reshape(2 * NZ * NX * NC, -1, part)
    parts = lax.all_to_all(sent, ("grp", "z", "xh", "core"), split_axis=0, concat_axis=0, tiled=True)
    parts = jnp.sum(parts.astype(F32).reshape(2, NZ, NX * NC, -1, part), axis=1)
    trunk_grad = jnp.transpose(parts, (2, 0, 1, 3)).reshape(-1, hidden_units)
    return (states, targets, trunk_grad)


def solution(mesh):
    fine = Mesh(mesh.devices.reshape(2, NZ, NY, NX, NC), AXES)
    return jax.shard_map(
        local,
        mesh=fine,
        in_specs=(
            P(AXES, None),
            P(AXES, None),
            P(AXES),
            P(AXES),
            P(FSDP, None),
            P(FSDP, None),
            P(),
            P(),
            P(),
            P(),
            P(),
            P(),
            P(None, AXES, None),
            P(None, AXES, None),
        ),
        out_specs=(P(AXES, None), P(None, AXES), P(FSDP, None)),
        check_vma=False,
    )
```

```python
import functools

import jax
import jax.numpy as jnp
from jax import lax
from jax.experimental import pallas as pl
from jax.experimental.pallas import tpu as pltpu
from jax.sharding import Mesh, PartitionSpec as P

GAMMA = 0.985
LAMBDA = 0.95
EPS = 1e-06
F32 = jnp.float32
BF16 = jnp.bfloat16

NZ, NY, NX, NC = 8, 4, 2, 2
AXES = ("grp", "z", "y", "xh", "core")
FSDP = ("z", "y", "xh", "core")


def shift(n, d):
    return [(i, (i + d) % n) for i in range(n)]


def x_line(move):
    pairs = []
    for g in range(2):
        for h in range(2):
            to = move(2 * h + g) % 4
            pairs.append((2 * g + h, 2 * (to % 2) + to // 2))
    return pairs


def along_x(a, move):
    return lax.ppermute(a, ("grp", "xh"), x_line(move))


def swap_core(a):
    return lax.ppermute(a, "core", shift(2, 1))


def split_ring(axis, n):
    return [(2 * i + c, 2 * ((i + 1 - 2 * c) % n) + c) for i in range(n) for c in range(2)]


def gather_weights(prior, transition, g, core, xh, order, packed_of):
    depth = transition.shape[0]
    cols = prior.shape[1]
    blocks = transition.shape[1] // cols
    other_p, other_t = swap_core(prior), swap_core(transition)

    def both(mine, other):
        return jnp.where(core == 0, jnp.concatenate([mine, other]), jnp.concatenate([other, mine]))

    chip_t = both(transition, other_t).reshape(2 * depth, blocks, cols)
    unit = jnp.stack([both(prior, other_p), jnp.swapaxes(chip_t, 0, 1).reshape(-1, cols)])
    unit, order = lax.optimization_barrier((unit, order))
    ring = [unit]
    for hop in range(4):
        pairs = split_ring("z", NZ)
        if hop == 3:
            pairs = [p for p in pairs if p[0] % 2]
        ring.append(lax.ppermute(ring[-1], ("z", "core"), pairs))
        if hop == 0:
            packed = packed_of(order)
            ring[-1], packed = lax.optimization_barrier((ring[-1], packed))
            near, away = relay_x(packed)
    ring[4], near, away = lax.optimization_barrier((ring[4], near, away))
    both = relay_rest(near, away, xh, core)
    own = jnp.where(core == 0, jnp.stack(ring[3::-1], axis=1), jnp.stack(ring[1:], axis=1))
    chosen = g == core

    def pair_hop(a):
        return along_x(a, lambda x: x + 1 if x % 2 else x - 1)

    def partner_hop(a):
        return along_x(a, lambda x: x ^ 1)

    def y_hop(a):
        return lax.ppermute(a, ("y", "core"), split_ring("y", NY))

    def half(a):
        return lax.dynamic_index_in_dim(a, g, 0, keepdims=False)

    near_1 = pair_hop(half(own))
    own_s = swap_core(own)
    mine = [jnp.stack([own[w], own_s[w]]) for w in range(2)]
    side_p = y_hop(mine[0])
    mine_t, side_p, near_1 = lax.optimization_barrier((mine[1], side_p, near_1))
    beside_p = jnp.where(chosen, side_p[0], side_p[1])
    side_t, beside_p1, near_2 = y_hop(mine_t), pair_hop(beside_p), partner_hop(near_1)
    side_ps, near_1s = swap_core(side_p), swap_core(near_1)
    beside_p1, near_2, side_ps, near_1s = lax.optimization_barrier((beside_p1, near_2, side_ps, near_1s))
    beside_p2 = partner_hop(beside_p1)
    near_2s, beside_p1s = swap_core(near_2), swap_core(beside_p1)
    side_t, near_2s, beside_p1s, beside_p2 = lax.optimization_barrier((side_t, near_2s, beside_p1s, beside_p2))
    beside_t1 = pair_hop(jnp.where(chosen, side_t[0], side_t[1]))
    far = y_hop(jnp.stack([side_p[0], side_t[0]]))
    side_ts, both = lax.optimization_barrier((swap_core(side_t), both))
    dealt = deal(both)
    far, beside_t1, side_ts = lax.optimization_barrier((far, beside_t1, side_ts))
    away_1, beside_t2 = pair_hop(half(far)), partner_hop(beside_t1)
    far_s, beside_p2s, beside_t1s = swap_core(far), swap_core(beside_p2), swap_core(beside_t1)
    away_1, beside_t2, far_s, beside_p2s, beside_t1s = lax.optimization_barrier(
        (away_1, beside_t2, far_s, beside_p2s, beside_t1s)
    )
    away_2 = partner_hop(away_1)
    beside_t2s, away_1s = swap_core(beside_t2), swap_core(away_1)
    away_2, beside_t2s, away_1s, dealt = lax.optimization_barrier((away_2, beside_t2s, away_1s, dealt))
    flat = [own, own_s, far, far_s, side_p, side_ps, side_t, side_ts]
    flat += [near_1, near_1s, near_2, near_2s]
    flat += [beside_p1, beside_p1s, beside_p2, beside_p2s]
    flat += [beside_t1, beside_t1s, beside_t2, beside_t2s]
    flat += [away_1, away_1s, away_2, swap_core(away_2)]
    return dealt, flat


def pieces_of(flat, w):
    across = [flat[8 + 4 * k : 12 + 4 * k] for k in (0, 1 + w, 3)]
    return flat[:4] + flat[4 + 2 * w : 6 + 2 * w] + across[0] + across[1] + across[2]


N_PIECES = 18


def place_all(w, where, pieces, full, sem):
    y, xh, core, g = (where[i] for i in range(1, 5))
    own, own_s, far, far_s, side, side_s = pieces[:6]
    turn = jnp.where(core == 0, -1, 1)

    def copy(src, group, dy, h):
        dst = full.at[pl.ds(4 * group, 4), lax.rem(y + NY + dy, NY), h]
        pltpu.make_async_copy(src, dst, sem).start()

    copy(own.at[w], core, 0, xh)
    copy(own_s.at[w], 1 - core, 0, xh)
    for r in range(2):
        copy(side.at[r], jnp.bitwise_xor(core, r), turn, xh)
        copy(side_s.at[r], jnp.bitwise_xor(1 - core, r), -turn, xh)
    copy(far.at[w], core, 2, xh)
    copy(far_s.at[w], 1 - core, 2, xh)
    near, beside, away = (pieces[6 + 4 * k : 10 + 4 * k] for k in range(3))
    for way, group in ((0, 1 - g), (2, g)):
        copy(beside[way], group, turn, 1 - xh)
        copy(beside[way + 1], group, -turn, 1 - xh)

        @pl.when(group == w)
        def _():
            copy(near[way], core, 0, 1 - xh)
            copy(near[way + 1], 1 - core, 0, 1 - xh)
            copy(away[way], core, 2, 1 - xh)
            copy(away[way + 1], 1 - core, 2, 1 - xh)


def turn_columns(where, src, dst):
    size = dst.shape[1] // NZ
    for i in range(NZ):
        at = lax.rem(where[0] + NZ - 3 + i, NZ) * size
        dst[:, i * size : (i + 1) * size] = src[:, pl.ds(pl.multiple_of(at, size), size)]


def wait_all(full, sem):
    pltpu.make_async_copy(full, full, sem).wait()


def silu(v):
    return v / (1.0 + jnp.exp(-v))


TILE = 512


def prior_dot(h, full, n):
    cols = pl.ds(pl.multiple_of(n * TILE, TILE), TILE)
    return jnp.dot(h, full[:, :, :, :, cols].reshape(h.shape[1], TILE), preferred_element_type=F32), cols


def first_kernel(where, dealt, *refs):
    pieces, (latents, full, turned, sem) = refs[:N_PIECES], refs[N_PIECES:]
    place_all(0, where, pieces, full, sem)
    width = dealt.shape[1] - latents.shape[1]
    turn_columns(where, dealt, turned)
    wait_all(full, sem)

    @pl.loop(0, latents.shape[1] // TILE)
    def _(n):
        acc, cols = prior_dot(turned[...], full, n)
        embed = dealt[:, pl.ds(pl.multiple_of(width + n * TILE, TILE), TILE)]
        latents[:, cols] = (acc + embed.astype(F32)).astype(BF16)


def step_kernel(last, scale, where, states_in, latents_in, trunk_hbm, head, policy, action_w, reward_w, spread, act_noise, lat_noise, *refs):
    refs = list(refs)
    if last:
        value_0, reward_0 = refs[:2]
        refs = refs[2:]
    p_pieces, t_pieces, refs = refs[:N_PIECES], refs[N_PIECES : 2 * N_PIECES], refs[2 * N_PIECES :]
    if last:
        states_out, outs, refs = refs[0], refs[1], refs[2:]
    else:
        states_out, latents_out, value_out, reward_out = refs[:4]
        refs = refs[4:]
    p_full, t_full, trunk_w, trunk, mixed, turned_h, turned_z, sems = refs[:8]
    if last:
        latents_out = refs[8]
    trunk_copy = pltpu.make_async_copy(trunk_hbm, trunk_w, sems.at[0])
    trunk_copy.start()
    place_all(1, where, t_pieces, t_full, sems.at[1])
    place_all(0, where, p_pieces, p_full, sems.at[2])
    turn_columns(where, latents_in, turned_z)
    trunk_copy.wait()
    rows, width = mixed.shape
    hidden = trunk_w.shape[1]

    def critic(z_ref):
        def tile(n, value):
            cols = pl.ds(pl.multiple_of(n * TILE, TILE), TILE)
            pre = jnp.dot(z_ref[...], trunk_w[:, cols], preferred_element_type=F32)
            out = silu(pre).astype(BF16)
            trunk[:, cols] = out
            part = out.astype(F32) * head[:, cols].astype(F32)
            return value + jnp.sum(part, axis=1, keepdims=True)

        return lax.fori_loop(0, hidden // TILE, tile, jnp.zeros((rows, 1), F32))

    value = critic(latents_in)
    action = jnp.tanh(
        lax.dot_general(trunk[...], policy[...], (((1,), (1,)), ((), ())), preferred_element_type=F32)
        + act_noise[...].astype(F32)
    ).astype(BF16)
    wait_all(t_full, sems.at[1])
    blocks = t_full.shape[3] // 16
    block = width // blocks
    square = jnp.zeros((rows, 1), F32)
    for q in range(blocks):

        def tile(n, square):
            cols = pl.ds(pl.multiple_of(n * TILE, TILE), TILE)
            at = pl.ds(pl.multiple_of(q * block + n * TILE, TILE), TILE)
            weight = t_full[:, :, :, q * 16 : (q + 1) * 16, cols].reshape(latents_in.shape[1], TILE)
            drive = jnp.dot(turned_z[...], weight, preferred_element_type=F32) + jnp.dot(
                action, action_w[:, at], preferred_element_type=F32
            )
            m = states_in[:, at].astype(F32) + silu(drive)
            mixed[:, at] = m
            return square + jnp.sum(m * m, axis=1, keepdims=True)

        square = lax.fori_loop(0, block // TILE, tile, square)
    norm = lax.rsqrt(square * (1.0 / width) + EPS)

    def normed(n, reward):
        at = pl.ds(pl.multiple_of(n * TILE, TILE), TILE)
        out = (mixed[:, at] * norm).astype(BF16)
        states_out[:, at] = out
        return reward + jnp.sum(out.astype(F32) * reward_w[:, at].astype(F32), axis=1, keepdims=True)

    reward = lax.fori_loop(0, width // TILE, normed, jnp.zeros((rows, 1), F32))
    turn_columns(where, states_out, turned_h)
    wait_all(p_full, sems.at[2])

    @pl.loop(0, latents_out.shape[1] // TILE)
    def _(n):
        acc, cols = prior_dot(turned_h[...], p_full, n)
        latents_out[:, cols] = (acc + spread[:, cols] * lat_noise[:, cols].astype(F32)).astype(BF16)

    if not last:
        value_out[...] = value
        reward_out[...] = reward
        return
    last_value = critic(latents_out)
    second = reward + GAMMA * ((1.0 - LAMBDA) * last_value + LAMBDA * last_value)
    first = reward_0[...] + GAMMA * ((1.0 - LAMBDA) * value + LAMBDA * second)
    place = lax.broadcasted_iota(jnp.int32, (rows, 128), 1)
    out = jnp.where(place == 0, first, jnp.where(place == 1, second, 0.0))
    out = jnp.where(place == 2, (value_0[...] - first) * scale, out)
    out = jnp.where(place == 3, (value - second) * scale, out)
    outs[...] = out


VMEM_SPEC = pl.BlockSpec(memory_space=pltpu.VMEM)
ANY_SPEC = pl.BlockSpec(memory_space=pl.ANY)
SMEM_SPEC = pl.BlockSpec(memory_space=pltpu.SMEM)
LIMIT = 50 * 2**20
SMALL_LIMIT = 24 * 2**20


def full_scratch(cols):
    return pltpu.VMEM((NZ, NY, NX, 64, cols), BF16)


def first_call(where, dealt, pieces, cols):
    return pl.pallas_call(
        first_kernel,
        name="first_latents",
        out_shape=jax.ShapeDtypeStruct((dealt.shape[0], cols), BF16),
        in_specs=[SMEM_SPEC, VMEM_SPEC] + [ANY_SPEC] * len(pieces),
        out_specs=VMEM_SPEC,
        scratch_shapes=[
            full_scratch(cols),
            pltpu.VMEM((dealt.shape[0], dealt.shape[1] - cols), BF16),
            pltpu.SemaphoreType.DMA,
        ],
        compiler_params=pltpu.CompilerParams(vmem_limit_bytes=LIMIT),
        cost_estimate=pl.CostEstimate(flops=2 * 128 * 4096 * 1024, bytes_accessed=10 * 2**20, transcendentals=0),
    )(where, dealt, *pieces)


def step_call(last, scale, where, states, latents, weights, noise, early, p_pieces, t_pieces):
    trunk_weight, head, policy, action_w, reward_w, spread = weights
    rows, cols = latents.shape
    width, hidden = action_w.shape[1], trunk_weight.shape[1]
    column = jax.ShapeDtypeStruct((rows, 1), F32)
    shapes = [jax.ShapeDtypeStruct((rows, width), BF16)]
    if last:
        shapes += [jax.ShapeDtypeStruct((rows, 128), F32)]
    else:
        shapes += [jax.ShapeDtypeStruct((rows, cols), BF16), column, column]
    scratch = [
        full_scratch(cols),
        full_scratch(cols),
        pltpu.VMEM((cols, hidden), BF16),
        pltpu.VMEM((rows, hidden), BF16),
        pltpu.VMEM((rows, width), F32),
        pltpu.VMEM((rows, width), BF16),
        pltpu.VMEM((rows, cols), BF16),
        pltpu.SemaphoreType.DMA((3,)),
    ]
    if last:
        scratch.append(pltpu.VMEM((rows, cols), BF16))
    small = [states, latents]
    heads = [head, policy, action_w, reward_w, spread, *noise, *early]
    specs = [SMEM_SPEC] + [VMEM_SPEC] * 2 + [ANY_SPEC] + [VMEM_SPEC] * len(heads) + [ANY_SPEC] * (2 * N_PIECES)
    return pl.pallas_call(
        functools.partial(step_kernel, last, scale),
        name="last_step" if last else "first_step",
        out_shape=shapes,
        in_specs=specs,
        out_specs=[VMEM_SPEC] * len(shapes),
        scratch_shapes=scratch,
        compiler_params=pltpu.CompilerParams(vmem_limit_bytes=LIMIT),
        cost_estimate=pl.CostEstimate(flops=2 * 128 * 1024 * 10240, bytes_accessed=24 * 2**20, transcendentals=0),
    )(where, *small, trunk_weight, *heads, *p_pieces, *t_pieces)


def slope_kernel(*refs):
    pieces, (trunk_part, head_part, turned, slopes) = refs[:16], refs[16:]
    for i, piece in enumerate(pieces):
        rows = piece.shape[0]
        at = i * rows
        latents = piece[...]
        pre = jnp.dot(latents, trunk_part[...], preferred_element_type=F32)
        sig = 1.0 / (1.0 + jnp.exp(-pre))
        slopes[at : at + rows] = head_part[...] * (sig * (1.0 + pre * (1.0 - sig)))
        turned[:, at : at + rows] = latents.T


def slope_call(kept, trunk_part, head_part):
    count = 16 * kept[0][0].shape[0]
    cols, part = trunk_part.shape
    return pl.pallas_call(
        slope_kernel,
        name="slopes",
        out_shape=[jax.ShapeDtypeStruct((cols, count), BF16), jax.ShapeDtypeStruct((count, part), F32)],
        in_specs=[VMEM_SPEC] * 18,
        out_specs=[VMEM_SPEC] * 2,
        compiler_params=pltpu.CompilerParams(vmem_limit_bytes=SMALL_LIMIT),
        cost_estimate=pl.CostEstimate(flops=2 * 2048 * 1024 * 256, bytes_accessed=12 * 2**20, transcendentals=0),
    )(*kept[0], *kept[1], trunk_part, head_part)


def share_kernel(where, pair, below, above, away, turned, slopes, *refs):
    outs, (back, total) = refs[:4], refs[4:]
    line = [part[c] for part in (pair, below, above, away) for c in range(2)]
    rows = pair.shape[1]
    for step in range(2):
        for i, column in enumerate(line):
            at = (8 * step + i) * rows
            back[at : at + rows] = (column[:, 2 + step : 3 + step] * slopes[at : at + rows]).astype(BF16)
    share = jnp.dot(turned[...], back[...], preferred_element_type=F32).astype(BF16)
    total[...] = share.reshape(total.shape)
    for out, d in zip(outs, (0, 1, -1, 2)):
        out[...] = total[:, lax.rem(where[1] + NY + d, NY)]


def share_call(where, columns, turned, slopes):
    cols, part = turned.shape[0], slopes.shape[1]
    block = jax.ShapeDtypeStruct((NZ, cols // (NZ * NY), part), BF16)
    return pl.pallas_call(
        share_kernel,
        name="gradient_share",
        out_shape=[block] * 4,
        in_specs=[SMEM_SPEC] + [VMEM_SPEC] * 6,
        out_specs=[VMEM_SPEC] * 4,
        scratch_shapes=[
            pltpu.VMEM(slopes.shape, BF16),
            pltpu.VMEM((NZ, NY, cols // (NZ * NY), part), BF16),
        ],
        compiler_params=pltpu.CompilerParams(vmem_limit_bytes=SMALL_LIMIT),
        cost_estimate=pl.CostEstimate(flops=2 * 2048 * 1024 * 256, bytes_accessed=8 * 2**20, transcendentals=0),
    )(where, *columns, turned, slopes)


def relay_x(packed):
    near = along_x(packed[0], lambda x: x ^ 1)
    away = along_x(packed[1], lambda x: x - 1 if x % 2 == 0 else x + 1)
    return near, away


def relay_rest(near, away, xh, core):
    crossed = swap_core(jnp.stack([near[1], away[1]]))
    first, second = core == 0, xh == 0

    def by_core(mine, other):
        return [jnp.where(first, mine, other), jnp.where(first, other, mine)]

    same, other = by_core(near[0], crossed[0]), by_core(away[0], crossed[1])
    low = [jnp.where(second, same[c], other[c]) for c in range(2)]
    high = [jnp.where(second, other[c], same[c]) for c in range(2)]
    both = jnp.stack(low + high, axis=1)
    return both


def deal(both):
    dealt = lax.all_to_all(both, ("z", "y"), split_axis=0, concat_axis=0, tiled=True)
    return dealt.reshape(-1, dealt.shape[-1])


def x_gather(latents):
    mine = [latents] + [along_x(latents, lambda x, d=d: x + d) for d in (1, -1, 2)]
    return [swap_core(mine[0])] + mine


def x_gather_rest(line):
    pieces = [line[1], line[0]]
    for a in line[2:]:
        pieces += [a, swap_core(a)]
    return pieces


def x_columns(column):
    pair = jnp.stack([column, swap_core(column)])
    return [pair] + [along_x(pair, lambda x, d=d: x + d) for d in (1, -1, 2)]


def local(
    replay_states,
    replay_embed,
    replay_index,
    episode_first,
    prior_weight,
    transition_weight,
    action_weight,
    trunk_weight,
    value_head,
    policy_head,
    reward_head,
    latent_scale,
    action_noise,
    latent_noise,
):
    g, z, y = lax.axis_index("grp"), lax.axis_index("z"), lax.axis_index("y")
    xh, core = lax.axis_index("xh"), lax.axis_index("core")
    width = replay_states.shape[1]
    rows = replay_index.shape[0]
    order = jnp.stack([replay_index, episode_first]).reshape(2, NZ * NY, NX, NC)
    order = jnp.transpose(order, (2, 3, 0, 1))
    order = jnp.where(xh == 0, order, order[::-1])
    order = jnp.where(core == 0, order, order[:, ::-1])
    order = jnp.swapaxes(order, 1, 2).swapaxes(0, 1).reshape(2, rows)

    def packed_of(order):
        keep = (1 - order[1]).astype(BF16)[:, None]
        return jnp.concatenate(
            [jnp.take(replay_states, order[0], axis=0) * keep, jnp.take(replay_embed, order[0], axis=0)],
            axis=1,
        ).reshape(NX, NC, NZ * NY, -1)

    dealt, flat = gather_weights(prior_weight, transition_weight, g, core, xh, order, packed_of)
    p_pieces, t_pieces = pieces_of(flat, 0), pieces_of(flat, 1)
    where = jnp.stack([z, y, xh, core, g]).astype(jnp.int32)
    steps = action_noise.shape[0]
    hidden_units = trunk_weight.shape[1]
    cols = prior_weight.shape[1]
    part = hidden_units // 8
    slot = (g * 2 + xh) * 2 + core
    trunk_part = lax.dynamic_slice(trunk_weight, (0, slot * part), (trunk_weight.shape[0], part))
    head_part = lax.dynamic_slice(value_head, (slot * part,), (part,)).astype(F32)
    count = lax.axis_size("grp") * NZ * NY * NX * NC
    grad_scale = 4.0 * (float(hidden_units) / float(count * rows * steps)) ** 0.5
    weights = (
        trunk_weight,
        value_head[None],
        policy_head.T,
        action_weight,
        reward_head[None],
        latent_scale[None],
    )

    latents = first_call(where, dealt, p_pieces, cols)
    latents, trunk_part, head_part = lax.optimization_barrier((latents, trunk_part, head_part))
    kept = [x_gather(latents)]
    states, latents, value_0, reward_0 = step_call(
        False, grad_scale, where, dealt, latents, weights, (action_noise[0], latent_noise[0]), (), p_pieces, t_pieces
    )
    latents, kept[0] = lax.optimization_barrier((latents, kept[0]))
    kept.append(x_gather(latents))
    states, outs = step_call(
        True, grad_scale, where, states, latents, weights, (action_noise[1], latent_noise[1]), (value_0, reward_0), p_pieces, t_pieces
    )
    outs, kept[1] = lax.optimization_barrier((outs, kept[1]))
    columns = x_columns(outs)
    kept = [x_gather_rest(line) for line in kept]
    turned, slopes = slope_call(kept, trunk_part, head_part[None])
    keep, *others = share_call(where, columns, turned, slopes)
    targets = outs[:, :2].T
    met = keep.astype(F32)
    for block, d in zip(others, (1, -1, 2)):
        met = met + lax.ppermute(block, "y", shift(NY, d)).astype(F32)
    sent = met.astype(BF16).reshape(1, NZ, NX * NC, -1, part)
    sent = jnp.concatenate([sent, sent], axis=0).reshape(2 * NZ * NX * NC, -1, part)
    parts = lax.all_to_all(sent, ("grp", "z", "xh", "core"), split_axis=0, concat_axis=0, tiled=True)
    parts = jnp.sum(parts.astype(F32).reshape(2, NZ, NX * NC, -1, part), axis=1)
    trunk_grad = jnp.transpose(parts, (2, 0, 1, 3)).reshape(-1, hidden_units)
    return (states, targets, trunk_grad)


def solution(mesh):
    fine = Mesh(mesh.devices.reshape(2, NZ, NY, NX, NC), AXES)
    return jax.shard_map(
        local,
        mesh=fine,
        in_specs=(
            P(AXES, None),
            P(AXES, None),
            P(AXES),
            P(AXES),
            P(FSDP, None),
            P(FSDP, None),
            P(),
            P(),
            P(),
            P(),
            P(),
            P(),
            P(None, AXES, None),
            P(None, AXES, None),
        ),
        out_specs=(P(AXES, None), P(None, AXES), P(FSDP, None)),
        check_vma=False,
    )
```

```python
import functools

import jax
import jax.numpy as jnp
from jax import lax
from jax.experimental import pallas as pl
from jax.experimental.pallas import tpu as pltpu
from jax.sharding import Mesh, PartitionSpec as P

GAMMA = 0.985
LAMBDA = 0.95
EPS = 1e-06
F32 = jnp.float32
BF16 = jnp.bfloat16

NZ, NY, NX, NC = 8, 4, 2, 2
AXES = ("grp", "z", "y", "xh", "core")
FSDP = ("z", "y", "xh", "core")


def shift(n, d):
    return [(i, (i + d) % n) for i in range(n)]


def x_line(move):
    pairs = []
    for g in range(2):
        for h in range(2):
            to = move(2 * h + g) % 4
            pairs.append((2 * g + h, 2 * (to % 2) + to // 2))
    return pairs


def along_x(a, move):
    return lax.ppermute(a, ("grp", "xh"), x_line(move))


def swap_core(a):
    return lax.ppermute(a, "core", shift(2, 1))


def split_ring(axis, n):
    return [(2 * i + c, 2 * ((i + 1 - 2 * c) % n) + c) for i in range(n) for c in range(2)]


def gather_weights(prior, transition, g, core, xh, order, packed_of):
    depth = transition.shape[0]
    cols = prior.shape[1]
    blocks = transition.shape[1] // cols
    other_p, other_t = swap_core(prior), swap_core(transition)

    def both(mine, other):
        return jnp.where(core == 0, jnp.concatenate([mine, other]), jnp.concatenate([other, mine]))

    chip_t = both(transition, other_t).reshape(2 * depth, blocks, cols)
    unit = jnp.stack([both(prior, other_p), jnp.swapaxes(chip_t, 0, 1).reshape(-1, cols)])
    unit, order = lax.optimization_barrier((unit, order))
    ring = [unit]
    for hop in range(4):
        pairs = split_ring("z", NZ)
        if hop == 3:
            pairs = [p for p in pairs if p[0] % 2]
        ring.append(lax.ppermute(ring[-1], ("z", "core"), pairs))
        if hop == 0:
            packed = packed_of(order)
            ring[-1], packed = lax.optimization_barrier((ring[-1], packed))
            near, away = relay_x(packed)
    ring[4], near, away = lax.optimization_barrier((ring[4], near, away))
    both = relay_rest(near, away, xh, core)
    own = jnp.where(core == 0, jnp.stack(ring[3::-1], axis=1), jnp.stack(ring[1:], axis=1))
    chosen = g == core

    def pair_hop(a):
        return along_x(a, lambda x: x + 1 if x % 2 else x - 1)

    def partner_hop(a):
        return along_x(a, lambda x: x ^ 1)

    def y_hop(a):
        return lax.ppermute(a, ("y", "core"), split_ring("y", NY))

    def half(a):
        return lax.dynamic_index_in_dim(a, g, 0, keepdims=False)

    near_1 = pair_hop(half(own))
    own_s = swap_core(own)
    mine = [jnp.stack([own[w], own_s[w]]) for w in range(2)]
    side_p = y_hop(mine[0])
    near_1s = swap_core(near_1)
    mine_t, side_p, near_1, near_1s = lax.optimization_barrier((mine[1], side_p, near_1, near_1s))
    dealt = deal(both)
    beside_p = jnp.where(chosen, side_p[0], side_p[1])
    side_t, beside_p1, near_2 = y_hop(mine_t), pair_hop(beside_p), partner_hop(near_1)
    side_ps = swap_core(side_p)
    beside_p1, near_2, side_ps = lax.optimization_barrier((beside_p1, near_2, side_ps))
    beside_p2 = partner_hop(beside_p1)
    near_2s, beside_p1s = swap_core(near_2), swap_core(beside_p1)
    side_t, near_2s, beside_p1s, beside_p2, dealt = lax.optimization_barrier(
        (side_t, near_2s, beside_p1s, beside_p2, dealt)
    )
    beside_t1 = pair_hop(jnp.where(chosen, side_t[0], side_t[1]))
    far = y_hop(jnp.stack([side_p[0], side_t[0]]))
    side_ts = swap_core(side_t)
    far, beside_t1, side_ts = lax.optimization_barrier((far, beside_t1, side_ts))
    away_1, beside_t2 = pair_hop(half(far)), partner_hop(beside_t1)
    far_s, beside_p2s, beside_t1s = swap_core(far), swap_core(beside_p2), swap_core(beside_t1)
    away_1, beside_t2, far_s, beside_p2s, beside_t1s = lax.optimization_barrier(
        (away_1, beside_t2, far_s, beside_p2s, beside_t1s)
    )
    away_2 = partner_hop(away_1)
    beside_t2s, away_1s = swap_core(beside_t2), swap_core(away_1)
    away_2, beside_t2s, away_1s = lax.optimization_barrier((away_2, beside_t2s, away_1s))
    flat = [own, own_s, far, far_s, side_p, side_ps, side_t, side_ts]
    flat += [near_1, near_1s, near_2, near_2s]
    flat += [beside_p1, beside_p1s, beside_p2, beside_p2s]
    flat += [beside_t1, beside_t1s, beside_t2, beside_t2s]
    flat += [away_1, away_1s, away_2, swap_core(away_2)]
    return dealt, flat


def pieces_of(flat, w):
    across = [flat[8 + 4 * k : 12 + 4 * k] for k in (0, 1 + w, 3)]
    return flat[:4] + flat[4 + 2 * w : 6 + 2 * w] + across[0] + across[1] + across[2]


N_PIECES = 18


def place_all(w, where, pieces, full, sem):
    y, xh, core, g = (where[i] for i in range(1, 5))
    own, own_s, far, far_s, side, side_s = pieces[:6]
    turn = jnp.where(core == 0, -1, 1)

    def copy(src, group, dy, h):
        dst = full.at[pl.ds(4 * group, 4), lax.rem(y + NY + dy, NY), h]
        pltpu.make_async_copy(src, dst, sem).start()

    copy(own.at[w], core, 0, xh)
    copy(own_s.at[w], 1 - core, 0, xh)
    for r in range(2):
        copy(side.at[r], jnp.bitwise_xor(core, r), turn, xh)
        copy(side_s.at[r], jnp.bitwise_xor(1 - core, r), -turn, xh)
    copy(far.at[w], core, 2, xh)
    copy(far_s.at[w], 1 - core, 2, xh)
    near, beside, away = (pieces[6 + 4 * k : 10 + 4 * k] for k in range(3))
    for way, group in ((0, 1 - g), (2, g)):
        copy(beside[way], group, turn, 1 - xh)
        copy(beside[way + 1], group, -turn, 1 - xh)

        @pl.when(group == w)
        def _():
            copy(near[way], core, 0, 1 - xh)
            copy(near[way + 1], 1 - core, 0, 1 - xh)
            copy(away[way], core, 2, 1 - xh)
            copy(away[way + 1], 1 - core, 2, 1 - xh)


def turn_columns(where, src, dst):
    size = dst.shape[1] // NZ
    for i in range(NZ):
        at = lax.rem(where[0] + NZ - 3 + i, NZ) * size
        dst[:, i * size : (i + 1) * size] = src[:, pl.ds(pl.multiple_of(at, size), size)]


def wait_all(full, sem):
    pltpu.make_async_copy(full, full, sem).wait()


def silu(v):
    return v / (1.0 + jnp.exp(-v))


TILE = 512


def prior_dot(h, full, n):
    cols = pl.ds(pl.multiple_of(n * TILE, TILE), TILE)
    return jnp.dot(h, full[:, :, :, :, cols].reshape(h.shape[1], TILE), preferred_element_type=F32), cols


def first_kernel(where, dealt, *refs):
    pieces, (latents, full, turned, sem) = refs[:N_PIECES], refs[N_PIECES:]
    place_all(0, where, pieces, full, sem)
    width = dealt.shape[1] - latents.shape[1]
    turn_columns(where, dealt, turned)
    wait_all(full, sem)

    @pl.loop(0, latents.shape[1] // TILE)
    def _(n):
        acc, cols = prior_dot(turned[...], full, n)
        embed = dealt[:, pl.ds(pl.multiple_of(width + n * TILE, TILE), TILE)]
        latents[:, cols] = (acc + embed.astype(F32)).astype(BF16)


def step_kernel(last, scale, where, states_in, latents_in, trunk_hbm, head, policy, action_w, reward_w, spread, act_noise, noise_hbm, *refs):
    refs = list(refs)
    if last:
        value_0, reward_0 = refs[:2]
        refs = refs[2:]
    p_pieces, t_pieces, refs = refs[:N_PIECES], refs[N_PIECES : 2 * N_PIECES], refs[2 * N_PIECES :]
    if last:
        states_out, outs, refs = refs[0], refs[1], refs[2:]
    else:
        states_out, latents_out, value_out, reward_out = refs[:4]
        refs = refs[4:]
    p_full, t_full, trunk_w, trunk, mixed, turned_h, turned_z, lat_noise, sems = refs[:9]
    if last:
        latents_out = refs[9]
    trunk_copy = pltpu.make_async_copy(trunk_hbm, trunk_w, sems.at[0])
    trunk_copy.start()
    place_all(1, where, t_pieces, t_full, sems.at[1])
    noise_copy = pltpu.make_async_copy(noise_hbm.at[int(last)], lat_noise, sems.at[3])
    noise_copy.start()
    place_all(0, where, p_pieces, p_full, sems.at[2])
    turn_columns(where, latents_in, turned_z)
    trunk_copy.wait()
    rows, width = mixed.shape
    hidden = trunk_w.shape[1]

    def critic(z_ref):
        def tile(n, value):
            cols = pl.ds(pl.multiple_of(n * TILE, TILE), TILE)
            pre = jnp.dot(z_ref[...], trunk_w[:, cols], preferred_element_type=F32)
            out = silu(pre).astype(BF16)
            trunk[:, cols] = out
            part = out.astype(F32) * head[:, cols].astype(F32)
            return value + jnp.sum(part, axis=1, keepdims=True)

        return lax.fori_loop(0, hidden // TILE, tile, jnp.zeros((rows, 1), F32))

    value = critic(latents_in)
    action = jnp.tanh(
        lax.dot_general(trunk[...], policy[...], (((1,), (1,)), ((), ())), preferred_element_type=F32)
        + act_noise[...].astype(F32)
    ).astype(BF16)
    wait_all(t_full, sems.at[1])
    blocks = t_full.shape[3] // 16
    block = width // blocks
    square = jnp.zeros((rows, 1), F32)
    for q in range(blocks):

        def tile(n, square):
            cols = pl.ds(pl.multiple_of(n * TILE, TILE), TILE)
            at = pl.ds(pl.multiple_of(q * block + n * TILE, TILE), TILE)
            weight = t_full[:, :, :, q * 16 : (q + 1) * 16, cols].reshape(latents_in.shape[1], TILE)
            drive = jnp.dot(turned_z[...], weight, preferred_element_type=F32) + jnp.dot(
                action, action_w[:, at], preferred_element_type=F32
            )
            m = states_in[:, at].astype(F32) + silu(drive)
            mixed[:, at] = m
            return square + jnp.sum(m * m, axis=1, keepdims=True)

        square = lax.fori_loop(0, block // TILE, tile, square)
    norm = lax.rsqrt(square * (1.0 / width) + EPS)

    def normed(n, reward):
        at = pl.ds(pl.multiple_of(n * TILE, TILE), TILE)
        out = (mixed[:, at] * norm).astype(BF16)
        states_out[:, at] = out
        return reward + jnp.sum(out.astype(F32) * reward_w[:, at].astype(F32), axis=1, keepdims=True)

    reward = lax.fori_loop(0, width // TILE, normed, jnp.zeros((rows, 1), F32))
    turn_columns(where, states_out, turned_h)
    noise_copy.wait()
    wait_all(p_full, sems.at[2])

    @pl.loop(0, latents_out.shape[1] // TILE)
    def _(n):
        acc, cols = prior_dot(turned_h[...], p_full, n)
        latents_out[:, cols] = (acc + spread[:, cols] * lat_noise[:, cols].astype(F32)).astype(BF16)

    if not last:
        value_out[...] = value
        reward_out[...] = reward
        return
    last_value = critic(latents_out)
    second = reward + GAMMA * ((1.0 - LAMBDA) * last_value + LAMBDA * last_value)
    first = reward_0[...] + GAMMA * ((1.0 - LAMBDA) * value + LAMBDA * second)
    place = lax.broadcasted_iota(jnp.int32, (rows, 128), 1)
    out = jnp.where(place == 0, first, jnp.where(place == 1, second, 0.0))
    out = jnp.where(place == 2, (value_0[...] - first) * scale, out)
    out = jnp.where(place == 3, (value - second) * scale, out)
    outs[...] = out


VMEM_SPEC = pl.BlockSpec(memory_space=pltpu.VMEM)
ANY_SPEC = pl.BlockSpec(memory_space=pl.ANY)
SMEM_SPEC = pl.BlockSpec(memory_space=pltpu.SMEM)
LIMIT = 50 * 2**20
SMALL_LIMIT = 24 * 2**20


def full_scratch(cols):
    return pltpu.VMEM((NZ, NY, NX, 64, cols), BF16)


def first_call(where, dealt, pieces, cols):
    return pl.pallas_call(
        first_kernel,
        name="first_latents",
        out_shape=jax.ShapeDtypeStruct((dealt.shape[0], cols), BF16),
        in_specs=[SMEM_SPEC, VMEM_SPEC] + [ANY_SPEC] * len(pieces),
        out_specs=VMEM_SPEC,
        scratch_shapes=[
            full_scratch(cols),
            pltpu.VMEM((dealt.shape[0], dealt.shape[1] - cols), BF16),
            pltpu.SemaphoreType.DMA,
        ],
        compiler_params=pltpu.CompilerParams(vmem_limit_bytes=LIMIT),
        cost_estimate=pl.CostEstimate(flops=2 * 128 * 4096 * 1024, bytes_accessed=10 * 2**20, transcendentals=0),
    )(where, dealt, *pieces)


def step_call(last, scale, where, states, latents, weights, noise, early, p_pieces, t_pieces):
    trunk_weight, head, policy, action_w, reward_w, spread = weights
    rows, cols = latents.shape
    width, hidden = action_w.shape[1], trunk_weight.shape[1]
    column = jax.ShapeDtypeStruct((rows, 1), F32)
    shapes = [jax.ShapeDtypeStruct((rows, width), BF16)]
    if last:
        shapes += [jax.ShapeDtypeStruct((rows, 128), F32)]
    else:
        shapes += [jax.ShapeDtypeStruct((rows, cols), BF16), column, column]
    scratch = [
        full_scratch(cols),
        full_scratch(cols),
        pltpu.VMEM((cols, hidden), BF16),
        pltpu.VMEM((rows, hidden), BF16),
        pltpu.VMEM((rows, width), F32),
        pltpu.VMEM((rows, width), BF16),
        pltpu.VMEM((rows, cols), BF16),
        pltpu.VMEM((rows, cols), BF16),
        pltpu.SemaphoreType.DMA((4,)),
    ]
    if last:
        scratch.append(pltpu.VMEM((rows, cols), BF16))
    small = [states, latents]
    heads = [head, policy, action_w, reward_w, spread, *noise, *early]
    specs = [SMEM_SPEC] + [VMEM_SPEC] * 2 + [ANY_SPEC] + [VMEM_SPEC] * 6 + [ANY_SPEC] + [VMEM_SPEC] * len(early)
    specs += [ANY_SPEC] * (2 * N_PIECES)
    return pl.pallas_call(
        functools.partial(step_kernel, last, scale),
        name="last_step" if last else "first_step",
        out_shape=shapes,
        in_specs=specs,
        out_specs=[VMEM_SPEC] * len(shapes),
        scratch_shapes=scratch,
        compiler_params=pltpu.CompilerParams(vmem_limit_bytes=LIMIT),
        cost_estimate=pl.CostEstimate(flops=2 * 128 * 1024 * 10240, bytes_accessed=24 * 2**20, transcendentals=0),
    )(where, *small, trunk_weight, *heads, *p_pieces, *t_pieces)


def slope_kernel(*refs):
    pieces, (trunk_part, head_part, turned, slopes) = refs[:16], refs[16:]
    for i, piece in enumerate(pieces):
        rows = piece.shape[0]
        at = i * rows
        latents = piece[...]
        pre = jnp.dot(latents, trunk_part[...], preferred_element_type=F32)
        sig = 1.0 / (1.0 + jnp.exp(-pre))
        slopes[at : at + rows] = head_part[...] * (sig * (1.0 + pre * (1.0 - sig)))
        turned[:, at : at + rows] = latents.T


def slope_call(kept, trunk_part, head_part):
    count = 16 * kept[0][0].shape[0]
    cols, part = trunk_part.shape
    return pl.pallas_call(
        slope_kernel,
        name="slopes",
        out_shape=[jax.ShapeDtypeStruct((cols, count), BF16), jax.ShapeDtypeStruct((count, part), F32)],
        in_specs=[VMEM_SPEC] * 18,
        out_specs=[VMEM_SPEC] * 2,
        compiler_params=pltpu.CompilerParams(vmem_limit_bytes=SMALL_LIMIT),
        cost_estimate=pl.CostEstimate(flops=2 * 2048 * 1024 * 256, bytes_accessed=12 * 2**20, transcendentals=0),
    )(*kept[0], *kept[1], trunk_part, head_part)


def share_kernel(where, pair, below, above, away, turned, slopes, *refs):
    outs, (back, total) = refs[:4], refs[4:]
    line = [part[c] for part in (pair, below, above, away) for c in range(2)]
    rows = pair.shape[1]
    for step in range(2):
        for i, column in enumerate(line):
            at = (8 * step + i) * rows
            back[at : at + rows] = (column[:, 2 + step : 3 + step] * slopes[at : at + rows]).astype(BF16)
    share = jnp.dot(turned[...], back[...], preferred_element_type=F32).astype(BF16)
    total[...] = share.reshape(total.shape)
    for out, d in zip(outs, (0, 1, -1, 2)):
        out[...] = total[:, lax.rem(where[1] + NY + d, NY)]


def share_call(where, columns, turned, slopes):
    cols, part = turned.shape[0], slopes.shape[1]
    block = jax.ShapeDtypeStruct((NZ, cols // (NZ * NY), part), BF16)
    return pl.pallas_call(
        share_kernel,
        name="gradient_share",
        out_shape=[block] * 4,
        in_specs=[SMEM_SPEC] + [VMEM_SPEC] * 6,
        out_specs=[VMEM_SPEC] * 4,
        scratch_shapes=[
            pltpu.VMEM(slopes.shape, BF16),
            pltpu.VMEM((NZ, NY, cols // (NZ * NY), part), BF16),
        ],
        compiler_params=pltpu.CompilerParams(vmem_limit_bytes=SMALL_LIMIT),
        cost_estimate=pl.CostEstimate(flops=2 * 2048 * 1024 * 256, bytes_accessed=8 * 2**20, transcendentals=0),
    )(where, *columns, turned, slopes)


def relay_x(packed):
    near = along_x(packed[0], lambda x: x ^ 1)
    away = along_x(packed[1], lambda x: x - 1 if x % 2 == 0 else x + 1)
    return near, away


def relay_rest(near, away, xh, core):
    crossed = swap_core(jnp.stack([near[1], away[1]]))
    first, second = core == 0, xh == 0

    def by_core(mine, other):
        return [jnp.where(first, mine, other), jnp.where(first, other, mine)]

    same, other = by_core(near[0], crossed[0]), by_core(away[0], crossed[1])
    low = [jnp.where(second, same[c], other[c]) for c in range(2)]
    high = [jnp.where(second, other[c], same[c]) for c in range(2)]
    both = jnp.stack(low + high, axis=1)
    return both


def deal(both):
    dealt = lax.all_to_all(both, ("z", "y"), split_axis=0, concat_axis=0, tiled=True)
    return dealt.reshape(-1, dealt.shape[-1])


def x_gather(latents):
    mine = [latents] + [along_x(latents, lambda x, d=d: x + d) for d in (1, -1, 2)]
    return [swap_core(mine[0])] + mine


def x_gather_rest(line):
    pieces = [line[1], line[0]]
    for a in line[2:]:
        pieces += [a, swap_core(a)]
    return pieces


def x_columns(column):
    pair = jnp.stack([column, swap_core(column)])
    return [pair] + [along_x(pair, lambda x, d=d: x + d) for d in (1, -1, 2)]


def local(
    replay_states,
    replay_embed,
    replay_index,
    episode_first,
    prior_weight,
    transition_weight,
    action_weight,
    trunk_weight,
    value_head,
    policy_head,
    reward_head,
    latent_scale,
    action_noise,
    latent_noise,
):
    g, z, y = lax.axis_index("grp"), lax.axis_index("z"), lax.axis_index("y")
    xh, core = lax.axis_index("xh"), lax.axis_index("core")
    width = replay_states.shape[1]
    rows = replay_index.shape[0]
    order = jnp.stack([replay_index, episode_first]).reshape(2, NZ * NY, NX, NC)
    order = jnp.transpose(order, (2, 3, 0, 1))
    order = jnp.where(xh == 0, order, order[::-1])
    order = jnp.where(core == 0, order, order[:, ::-1])
    order = jnp.swapaxes(order, 1, 2).swapaxes(0, 1).reshape(2, rows)

    def packed_of(order):
        keep = (1 - order[1]).astype(BF16)[:, None]
        return jnp.concatenate(
            [jnp.take(replay_states, order[0], axis=0) * keep, jnp.take(replay_embed, order[0], axis=0)],
            axis=1,
        ).reshape(NX, NC, NZ * NY, -1)

    dealt, flat = gather_weights(prior_weight, transition_weight, g, core, xh, order, packed_of)
    p_pieces, t_pieces = pieces_of(flat, 0), pieces_of(flat, 1)
    where = jnp.stack([z, y, xh, core, g]).astype(jnp.int32)
    steps = action_noise.shape[0]
    hidden_units = trunk_weight.shape[1]
    cols = prior_weight.shape[1]
    part = hidden_units // 8
    slot = (g * 2 + xh) * 2 + core
    trunk_part = lax.dynamic_slice(trunk_weight, (0, slot * part), (trunk_weight.shape[0], part))
    head_part = lax.dynamic_slice(value_head, (slot * part,), (part,)).astype(F32)
    count = lax.axis_size("grp") * NZ * NY * NX * NC
    grad_scale = 4.0 * (float(hidden_units) / float(count * rows * steps)) ** 0.5
    weights = (
        trunk_weight,
        value_head[None],
        policy_head.T,
        action_weight,
        reward_head[None],
        latent_scale[None],
    )

    latents = first_call(where, dealt, p_pieces, cols)
    latents, trunk_part, head_part = lax.optimization_barrier((latents, trunk_part, head_part))
    kept = [x_gather(latents)]
    states, latents, value_0, reward_0 = step_call(
        False, grad_scale, where, dealt, latents, weights, (action_noise[0], latent_noise), (), p_pieces, t_pieces
    )
    latents, kept[0] = lax.optimization_barrier((latents, kept[0]))
    kept.append(x_gather(latents))
    states, outs = step_call(
        True, grad_scale, where, states, latents, weights, (action_noise[1], latent_noise), (value_0, reward_0), p_pieces, t_pieces
    )
    outs, kept[1] = lax.optimization_barrier((outs, kept[1]))
    columns = x_columns(outs)
    kept = [x_gather_rest(line) for line in kept]
    turned, slopes = slope_call(kept, trunk_part, head_part[None])
    keep, *others = share_call(where, columns, turned, slopes)
    targets = outs[:, :2].T
    met = keep.astype(F32)
    for block, d in zip(others, (1, -1, 2)):
        met = met + lax.ppermute(block, "y", shift(NY, d)).astype(F32)
    met = lax.all_to_all(met.astype(BF16), "z", split_axis=0, concat_axis=0, tiled=True)
    met = jnp.sum(met.astype(F32), axis=0).reshape(NX * NC, -1, part)
    sent = jnp.concatenate([met, met], axis=0)
    parts = lax.all_to_all(sent, ("grp", "xh", "core"), split_axis=0, concat_axis=0, tiled=True)
    trunk_grad = jnp.swapaxes(parts, 0, 1).reshape(-1, hidden_units)
    return (states, targets, trunk_grad)


def solution(mesh):
    fine = Mesh(mesh.devices.reshape(2, NZ, NY, NX, NC), AXES)
    return jax.shard_map(
        local,
        mesh=fine,
        in_specs=(
            P(AXES, None),
            P(AXES, None),
            P(AXES),
            P(AXES),
            P(FSDP, None),
            P(FSDP, None),
            P(),
            P(),
            P(),
            P(),
            P(),
            P(),
            P(None, AXES, None),
            P(None, AXES, None),
        ),
        out_specs=(P(AXES, None), P(None, AXES), P(FSDP, None)),
        check_vma=False,
    )
```

```python
import functools

import jax
import jax.numpy as jnp
from jax import lax
from jax.experimental import pallas as pl
from jax.experimental.pallas import tpu as pltpu
from jax.sharding import Mesh, PartitionSpec as P

GAMMA = 0.985
LAMBDA = 0.95
EPS = 1e-06
F32 = jnp.float32
BF16 = jnp.bfloat16

NZ, NY, NX, NC = 8, 4, 2, 2
AXES = ("grp", "z", "y", "xh", "core")
FSDP = ("z", "y", "xh", "core")


def shift(n, d):
    return [(i, (i + d) % n) for i in range(n)]


def x_line(move):
    pairs = []
    for g in range(2):
        for h in range(2):
            to = move(2 * h + g) % 4
            pairs.append((2 * g + h, 2 * (to % 2) + to // 2))
    return pairs


def along_x(a, move):
    return lax.ppermute(a, ("grp", "xh"), x_line(move))


def swap_core(a):
    return lax.ppermute(a, "core", shift(2, 1))


def split_ring(axis, n):
    return [(2 * i + c, 2 * ((i + 1 - 2 * c) % n) + c) for i in range(n) for c in range(2)]


def gather_weights(prior, transition, g, core, xh, order, packed_of):
    depth = transition.shape[0]
    cols = prior.shape[1]
    blocks = transition.shape[1] // cols
    other_p, other_t = swap_core(prior), swap_core(transition)

    def both(mine, other):
        return jnp.where(core == 0, jnp.concatenate([mine, other]), jnp.concatenate([other, mine]))

    chip_t = both(transition, other_t).reshape(2 * depth, blocks, cols)
    unit = jnp.stack([both(prior, other_p), jnp.swapaxes(chip_t, 0, 1).reshape(-1, cols)])
    unit, order = lax.optimization_barrier((unit, order))
    ring = [unit]
    for hop in range(4):
        pairs = split_ring("z", NZ)
        if hop == 3:
            pairs = [p for p in pairs if p[0] % 2]
        ring.append(lax.ppermute(ring[-1], ("z", "core"), pairs))
        if hop == 0:
            packed = packed_of(order)
            ring[-1], packed = lax.optimization_barrier((ring[-1], packed))
            near, away = relay_x(packed)
    ring[4], near, away = lax.optimization_barrier((ring[4], near, away))
    both = relay_rest(near, away, xh, core)
    own = jnp.where(core == 0, jnp.stack(ring[3::-1], axis=1), jnp.stack(ring[1:], axis=1))
    chosen = g == core

    def pair_hop(a):
        return along_x(a, lambda x: x + 1 if x % 2 else x - 1)

    def partner_hop(a):
        return along_x(a, lambda x: x ^ 1)

    def y_hop(a):
        return lax.ppermute(a, ("y", "core"), split_ring("y", NY))

    def half(a):
        return lax.dynamic_index_in_dim(a, g, 0, keepdims=False)

    near_1 = pair_hop(half(own))
    own_s = swap_core(own)
    mine = [jnp.stack([own[w], own_s[w]]) for w in range(2)]
    side_p = y_hop(mine[0])
    near_1s = swap_core(near_1)
    mine_t, side_p, near_1, near_1s = lax.optimization_barrier((mine[1], side_p, near_1, near_1s))
    dealt = deal(both)
    beside_p = jnp.where(chosen, side_p[0], side_p[1])
    side_t, beside_p1, near_2 = y_hop(mine_t), pair_hop(beside_p), partner_hop(near_1)
    side_ps = swap_core(side_p)
    beside_p1, near_2, side_ps = lax.optimization_barrier((beside_p1, near_2, side_ps))
    beside_p2 = partner_hop(beside_p1)
    near_2s, beside_p1s = swap_core(near_2), swap_core(beside_p1)
    side_t, near_2s, beside_p1s, dealt = lax.optimization_barrier((side_t, near_2s, beside_p1s, dealt))
    beside_t1 = pair_hop(jnp.where(chosen, side_t[0], side_t[1]))
    far = y_hop(jnp.stack([side_p[0], side_t[0]]))
    side_ts = swap_core(side_t)
    far, beside_t1, beside_p2, side_ts = lax.optimization_barrier((far, beside_t1, beside_p2, side_ts))
    dealt = dealt.reshape(-1, dealt.shape[-1])
    away_1, beside_t2 = pair_hop(half(far)), partner_hop(beside_t1)
    far_s, beside_p2s, beside_t1s = swap_core(far), swap_core(beside_p2), swap_core(beside_t1)
    away_1, beside_t2, far_s, beside_p2s, beside_t1s = lax.optimization_barrier(
        (away_1, beside_t2, far_s, beside_p2s, beside_t1s)
    )
    away_2 = partner_hop(away_1)
    beside_t2s, away_1s = swap_core(beside_t2), swap_core(away_1)
    away_2, beside_t2s, away_1s = lax.optimization_barrier((away_2, beside_t2s, away_1s))
    flat = [own, own_s, far, far_s, side_p, side_ps, side_t, side_ts]
    flat += [near_1, near_1s, near_2, near_2s]
    flat += [beside_p1, beside_p1s, beside_p2, beside_p2s]
    flat += [beside_t1, beside_t1s, beside_t2, beside_t2s]
    flat += [away_1, away_1s, away_2, swap_core(away_2)]
    return dealt, flat


def pieces_of(flat, w):
    across = [flat[8 + 4 * k : 12 + 4 * k] for k in (0, 1 + w, 3)]
    return flat[:4] + flat[4 + 2 * w : 6 + 2 * w] + across[0] + across[1] + across[2]


N_PIECES = 18


def place_all(w, where, pieces, full, sem):
    y, xh, core, g = (where[i] for i in range(1, 5))
    own, own_s, far, far_s, side, side_s = pieces[:6]
    turn = jnp.where(core == 0, -1, 1)

    def copy(src, group, dy, h):
        dst = full.at[pl.ds(4 * group, 4), lax.rem(y + NY + dy, NY), h]
        pltpu.make_async_copy(src, dst, sem).start()

    copy(own.at[w], core, 0, xh)
    copy(own_s.at[w], 1 - core, 0, xh)
    for r in range(2):
        copy(side.at[r], jnp.bitwise_xor(core, r), turn, xh)
        copy(side_s.at[r], jnp.bitwise_xor(1 - core, r), -turn, xh)
    copy(far.at[w], core, 2, xh)
    copy(far_s.at[w], 1 - core, 2, xh)
    near, beside, away = (pieces[6 + 4 * k : 10 + 4 * k] for k in range(3))
    for way, group in ((0, 1 - g), (2, g)):
        copy(beside[way], group, turn, 1 - xh)
        copy(beside[way + 1], group, -turn, 1 - xh)

        @pl.when(group == w)
        def _():
            copy(near[way], core, 0, 1 - xh)
            copy(near[way + 1], 1 - core, 0, 1 - xh)
            copy(away[way], core, 2, 1 - xh)
            copy(away[way + 1], 1 - core, 2, 1 - xh)


def turn_columns(where, src, dst):
    size = dst.shape[1] // NZ
    for i in range(NZ):
        at = lax.rem(where[0] + NZ - 3 + i, NZ) * size
        dst[:, i * size : (i + 1) * size] = src[:, pl.ds(pl.multiple_of(at, size), size)]


def wait_all(full, sem):
    pltpu.make_async_copy(full, full, sem).wait()


def silu(v):
    return v / (1.0 + jnp.exp(-v))


TILE = 512


def prior_dot(h, full, n):
    cols = pl.ds(pl.multiple_of(n * TILE, TILE), TILE)
    return jnp.dot(h, full[:, :, :, :, cols].reshape(h.shape[1], TILE), preferred_element_type=F32), cols


def first_kernel(where, dealt, *refs):
    pieces, (latents, full, turned, sem) = refs[:N_PIECES], refs[N_PIECES:]
    place_all(0, where, pieces, full, sem)
    width = dealt.shape[1] - latents.shape[1]
    turn_columns(where, dealt, turned)
    wait_all(full, sem)

    @pl.loop(0, latents.shape[1] // TILE)
    def _(n):
        acc, cols = prior_dot(turned[...], full, n)
        embed = dealt[:, pl.ds(pl.multiple_of(width + n * TILE, TILE), TILE)]
        latents[:, cols] = (acc + embed.astype(F32)).astype(BF16)


def step_kernel(last, scale, where, states_in, latents_in, trunk_hbm, head, policy, action_w, reward_w, spread, act_noise, noise_hbm, *refs):
    refs = list(refs)
    if last:
        value_0, reward_0 = refs[:2]
        refs = refs[2:]
    p_pieces, t_pieces, refs = refs[:N_PIECES], refs[N_PIECES : 2 * N_PIECES], refs[2 * N_PIECES :]
    if last:
        states_out, outs, refs = refs[0], refs[1], refs[2:]
    else:
        states_out, latents_out, value_out, reward_out = refs[:4]
        refs = refs[4:]
    p_full, t_full, trunk_w, trunk, mixed, turned_h, turned_z, lat_noise, sems = refs[:9]
    if last:
        latents_out = refs[9]
    trunk_copy = pltpu.make_async_copy(trunk_hbm, trunk_w, sems.at[0])
    trunk_copy.start()
    place_all(1, where, t_pieces, t_full, sems.at[1])
    noise_copy = pltpu.make_async_copy(noise_hbm.at[int(last)], lat_noise, sems.at[3])
    noise_copy.start()
    place_all(0, where, p_pieces, p_full, sems.at[2])
    turn_columns(where, latents_in, turned_z)
    trunk_copy.wait()
    rows, width = mixed.shape
    hidden = trunk_w.shape[1]

    def critic(z_ref):
        def tile(n, value):
            cols = pl.ds(pl.multiple_of(n * TILE, TILE), TILE)
            pre = jnp.dot(z_ref[...], trunk_w[:, cols], preferred_element_type=F32)
            out = silu(pre).astype(BF16)
            trunk[:, cols] = out
            part = out.astype(F32) * head[:, cols].astype(F32)
            return value + jnp.sum(part, axis=1, keepdims=True)

        return lax.fori_loop(0, hidden // TILE, tile, jnp.zeros((rows, 1), F32))

    value = critic(latents_in)
    action = jnp.tanh(
        lax.dot_general(trunk[...], policy[...], (((1,), (1,)), ((), ())), preferred_element_type=F32)
        + act_noise[...].astype(F32)
    ).astype(BF16)
    wait_all(t_full, sems.at[1])
    blocks = t_full.shape[3] // 16
    block = width // blocks
    square = jnp.zeros((rows, 1), F32)
    for q in range(blocks):

        def tile(n, square):
            cols = pl.ds(pl.multiple_of(n * TILE, TILE), TILE)
            at = pl.ds(pl.multiple_of(q * block + n * TILE, TILE), TILE)
            weight = t_full[:, :, :, q * 16 : (q + 1) * 16, cols].reshape(latents_in.shape[1], TILE)
            drive = jnp.dot(turned_z[...], weight, preferred_element_type=F32) + jnp.dot(
                action, action_w[:, at], preferred_element_type=F32
            )
            m = states_in[:, at].astype(F32) + silu(drive)
            mixed[:, at] = m
            return square + jnp.sum(m * m, axis=1, keepdims=True)

        square = lax.fori_loop(0, block // TILE, tile, square)
    norm = lax.rsqrt(square * (1.0 / width) + EPS)

    def normed(n, reward):
        at = pl.ds(pl.multiple_of(n * TILE, TILE), TILE)
        out = (mixed[:, at] * norm).astype(BF16)
        states_out[:, at] = out
        return reward + jnp.sum(out.astype(F32) * reward_w[:, at].astype(F32), axis=1, keepdims=True)

    reward = lax.fori_loop(0, width // TILE, normed, jnp.zeros((rows, 1), F32))
    turn_columns(where, states_out, turned_h)
    noise_copy.wait()
    wait_all(p_full, sems.at[2])

    @pl.loop(0, latents_out.shape[1] // TILE)
    def _(n):
        acc, cols = prior_dot(turned_h[...], p_full, n)
        latents_out[:, cols] = (acc + spread[:, cols] * lat_noise[:, cols].astype(F32)).astype(BF16)

    if not last:
        value_out[...] = value
        reward_out[...] = reward
        return
    last_value = critic(latents_out)
    second = reward + GAMMA * ((1.0 - LAMBDA) * last_value + LAMBDA * last_value)
    first = reward_0[...] + GAMMA * ((1.0 - LAMBDA) * value + LAMBDA * second)
    place = lax.broadcasted_iota(jnp.int32, (rows, 128), 1)
    out = jnp.where(place == 0, first, jnp.where(place == 1, second, 0.0))
    out = jnp.where(place == 2, (value_0[...] - first) * scale, out)
    out = jnp.where(place == 3, (value - second) * scale, out)
    outs[...] = out


VMEM_SPEC = pl.BlockSpec(memory_space=pltpu.VMEM)
ANY_SPEC = pl.BlockSpec(memory_space=pl.ANY)
SMEM_SPEC = pl.BlockSpec(memory_space=pltpu.SMEM)
LIMIT = 50 * 2**20
SMALL_LIMIT = 24 * 2**20


def full_scratch(cols):
    return pltpu.VMEM((NZ, NY, NX, 64, cols), BF16)


def first_call(where, dealt, pieces, cols):
    return pl.pallas_call(
        first_kernel,
        name="first_latents",
        out_shape=jax.ShapeDtypeStruct((dealt.shape[0], cols), BF16),
        in_specs=[SMEM_SPEC, VMEM_SPEC] + [ANY_SPEC] * len(pieces),
        out_specs=VMEM_SPEC,
        scratch_shapes=[
            full_scratch(cols),
            pltpu.VMEM((dealt.shape[0], dealt.shape[1] - cols), BF16),
            pltpu.SemaphoreType.DMA,
        ],
        compiler_params=pltpu.CompilerParams(vmem_limit_bytes=LIMIT),
        cost_estimate=pl.CostEstimate(flops=2 * 128 * 4096 * 1024, bytes_accessed=10 * 2**20, transcendentals=0),
    )(where, dealt, *pieces)


def step_call(last, scale, where, states, latents, weights, noise, early, p_pieces, t_pieces):
    trunk_weight, head, policy, action_w, reward_w, spread = weights
    rows, cols = latents.shape
    width, hidden = action_w.shape[1], trunk_weight.shape[1]
    column = jax.ShapeDtypeStruct((rows, 1), F32)
    shapes = [jax.ShapeDtypeStruct((rows, width), BF16)]
    if last:
        shapes += [jax.ShapeDtypeStruct((rows, 128), F32)]
    else:
        shapes += [jax.ShapeDtypeStruct((rows, cols), BF16), column, column]
    scratch = [
        full_scratch(cols),
        full_scratch(cols),
        pltpu.VMEM((cols, hidden), BF16),
        pltpu.VMEM((rows, hidden), BF16),
        pltpu.VMEM((rows, width), F32),
        pltpu.VMEM((rows, width), BF16),
        pltpu.VMEM((rows, cols), BF16),
        pltpu.VMEM((rows, cols), BF16),
        pltpu.SemaphoreType.DMA((4,)),
    ]
    if last:
        scratch.append(pltpu.VMEM((rows, cols), BF16))
    small = [states, latents]
    heads = [head, policy, action_w, reward_w, spread, *noise, *early]
    specs = [SMEM_SPEC] + [VMEM_SPEC] * 2 + [ANY_SPEC] + [VMEM_SPEC] * 6 + [ANY_SPEC] + [VMEM_SPEC] * len(early)
    specs += [ANY_SPEC] * (2 * N_PIECES)
    return pl.pallas_call(
        functools.partial(step_kernel, last, scale),
        name="last_step" if last else "first_step",
        out_shape=shapes,
        in_specs=specs,
        out_specs=[VMEM_SPEC] * len(shapes),
        scratch_shapes=scratch,
        compiler_params=pltpu.CompilerParams(vmem_limit_bytes=LIMIT),
        cost_estimate=pl.CostEstimate(flops=2 * 128 * 1024 * 10240, bytes_accessed=24 * 2**20, transcendentals=0),
    )(where, *small, trunk_weight, *heads, *p_pieces, *t_pieces)


def slope_kernel(*refs):
    pieces, (trunk_part, head_part, turned, slopes) = refs[:16], refs[16:]
    for i, piece in enumerate(pieces):
        rows = piece.shape[0]
        at = i * rows
        latents = piece[...]
        pre = jnp.dot(latents, trunk_part[...], preferred_element_type=F32)
        sig = 1.0 / (1.0 + jnp.exp(-pre))
        slopes[at : at + rows] = head_part[...] * (sig * (1.0 + pre * (1.0 - sig)))
        turned[:, at : at + rows] = latents.T


def slope_call(kept, trunk_part, head_part):
    count = 16 * kept[0][0].shape[0]
    cols, part = trunk_part.shape
    return pl.pallas_call(
        slope_kernel,
        name="slopes",
        out_shape=[jax.ShapeDtypeStruct((cols, count), BF16), jax.ShapeDtypeStruct((count, part), F32)],
        in_specs=[VMEM_SPEC] * 18,
        out_specs=[VMEM_SPEC] * 2,
        compiler_params=pltpu.CompilerParams(vmem_limit_bytes=SMALL_LIMIT),
        cost_estimate=pl.CostEstimate(flops=2 * 2048 * 1024 * 256, bytes_accessed=12 * 2**20, transcendentals=0),
    )(*kept[0], *kept[1], trunk_part, head_part)


def share_kernel(where, pair, below, above, away, turned, slopes, *refs):
    outs, (back, total) = refs[:4], refs[4:]
    line = [part[c] for part in (pair, below, above, away) for c in range(2)]
    rows = pair.shape[1]
    for step in range(2):
        for i, column in enumerate(line):
            at = (8 * step + i) * rows
            back[at : at + rows] = (column[:, 2 + step : 3 + step] * slopes[at : at + rows]).astype(BF16)
    share = jnp.dot(turned[...], back[...], preferred_element_type=F32).astype(BF16)
    total[...] = share.reshape(total.shape)
    for out, d in zip(outs, (0, 1, -1, 2)):
        out[...] = total[:, lax.rem(where[1] + NY + d, NY)]


def share_call(where, columns, turned, slopes):
    cols, part = turned.shape[0], slopes.shape[1]
    block = jax.ShapeDtypeStruct((NZ, cols // (NZ * NY), part), BF16)
    return pl.pallas_call(
        share_kernel,
        name="gradient_share",
        out_shape=[block] * 4,
        in_specs=[SMEM_SPEC] + [VMEM_SPEC] * 6,
        out_specs=[VMEM_SPEC] * 4,
        scratch_shapes=[
            pltpu.VMEM(slopes.shape, BF16),
            pltpu.VMEM((NZ, NY, cols // (NZ * NY), part), BF16),
        ],
        compiler_params=pltpu.CompilerParams(vmem_limit_bytes=SMALL_LIMIT),
        cost_estimate=pl.CostEstimate(flops=2 * 2048 * 1024 * 256, bytes_accessed=8 * 2**20, transcendentals=0),
    )(where, *columns, turned, slopes)


def relay_x(packed):
    near = along_x(packed[0], lambda x: x ^ 1)
    away = along_x(packed[1], lambda x: x - 1 if x % 2 == 0 else x + 1)
    return near, away


def relay_rest(near, away, xh, core):
    crossed = swap_core(jnp.stack([near[1], away[1]]))
    first, second = core == 0, xh == 0

    def by_core(mine, other):
        return [jnp.where(first, mine, other), jnp.where(first, other, mine)]

    same, other = by_core(near[0], crossed[0]), by_core(away[0], crossed[1])
    low = [jnp.where(second, same[c], other[c]) for c in range(2)]
    high = [jnp.where(second, other[c], same[c]) for c in range(2)]
    both = jnp.stack(low + high, axis=1)
    return both


def deal(both):
    dealt = lax.all_to_all(both, ("z", "y"), split_axis=0, concat_axis=0, tiled=True)
    return dealt


def x_gather(latents):
    mine = [latents] + [along_x(latents, lambda x, d=d: x + d) for d in (1, -1, 2)]
    return [swap_core(mine[0])] + mine


def x_gather_rest(line):
    pieces = [line[1], line[0]]
    for a in line[2:]:
        pieces += [a, swap_core(a)]
    return pieces


def x_columns(column):
    pair = jnp.stack([column, swap_core(column)])
    return [pair] + [along_x(pair, lambda x, d=d: x + d) for d in (1, -1, 2)]


def local(
    replay_states,
    replay_embed,
    replay_index,
    episode_first,
    prior_weight,
    transition_weight,
    action_weight,
    trunk_weight,
    value_head,
    policy_head,
    reward_head,
    latent_scale,
    action_noise,
    latent_noise,
):
    g, z, y = lax.axis_index("grp"), lax.axis_index("z"), lax.axis_index("y")
    xh, core = lax.axis_index("xh"), lax.axis_index("core")
    width = replay_states.shape[1]
    rows = replay_index.shape[0]
    order = jnp.stack([replay_index, episode_first]).reshape(2, NZ * NY, NX, NC)
    order = jnp.transpose(order, (2, 3, 0, 1))
    order = jnp.where(xh == 0, order, order[::-1])
    order = jnp.where(core == 0, order, order[:, ::-1])
    order = jnp.swapaxes(order, 1, 2).swapaxes(0, 1).reshape(2, rows)

    def packed_of(order):
        keep = (1 - order[1]).astype(BF16)[:, None]
        return jnp.concatenate(
            [jnp.take(replay_states, order[0], axis=0) * keep, jnp.take(replay_embed, order[0], axis=0)],
            axis=1,
        ).reshape(NX, NC, NZ * NY, -1)

    dealt, flat = gather_weights(prior_weight, transition_weight, g, core, xh, order, packed_of)
    p_pieces, t_pieces = pieces_of(flat, 0), pieces_of(flat, 1)
    where = jnp.stack([z, y, xh, core, g]).astype(jnp.int32)
    steps = action_noise.shape[0]
    hidden_units = trunk_weight.shape[1]
    cols = prior_weight.shape[1]
    part = hidden_units // 8
    slot = (g * 2 + xh) * 2 + core
    trunk_part = lax.dynamic_slice(trunk_weight, (0, slot * part), (trunk_weight.shape[0], part))
    head_part = lax.dynamic_slice(value_head, (slot * part,), (part,)).astype(F32)
    count = lax.axis_size("grp") * NZ * NY * NX * NC
    grad_scale = 4.0 * (float(hidden_units) / float(count * rows * steps)) ** 0.5
    weights = (
        trunk_weight,
        value_head[None],
        policy_head.T,
        action_weight,
        reward_head[None],
        latent_scale[None],
    )

    latents = first_call(where, dealt, p_pieces, cols)
    latents, trunk_part, head_part = lax.optimization_barrier((latents, trunk_part, head_part))
    kept = [x_gather(latents)]
    states, latents, value_0, reward_0 = step_call(
        False, grad_scale, where, dealt, latents, weights, (action_noise[0], latent_noise), (), p_pieces, t_pieces
    )
    latents, kept[0] = lax.optimization_barrier((latents, kept[0]))
    kept.append(x_gather(latents))
    states, outs = step_call(
        True, grad_scale, where, states, latents, weights, (action_noise[1], latent_noise), (value_0, reward_0), p_pieces, t_pieces
    )
    outs, kept[1] = lax.optimization_barrier((outs, kept[1]))
    columns = x_columns(outs)
    kept = [x_gather_rest(line) for line in kept]
    turned, slopes = slope_call(kept, trunk_part, head_part[None])
    keep, *others = share_call(where, columns, turned, slopes)
    targets = outs[:, :2].T
    met = keep.astype(F32)
    for block, d in zip(others, (1, -1, 2)):
        met = met + lax.ppermute(block, "y", shift(NY, d)).astype(F32)
    sent = met.astype(BF16).reshape(1, NZ, NX * NC, -1, part)
    sent = jnp.concatenate([sent, sent], axis=0).reshape(2 * NZ * NX * NC, -1, part)
    parts = lax.all_to_all(sent, ("grp", "z", "xh", "core"), split_axis=0, concat_axis=0, tiled=True)
    parts = jnp.sum(parts.astype(F32).reshape(2, NZ, NX * NC, -1, part), axis=1)
    trunk_grad = jnp.transpose(parts, (2, 0, 1, 3)).reshape(-1, hidden_units)
    return (states, targets, trunk_grad)


def solution(mesh):
    fine = Mesh(mesh.devices.reshape(2, NZ, NY, NX, NC), AXES)
    return jax.shard_map(
        local,
        mesh=fine,
        in_specs=(
            P(AXES, None),
            P(AXES, None),
            P(AXES),
            P(AXES),
            P(FSDP, None),
            P(FSDP, None),
            P(),
            P(),
            P(),
            P(),
            P(),
            P(),
            P(None, AXES, None),
            P(None, AXES, None),
        ),
        out_specs=(P(AXES, None), P(None, AXES), P(FSDP, None)),
        check_vma=False,
    )
```

```python
import functools

import jax
import jax.numpy as jnp
from jax import lax
from jax.experimental import pallas as pl
from jax.experimental.pallas import tpu as pltpu
from jax.sharding import Mesh, PartitionSpec as P

GAMMA = 0.985
LAMBDA = 0.95
EPS = 1e-06
F32 = jnp.float32
BF16 = jnp.bfloat16

NZ, NY, NX, NC = 8, 4, 2, 2
AXES = ("grp", "z", "y", "xh", "core")
FSDP = ("z", "y", "xh", "core")


def shift(n, d):
    return [(i, (i + d) % n) for i in range(n)]


def x_line(move):
    pairs = []
    for g in range(2):
        for h in range(2):
            to = move(2 * h + g) % 4
            pairs.append((2 * g + h, 2 * (to % 2) + to // 2))
    return pairs


def along_x(a, move):
    return lax.ppermute(a, ("grp", "xh"), x_line(move))


def swap_core(a):
    return lax.ppermute(a, "core", shift(2, 1))


def split_ring(axis, n):
    return [(2 * i + c, 2 * ((i + 1 - 2 * c) % n) + c) for i in range(n) for c in range(2)]


def gather_weights(prior, transition, g, core, xh, order, packed_of):
    depth = transition.shape[0]
    cols = prior.shape[1]
    blocks = transition.shape[1] // cols
    other_p, other_t = swap_core(prior), swap_core(transition)

    def both(mine, other):
        return jnp.where(core == 0, jnp.concatenate([mine, other]), jnp.concatenate([other, mine]))

    chip_t = both(transition, other_t).reshape(2 * depth, blocks, cols)
    unit = jnp.stack([both(prior, other_p), jnp.swapaxes(chip_t, 0, 1).reshape(-1, cols)])
    unit, order = lax.optimization_barrier((unit, order))
    ring = [unit]
    for hop in range(4):
        pairs = split_ring("z", NZ)
        if hop == 3:
            pairs = [p for p in pairs if p[0] % 2]
        ring.append(lax.ppermute(ring[-1], ("z", "core"), pairs))
        if hop == 0:
            packed = packed_of(order)
            ring[-1], packed = lax.optimization_barrier((ring[-1], packed))
            near, away = relay_x(packed)
    ring[4], near, away = lax.optimization_barrier((ring[4], near, away))
    both = relay_rest(near, away, xh, core)
    own = jnp.where(core == 0, jnp.stack(ring[3::-1], axis=1), jnp.stack(ring[1:], axis=1))
    chosen = g == core

    def pair_hop(a):
        return along_x(a, lambda x: x + 1 if x % 2 else x - 1)

    def partner_hop(a):
        return along_x(a, lambda x: x ^ 1)

    def y_hop(a):
        return lax.ppermute(a, ("y", "core"), split_ring("y", NY))

    def half(a):
        return lax.dynamic_index_in_dim(a, g, 0, keepdims=False)

    near_1 = pair_hop(half(own))
    own_s = swap_core(own)
    mine = [jnp.stack([own[w], own_s[w]]) for w in range(2)]
    side_p = y_hop(mine[0])
    near_1s = swap_core(near_1)
    mine_t, side_p, near_1, near_1s = lax.optimization_barrier((mine[1], side_p, near_1, near_1s))
    dealt = deal(both)
    beside_p = jnp.where(chosen, side_p[0], side_p[1])
    side_t, beside_p1, near_2 = y_hop(mine_t), pair_hop(beside_p), partner_hop(near_1)
    side_ps = swap_core(side_p)
    beside_p1, near_2, side_ps = lax.optimization_barrier((beside_p1, near_2, side_ps))
    beside_p2 = partner_hop(beside_p1)
    near_2s, beside_p1s = swap_core(near_2), swap_core(beside_p1)
    side_t, near_2s, beside_p1s, dealt = lax.optimization_barrier((side_t, near_2s, beside_p1s, dealt))
    beside_t1 = pair_hop(jnp.where(chosen, side_t[0], side_t[1]))
    far = y_hop(jnp.stack([side_p[0], side_t[0]]))
    side_ts = swap_core(side_t)
    far, beside_t1, beside_p2, side_ts = lax.optimization_barrier((far, beside_t1, beside_p2, side_ts))
    dealt = dealt.reshape(-1, dealt.shape[-1])
    away_1, beside_t2 = pair_hop(half(far)), partner_hop(beside_t1)
    far_s, beside_p2s, beside_t1s = swap_core(far), swap_core(beside_p2), swap_core(beside_t1)
    away_1, beside_t2, far_s, beside_p2s, beside_t1s = lax.optimization_barrier(
        (away_1, beside_t2, far_s, beside_p2s, beside_t1s)
    )
    away_2 = partner_hop(away_1)
    beside_t2s, away_1s = swap_core(beside_t2), swap_core(away_1)
    away_2, beside_t2s, away_1s = lax.optimization_barrier((away_2, beside_t2s, away_1s))
    flat = [own, own_s, far, far_s, side_p, side_ps, side_t, side_ts]
    flat += [near_1, near_1s, near_2, near_2s]
    flat += [beside_p1, beside_p1s, beside_p2, beside_p2s]
    flat += [beside_t1, beside_t1s, beside_t2, beside_t2s]
    flat += [away_1, away_1s, away_2, swap_core(away_2)]
    return dealt, flat


def pieces_of(flat, w):
    across = [flat[8 + 4 * k : 12 + 4 * k] for k in (0, 1 + w, 3)]
    return flat[:4] + flat[4 + 2 * w : 6 + 2 * w] + across[0] + across[1] + across[2]


N_PIECES = 18


def place_all(w, where, pieces, full, sem):
    y, xh, core, g = (where[i] for i in range(1, 5))
    own, own_s, far, far_s, side, side_s = pieces[:6]
    turn = jnp.where(core == 0, -1, 1)

    def copy(src, group, dy, h):
        dst = full.at[pl.ds(4 * group, 4), lax.rem(y + NY + dy, NY), h]
        pltpu.make_async_copy(src, dst, sem).start()

    copy(own.at[w], core, 0, xh)
    copy(own_s.at[w], 1 - core, 0, xh)
    for r in range(2):
        copy(side.at[r], jnp.bitwise_xor(core, r), turn, xh)
        copy(side_s.at[r], jnp.bitwise_xor(1 - core, r), -turn, xh)
    copy(far.at[w], core, 2, xh)
    copy(far_s.at[w], 1 - core, 2, xh)
    near, beside, away = (pieces[6 + 4 * k : 10 + 4 * k] for k in range(3))
    for way, group in ((0, 1 - g), (2, g)):
        copy(beside[way], group, turn, 1 - xh)
        copy(beside[way + 1], group, -turn, 1 - xh)

        @pl.when(group == w)
        def _():
            copy(near[way], core, 0, 1 - xh)
            copy(near[way + 1], 1 - core, 0, 1 - xh)
            copy(away[way], core, 2, 1 - xh)
            copy(away[way + 1], 1 - core, 2, 1 - xh)


def turn_columns(where, src, dst):
    size = dst.shape[1] // NZ
    for i in range(NZ):
        at = lax.rem(where[0] + NZ - 3 + i, NZ) * size
        dst[:, i * size : (i + 1) * size] = src[:, pl.ds(pl.multiple_of(at, size), size)]


def wait_all(full, sem):
    pltpu.make_async_copy(full, full, sem).wait()


def silu(v):
    return v / (1.0 + jnp.exp(-v))


TILE = 512


def prior_dot(h, full, n):
    cols = pl.ds(pl.multiple_of(n * TILE, TILE), TILE)
    return jnp.dot(h, full[:, :, :, :, cols].reshape(h.shape[1], TILE), preferred_element_type=F32), cols


def first_kernel(where, dealt, *refs):
    pieces, (latents, full, turned, sem) = refs[:N_PIECES], refs[N_PIECES:]
    place_all(0, where, pieces, full, sem)
    width = dealt.shape[1] - latents.shape[1]
    turn_columns(where, dealt, turned)
    wait_all(full, sem)

    @pl.loop(0, latents.shape[1] // TILE)
    def _(n):
        acc, cols = prior_dot(turned[...], full, n)
        embed = dealt[:, pl.ds(pl.multiple_of(width + n * TILE, TILE), TILE)]
        latents[:, cols] = (acc + embed.astype(F32)).astype(BF16)


def step_kernel(last, scale, where, states_in, latents_in, trunk_hbm, head, policy, action_w, reward_w, spread, act_noise, noise_hbm, *refs):
    refs = list(refs)
    if last:
        value_0, reward_0 = refs[:2]
        refs = refs[2:]
    p_pieces, t_pieces, refs = refs[:N_PIECES], refs[N_PIECES : 2 * N_PIECES], refs[2 * N_PIECES :]
    if last:
        states_out, outs, refs = refs[0], refs[1], refs[2:]
    else:
        states_out, latents_out, value_out, reward_out = refs[:4]
        refs = refs[4:]
    p_full, t_full, trunk_w, trunk, mixed, turned_h, turned_z, lat_noise, sems = refs[:9]
    if last:
        latents_out = refs[9]
    trunk_copy = pltpu.make_async_copy(trunk_hbm, trunk_w, sems.at[0])
    trunk_copy.start()
    place_all(1, where, t_pieces, t_full, sems.at[1])
    noise_copy = pltpu.make_async_copy(noise_hbm.at[int(last)], lat_noise, sems.at[3])
    noise_copy.start()
    place_all(0, where, p_pieces, p_full, sems.at[2])
    turn_columns(where, latents_in, turned_z)
    trunk_copy.wait()
    rows, width = mixed.shape
    hidden = trunk_w.shape[1]

    def critic(z_ref):
        def tile(n, value):
            cols = pl.ds(pl.multiple_of(n * TILE, TILE), TILE)
            pre = jnp.dot(z_ref[...], trunk_w[:, cols], preferred_element_type=F32)
            out = silu(pre).astype(BF16)
            trunk[:, cols] = out
            part = out.astype(F32) * head[:, cols].astype(F32)
            return value + jnp.sum(part, axis=1, keepdims=True)

        return lax.fori_loop(0, hidden // TILE, tile, jnp.zeros((rows, 1), F32), unroll=True)

    value = critic(latents_in)
    action = jnp.tanh(
        lax.dot_general(trunk[...], policy[...], (((1,), (1,)), ((), ())), preferred_element_type=F32)
        + act_noise[...].astype(F32)
    ).astype(BF16)
    wait_all(t_full, sems.at[1])
    blocks = t_full.shape[3] // 16
    block = width // blocks
    square = jnp.zeros((rows, 1), F32)
    for q in range(blocks):

        def tile(n, square):
            cols = pl.ds(pl.multiple_of(n * TILE, TILE), TILE)
            at = pl.ds(pl.multiple_of(q * block + n * TILE, TILE), TILE)
            weight = t_full[:, :, :, q * 16 : (q + 1) * 16, cols].reshape(latents_in.shape[1], TILE)
            drive = jnp.dot(turned_z[...], weight, preferred_element_type=F32) + jnp.dot(
                action, action_w[:, at], preferred_element_type=F32
            )
            m = states_in[:, at].astype(F32) + silu(drive)
            mixed[:, at] = m
            return square + jnp.sum(m * m, axis=1, keepdims=True)

        square = lax.fori_loop(0, block // TILE, tile, square, unroll=True)
    norm = lax.rsqrt(square * (1.0 / width) + EPS)

    def normed(n, reward):
        at = pl.ds(pl.multiple_of(n * TILE, TILE), TILE)
        out = (mixed[:, at] * norm).astype(BF16)
        states_out[:, at] = out
        return reward + jnp.sum(out.astype(F32) * reward_w[:, at].astype(F32), axis=1, keepdims=True)

    reward = lax.fori_loop(0, width // TILE, normed, jnp.zeros((rows, 1), F32), unroll=True)
    turn_columns(where, states_out, turned_h)
    noise_copy.wait()
    wait_all(p_full, sems.at[2])

    @pl.loop(0, latents_out.shape[1] // TILE)
    def _(n):
        acc, cols = prior_dot(turned_h[...], p_full, n)
        latents_out[:, cols] = (acc + spread[:, cols] * lat_noise[:, cols].astype(F32)).astype(BF16)

    if not last:
        value_out[...] = value
        reward_out[...] = reward
        return
    last_value = critic(latents_out)
    second = reward + GAMMA * ((1.0 - LAMBDA) * last_value + LAMBDA * last_value)
    first = reward_0[...] + GAMMA * ((1.0 - LAMBDA) * value + LAMBDA * second)
    place = lax.broadcasted_iota(jnp.int32, (rows, 128), 1)
    out = jnp.where(place == 0, first, jnp.where(place == 1, second, 0.0))
    out = jnp.where(place == 2, (value_0[...] - first) * scale, out)
    out = jnp.where(place == 3, (value - second) * scale, out)
    outs[...] = out


VMEM_SPEC = pl.BlockSpec(memory_space=pltpu.VMEM)
ANY_SPEC = pl.BlockSpec(memory_space=pl.ANY)
SMEM_SPEC = pl.BlockSpec(memory_space=pltpu.SMEM)
LIMIT = 50 * 2**20
SMALL_LIMIT = 24 * 2**20


def full_scratch(cols):
    return pltpu.VMEM((NZ, NY, NX, 64, cols), BF16)


def first_call(where, dealt, pieces, cols):
    return pl.pallas_call(
        first_kernel,
        name="first_latents",
        out_shape=jax.ShapeDtypeStruct((dealt.shape[0], cols), BF16),
        in_specs=[SMEM_SPEC, VMEM_SPEC] + [ANY_SPEC] * len(pieces),
        out_specs=VMEM_SPEC,
        scratch_shapes=[
            full_scratch(cols),
            pltpu.VMEM((dealt.shape[0], dealt.shape[1] - cols), BF16),
            pltpu.SemaphoreType.DMA,
        ],
        compiler_params=pltpu.CompilerParams(vmem_limit_bytes=LIMIT),
        cost_estimate=pl.CostEstimate(flops=2 * 128 * 4096 * 1024, bytes_accessed=10 * 2**20, transcendentals=0),
    )(where, dealt, *pieces)


def step_call(last, scale, where, states, latents, weights, noise, early, p_pieces, t_pieces):
    trunk_weight, head, policy, action_w, reward_w, spread = weights
    rows, cols = latents.shape
    width, hidden = action_w.shape[1], trunk_weight.shape[1]
    column = jax.ShapeDtypeStruct((rows, 1), F32)
    shapes = [jax.ShapeDtypeStruct((rows, width), BF16)]
    if last:
        shapes += [jax.ShapeDtypeStruct((rows, 128), F32)]
    else:
        shapes += [jax.ShapeDtypeStruct((rows, cols), BF16), column, column]
    scratch = [
        full_scratch(cols),
        full_scratch(cols),
        pltpu.VMEM((cols, hidden), BF16),
        pltpu.VMEM((rows, hidden), BF16),
        pltpu.VMEM((rows, width), F32),
        pltpu.VMEM((rows, width), BF16),
        pltpu.VMEM((rows, cols), BF16),
        pltpu.VMEM((rows, cols), BF16),
        pltpu.SemaphoreType.DMA((4,)),
    ]
    if last:
        scratch.append(pltpu.VMEM((rows, cols), BF16))
    small = [states, latents]
    heads = [head, policy, action_w, reward_w, spread, *noise, *early]
    specs = [SMEM_SPEC] + [VMEM_SPEC] * 2 + [ANY_SPEC] + [VMEM_SPEC] * 6 + [ANY_SPEC] + [VMEM_SPEC] * len(early)
    specs += [ANY_SPEC] * (2 * N_PIECES)
    return pl.pallas_call(
        functools.partial(step_kernel, last, scale),
        name="last_step" if last else "first_step",
        out_shape=shapes,
        in_specs=specs,
        out_specs=[VMEM_SPEC] * len(shapes),
        scratch_shapes=scratch,
        compiler_params=pltpu.CompilerParams(vmem_limit_bytes=LIMIT),
        cost_estimate=pl.CostEstimate(flops=2 * 128 * 1024 * 10240, bytes_accessed=24 * 2**20, transcendentals=0),
    )(where, *small, trunk_weight, *heads, *p_pieces, *t_pieces)


def slope_kernel(*refs):
    pieces, (trunk_part, head_part, turned, slopes) = refs[:16], refs[16:]
    for i, piece in enumerate(pieces):
        rows = piece.shape[0]
        at = i * rows
        latents = piece[...]
        pre = jnp.dot(latents, trunk_part[...], preferred_element_type=F32)
        sig = 1.0 / (1.0 + jnp.exp(-pre))
        slopes[at : at + rows] = head_part[...] * (sig * (1.0 + pre * (1.0 - sig)))
        turned[:, at : at + rows] = latents.T


def slope_call(kept, trunk_part, head_part):
    count = 16 * kept[0][0].shape[0]
    cols, part = trunk_part.shape
    return pl.pallas_call(
        slope_kernel,
        name="slopes",
        out_shape=[jax.ShapeDtypeStruct((cols, count), BF16), jax.ShapeDtypeStruct((count, part), F32)],
        in_specs=[VMEM_SPEC] * 18,
        out_specs=[VMEM_SPEC] * 2,
        compiler_params=pltpu.CompilerParams(vmem_limit_bytes=SMALL_LIMIT),
        cost_estimate=pl.CostEstimate(flops=2 * 2048 * 1024 * 256, bytes_accessed=12 * 2**20, transcendentals=0),
    )(*kept[0], *kept[1], trunk_part, head_part)


def share_kernel(where, pair, below, above, away, turned, slopes, *refs):
    outs, (back, total) = refs[:4], refs[4:]
    line = [part[c] for part in (pair, below, above, away) for c in range(2)]
    rows = pair.shape[1]
    for step in range(2):
        for i, column in enumerate(line):
            at = (8 * step + i) * rows
            back[at : at + rows] = (column[:, 2 + step : 3 + step] * slopes[at : at + rows]).astype(BF16)
    share = jnp.dot(turned[...], back[...], preferred_element_type=F32).astype(BF16)
    total[...] = share.reshape(total.shape)
    for out, d in zip(outs, (0, 1, -1, 2)):
        out[...] = total[:, lax.rem(where[1] + NY + d, NY)]


def share_call(where, columns, turned, slopes):
    cols, part = turned.shape[0], slopes.shape[1]
    block = jax.ShapeDtypeStruct((NZ, cols // (NZ * NY), part), BF16)
    return pl.pallas_call(
        share_kernel,
        name="gradient_share",
        out_shape=[block] * 4,
        in_specs=[SMEM_SPEC] + [VMEM_SPEC] * 6,
        out_specs=[VMEM_SPEC] * 4,
        scratch_shapes=[
            pltpu.VMEM(slopes.shape, BF16),
            pltpu.VMEM((NZ, NY, cols // (NZ * NY), part), BF16),
        ],
        compiler_params=pltpu.CompilerParams(vmem_limit_bytes=SMALL_LIMIT),
        cost_estimate=pl.CostEstimate(flops=2 * 2048 * 1024 * 256, bytes_accessed=8 * 2**20, transcendentals=0),
    )(where, *columns, turned, slopes)


def relay_x(packed):
    near = along_x(packed[0], lambda x: x ^ 1)
    away = along_x(packed[1], lambda x: x - 1 if x % 2 == 0 else x + 1)
    return near, away


def relay_rest(near, away, xh, core):
    crossed = swap_core(jnp.stack([near[1], away[1]]))
    first, second = core == 0, xh == 0

    def by_core(mine, other):
        return [jnp.where(first, mine, other), jnp.where(first, other, mine)]

    same, other = by_core(near[0], crossed[0]), by_core(away[0], crossed[1])
    low = [jnp.where(second, same[c], other[c]) for c in range(2)]
    high = [jnp.where(second, other[c], same[c]) for c in range(2)]
    both = jnp.stack(low + high, axis=1)
    return both


def deal(both):
    dealt = lax.all_to_all(both, ("z", "y"), split_axis=0, concat_axis=0, tiled=True)
    return dealt


def x_gather(latents):
    mine = [latents] + [along_x(latents, lambda x, d=d: x + d) for d in (1, -1, 2)]
    return [swap_core(mine[0])] + mine


def x_gather_rest(line):
    pieces = [line[1], line[0]]
    for a in line[2:]:
        pieces += [a, swap_core(a)]
    return pieces


def x_columns(column):
    pair = jnp.stack([column, swap_core(column)])
    return [pair] + [along_x(pair, lambda x, d=d: x + d) for d in (1, -1, 2)]


def local(
    replay_states,
    replay_embed,
    replay_index,
    episode_first,
    prior_weight,
    transition_weight,
    action_weight,
    trunk_weight,
    value_head,
    policy_head,
    reward_head,
    latent_scale,
    action_noise,
    latent_noise,
):
    g, z, y = lax.axis_index("grp"), lax.axis_index("z"), lax.axis_index("y")
    xh, core = lax.axis_index("xh"), lax.axis_index("core")
    width = replay_states.shape[1]
    rows = replay_index.shape[0]
    order = jnp.stack([replay_index, episode_first]).reshape(2, NZ * NY, NX, NC)
    order = jnp.transpose(order, (2, 3, 0, 1))
    order = jnp.where(xh == 0, order, order[::-1])
    order = jnp.where(core == 0, order, order[:, ::-1])
    order = jnp.swapaxes(order, 1, 2).swapaxes(0, 1).reshape(2, rows)

    def packed_of(order):
        keep = (1 - order[1]).astype(BF16)[:, None]
        return jnp.concatenate(
            [jnp.take(replay_states, order[0], axis=0) * keep, jnp.take(replay_embed, order[0], axis=0)],
            axis=1,
        ).reshape(NX, NC, NZ * NY, -1)

    dealt, flat = gather_weights(prior_weight, transition_weight, g, core, xh, order, packed_of)
    p_pieces, t_pieces = pieces_of(flat, 0), pieces_of(flat, 1)
    where = jnp.stack([z, y, xh, core, g]).astype(jnp.int32)
    steps = action_noise.shape[0]
    hidden_units = trunk_weight.shape[1]
    cols = prior_weight.shape[1]
    part = hidden_units // 8
    slot = (g * 2 + xh) * 2 + core
    trunk_part = lax.dynamic_slice(trunk_weight, (0, slot * part), (trunk_weight.shape[0], part))
    head_part = lax.dynamic_slice(value_head, (slot * part,), (part,)).astype(F32)
    count = lax.axis_size("grp") * NZ * NY * NX * NC
    grad_scale = 4.0 * (float(hidden_units) / float(count * rows * steps)) ** 0.5
    weights = (
        trunk_weight,
        value_head[None],
        policy_head.T,
        action_weight,
        reward_head[None],
        latent_scale[None],
    )

    latents = first_call(where, dealt, p_pieces, cols)
    latents, trunk_part, head_part = lax.optimization_barrier((latents, trunk_part, head_part))
    kept = [x_gather(latents)]
    states, latents, value_0, reward_0 = step_call(
        False, grad_scale, where, dealt, latents, weights, (action_noise[0], latent_noise), (), p_pieces, t_pieces
    )
    latents, kept[0] = lax.optimization_barrier((latents, kept[0]))
    kept.append(x_gather(latents))
    states, outs = step_call(
        True, grad_scale, where, states, latents, weights, (action_noise[1], latent_noise), (value_0, reward_0), p_pieces, t_pieces
    )
    outs, kept[1] = lax.optimization_barrier((outs, kept[1]))
    columns = x_columns(outs)
    kept = [x_gather_rest(line) for line in kept]
    turned, slopes = slope_call(kept, trunk_part, head_part[None])
    keep, *others = share_call(where, columns, turned, slopes)
    targets = outs[:, :2].T
    met = keep.astype(F32)
    for block, d in zip(others, (1, -1, 2)):
        met = met + lax.ppermute(block, "y", shift(NY, d)).astype(F32)
    sent = met.astype(BF16).reshape(1, NZ, NX * NC, -1, part)
    sent = jnp.concatenate([sent, sent], axis=0).reshape(2 * NZ * NX * NC, -1, part)
    parts = lax.all_to_all(sent, ("grp", "z", "xh", "core"), split_axis=0, concat_axis=0, tiled=True)
    parts = jnp.sum(parts.astype(F32).reshape(2, NZ, NX * NC, -1, part), axis=1)
    trunk_grad = jnp.transpose(parts, (2, 0, 1, 3)).reshape(-1, hidden_units)
    return (states, targets, trunk_grad)


def solution(mesh):
    fine = Mesh(mesh.devices.reshape(2, NZ, NY, NX, NC), AXES)
    return jax.shard_map(
        local,
        mesh=fine,
        in_specs=(
            P(AXES, None),
            P(AXES, None),
            P(AXES),
            P(AXES),
            P(FSDP, None),
            P(FSDP, None),
            P(),
            P(),
            P(),
            P(),
            P(),
            P(),
            P(None, AXES, None),
            P(None, AXES, None),
        ),
        out_specs=(P(AXES, None), P(None, AXES), P(FSDP, None)),
        check_vma=False,
    )
```
